128 devices in a mesh: rep: 2 (over z_hi), fsdp: 64 (over z_lo, x, y, core).
Axes of the slice: x: 4, y: 4, z: 4 (z_hi: 2, z_lo: 2; z = z_hi * 2 + z_lo), core: 2. Of those that a mesh axis runs over, the one named last changes fastest.
Arguments:
- tokens: bfloat16 [32768, 1024], P(('rep', 'fsdp')), may hold values from -6 to 6
- gain_first: bfloat16 [1024], P('fsdp'), may hold values from 0.099609375 to 1.8984375
- w_in: bfloat16 [1024, 3072], P('fsdp'), may hold values from -0.1875 to 0.1875
- conv_weight: bfloat16 [1024, 3], P('fsdp'), may hold values from -3.5 to 3.5
- w_out: bfloat16 [1024, 1024], P('fsdp'), may hold values from -0.1875 to 0.1875
- gain_second: bfloat16 [1024], P('fsdp'), may hold values from 0.099609375 to 1.8984375
- w_gate: bfloat16 [1024, 4608], P('fsdp'), may hold values from -0.1875 to 0.1875
- w_up: bfloat16 [1024, 4608], P('fsdp'), may hold values from -0.1875 to 0.1875
- w_down: bfloat16 [4608, 1024], P('fsdp'), may hold values from -0.09375 to 0.09375
- cotangent: bfloat16 [32768, 1024], P(('rep', 'fsdp')), may hold values from -6 to 6
Outputs:
- result: bfloat16 [32768, 1024], P(('rep', 'fsdp'))
- grad_tokens: float32 [32768, 1024], P(('rep', 'fsdp'))
- grad_gain_first: float32 [1024], P('fsdp')
- grad_w_in: float32 [1024, 3072], P('fsdp')
- grad_conv_weight: float32 [1024, 3], P('fsdp')
- grad_w_out: float32 [1024, 1024], P('fsdp')
- grad_gain_second: float32 [1024], P('fsdp')
- grad_w_gate: float32 [1024, 4608], P('fsdp')
- grad_w_up: float32 [1024, 4608], P('fsdp')
- grad_w_down: float32 [4608, 1024], P('fsdp')
The draws below stay inside these ranges and needn't reach their ends.
All inputs are finite; a program needn't handle non-finite values.
Results may differ from the reference program's by a relative error of at most 0.012.
Values may be sent and summed in bfloat16 or wider, within the bound.
No kernel may reach another device: no remote copies, remote signals or barrier semaphores. Data moves between devices by JAX's collectives and lax.ppermute only.
A program may use at most 256 MiB of HBM per device.

```python
import jax
import jax.numpy as jnp
from jax import lax

D = 1024
FF = 4608
SEQ = 16384
TOKENS = 32768
N_REP = 2


def shard_levels(rng, extent, split, smallest, top_value):
    factor_of = 1.0
    for position, shards_of in split:
        draws = jax.random.uniform(jax.random.fold_in(jax.random.fold_in(rng, 6), position), (shards_of,), jnp.float32, smallest / len(split), top_value / len(split))
        factor_of = factor_of * jnp.repeat(jnp.exp(draws), extent[position] // shards_of).reshape((-1,) + (1,) * (len(extent) - 1 - position))
    return factor_of


def gaussian(stream_key, dims, deviation, most, split=(), kind=jnp.bfloat16):
    level = shard_levels(stream_key, dims, split, -0.22, 0.18) if split else 1.0
    drawn = jax.random.normal(stream_key, dims, jnp.float32) * deviation * level
    return jnp.minimum(jnp.maximum(drawn, -most), most).astype(kind)


def setup_inputs(seed: int = 0) -> dict:
    splits = jax.random.split(jax.random.key(seed), 11)
    return {
        "tokens": gaussian(splits[0], (TOKENS, D), 1.0, 6.0, ((0, 128),)),
        "gain_first": jnp.clip(1.0 + 0.18 * jax.random.normal(splits[1], (D,), jnp.float32), 0.099609375, 1.8984375).astype(jnp.bfloat16),
        "w_in": gaussian(splits[2], (D, 3 * D), D ** -0.5, 0.1875, ((0, 64),)),
        "conv_weight": gaussian(splits[3], (D, 3), 3 ** -0.5, 3.5, ((0, 64),)),
        "w_out": gaussian(splits[4], (D, D), D ** -0.5, 0.1875, ((0, 64),)),
        "gain_second": jnp.clip(1.0 + 0.18 * jax.random.normal(splits[5], (D,), jnp.float32), 0.099609375, 1.8984375).astype(jnp.bfloat16),
        "w_gate": gaussian(splits[6], (D, FF), D ** -0.5, 0.1875, ((0, 64),)),
        "w_up": gaussian(splits[7], (D, FF), D ** -0.5, 0.1875, ((0, 64),)),
        "w_down": gaussian(splits[8], (FF, D), FF ** -0.5, 0.09375, ((0, 64),)),
        "cotangent": gaussian(splits[9], (TOKENS, D), 1.0, 6.0, ((0, 128),)),
    }


@jax.custom_vjp
def low(v):
    return lax.optimization_barrier(v.astype(jnp.bfloat16)).astype(jnp.float32)

@jax.custom_vjp
def low_back(v):
    return v

def low_keep(v):
    return (low(v), None)

def low_pass(kept, grad):
    return (grad,)

def back_keep(v):
    return (v, None)

def back_low(kept, grad):
    return (low(grad),)
low.defvjp(low_keep, low_pass)
low_back.defvjp(back_keep, back_low)
epsilon = 1e-05

def matmul(left, right):
    return jnp.dot(left, right, precision=lax.Precision.HIGHEST)

def norm_scale(values):
    return lax.rsqrt(lax.optimization_barrier(jnp.mean(values * values, axis=-1, keepdims=True)) + epsilon)

def layer(inputs, gain_first, w_in, conv_weight, w_out, gain_second, w_gate, w_up, w_down):
    model_width = inputs.shape[1]
    length = inputs.shape[0]
    normed = low(inputs * norm_scale(inputs) * gain_first)
    projected = low_back(matmul(normed, w_in))
    in_gate = projected[:, :model_width]
    out_gate = projected[:, model_width:2 * model_width]
    carried = projected[:, 2 * model_width:]
    mixed = low(in_gate * carried)
    padded = jnp.concatenate([jnp.zeros((2, model_width), jnp.float32), mixed], 0)
    convolved = conv_weight[:, 0] * padded[2:] + conv_weight[:, 1] * padded[1:length + 1] + conv_weight[:, 2] * padded[:length]
    gated = low(out_gate * convolved)
    branch = low_back(matmul(gated, w_out))
    middle = inputs + branch
    normed_two = low(middle * norm_scale(middle) * gain_second)
    gate_value = low_back(matmul(normed_two, w_gate))
    up_value = low_back(matmul(normed_two, w_up))
    hidden = low(jax.nn.silu(gate_value) * up_value)
    return middle + matmul(hidden, w_down)

def reference(tokens, gain_first, w_in, conv_weight, w_out, gain_second, w_gate, w_up, w_down, cotangent):
    params = tuple((weight.astype(jnp.float32) for weight in (gain_first, w_in, conv_weight, w_out, gain_second, w_gate, w_up, w_down)))
    seq_inputs = tokens.astype(jnp.float32).reshape(N_REP, SEQ, D)
    seq_cotangents = cotangent.astype(jnp.float32).reshape(N_REP, SEQ, D)

    def one_sequence(running, sequence):
        inputs, outer = sequence
        output, pullback = jax.vjp(layer, inputs, *params)
        gradients = pullback(outer)
        running = tuple((total + grad_term for total, grad_term in zip(running, gradients[1:])))
        return (running, (output, gradients[0]))
    start = tuple((jnp.zeros_like(weight) for weight in params))
    totals, (outputs, input_grads) = lax.scan(one_sequence, start, (seq_inputs, seq_cotangents))
    return (outputs.reshape(TOKENS, D).astype(jnp.bfloat16), input_grads.reshape(TOKENS, D), totals[0], totals[1], totals[2], totals[3], totals[4], totals[5], totals[6], totals[7])
```

```python
import jax
import jax.numpy as jnp
from jax import lax
from jax.sharding import PartitionSpec as P

epsilon = 1e-05

SIDE = 4
PLANE = SIDE * SIDE
HALF = PLANE * 2


def place(z, plane, core):
    return (z * PLANE + plane) * 2 + core


def moves(target):
    return [
        (place(z, plane, core), place(*target(z, plane, core)))
        for z in range(2)
        for plane in range(PLANE)
        for core in range(2)
    ]


TO_CORE = moves(lambda z, plane, core: (z, plane, 1 - core))
TO_Z = moves(lambda z, plane, core: (1 - z, plane, core))
TO_NEXT = moves(lambda z, plane, core: (z, (plane + 1) % PLANE, core))
TO_PREVIOUS = moves(lambda z, plane, core: (z, (plane - 1) % PLANE, core))
TEAMS = [
    [place(z, plane, core) for z in range(2) for core in range(2)] for plane in range(PLANE)
]
PLANES = [
    [place(z, plane, core) for plane in range(PLANE)] for z in range(2) for core in range(2)
]
BOTH_TEAMS = [[rep * 2 * HALF + member for rep in range(2) for member in team] for team in TEAMS]


def to_core(value):
    return lax.ppermute(value, "fsdp", TO_CORE)


def to_z(value):
    return lax.ppermute(value, "fsdp", TO_Z)


def norm_scale(values):
    return lax.rsqrt(jnp.mean(values * values, axis=-1, keepdims=True) + epsilon)


def norm_back(grad_normed, values, scale):
    inner = jnp.mean(grad_normed * values, axis=-1, keepdims=True)
    return scale * (grad_normed - values * scale * scale * inner)


def contract_rows(left, right):
    return lax.dot_general(
        left, right, (((0,), (0,)), ((), ())), preferred_element_type=jnp.float32
    )


def contract_cols(left, right):
    return lax.dot_general(
        left, right, (((1,), (1,)), ((), ())), preferred_element_type=jnp.float32
    )


def by_member(shard, parts):
    rows, columns = shard.shape
    width = columns // (parts * 2 * HALF)
    split = shard.reshape(rows, parts, 2, PLANE, 2, width)
    return split.transpose(2, 4, 0, 1, 3, 5).reshape(4, rows, columns // 4)


def from_members(blocks, parts):
    members, rows, columns = blocks.shape
    width = columns // (parts * PLANE)
    split = blocks.reshape(2, 2, rows, parts, PLANE, width)
    return split.transpose(2, 3, 0, 4, 1, 5).reshape(rows, 4 * columns)


def team_swap(blocks):
    return lax.all_to_all(blocks, "fsdp", 0, 0, tiled=True, axis_index_groups=TEAMS)


def plane_gather(value, axis):
    return lax.all_gather(value, "fsdp", axis=axis, tiled=True, axis_index_groups=PLANES)


def plane_scatter(value, axis):
    return lax.psum_scatter(
        value, "fsdp", scatter_dimension=axis, tiled=True, axis_index_groups=PLANES
    )


def gather_rows(blocks):
    members, rows, columns = blocks.shape
    return plane_gather(blocks.reshape(2, 2 * rows, columns), 1).reshape(-1, columns)


def scatter_rows(value):
    total, columns = value.shape
    shared = plane_scatter(value.reshape(2, total // 2, columns), 1)
    return shared.reshape(4, -1, columns)


def team_tokens(own):
    pair = jnp.stack([own, to_z(own)])
    return with_core(pair)


def with_core(pair):
    other = to_core(pair)
    return jnp.stack([pair[0], other[0], pair[1], other[1]])


def core_sum(partial):
    sent = jnp.stack([partial[1], partial[3]]).astype(jnp.bfloat16)
    return jnp.stack([partial[0], partial[2]]) + to_core(sent).astype(jnp.float32)


def team_sum(partial):
    pair = core_sum(partial)
    other = to_z(pair.astype(jnp.bfloat16)).astype(jnp.float32)
    return pair + other[::-1]


def own_sum(partial):
    pair = core_sum(partial)
    return pair[0] + to_z(pair[1].astype(jnp.bfloat16)).astype(jnp.float32)


def body(
    tokens, gain_first, w_in, conv_weight, w_out, gain_second, w_gate, w_up, w_down, cotangent
):
    low, wide = jnp.bfloat16, jnp.float32
    length, model_width = tokens.shape
    position = lax.axis_index("fsdp")
    core, plane, z = position % 2, position // 2 % PLANE, position // HALF
    rows = w_in.shape[0]
    channels = model_width // 4

    gains = jnp.pad(jnp.stack([gain_first, gain_second], 1), ((0, 0), (0, 126)))
    in_pack = jnp.concatenate(
        [by_member(w_in, 3), jnp.broadcast_to(gains, (4,) + gains.shape)], 2
    )
    in_all = gather_rows(team_swap(in_pack))
    out_pack = jnp.concatenate([w_out, jnp.pad(conv_weight, ((0, 0), (0, 125)))], 1)
    out_all = plane_gather(out_pack, 0)
    ff_pack = team_swap(jnp.concatenate([by_member(w_gate, 1), by_member(w_up, 1)], 2))
    ff_all = gather_rows(ff_pack)
    down_full = plane_gather(w_down, 0)

    in_full = in_all[:, : 3 * channels]
    gain_one = in_all[:, 3 * channels].astype(wide)
    gain_two = in_all[:, 3 * channels + 1].astype(wide)
    out_full = out_all[:, :model_width]
    kernel = out_all[:, model_width : model_width + 3].astype(wide).T
    units = ff_all.shape[1] // 2
    gate_full, up_full = ff_all[:, :units], ff_all[:, units:]

    team_inputs = team_tokens(tokens)
    team_outer = team_tokens(cotangent)
    outer_flat = team_outer.reshape(4 * length, model_width)

    inputs = team_inputs.astype(wide)
    scale_one = norm_scale(inputs)
    normed = (inputs * scale_one * gain_one).astype(low).reshape(4 * length, model_width)
    projected = jnp.dot(normed, in_full, preferred_element_type=wide)
    in_gate = projected[:, :channels].reshape(4, length, channels)
    out_gate = projected[:, channels : 2 * channels].reshape(4, length, channels)
    carried = projected[:, 2 * channels :].reshape(4, length, channels)
    mixed = (in_gate * carried).astype(low)

    def by_core(first, second):
        return jnp.where(core == 0, first, second)

    tails = mixed[:, length - 2 :]
    sent = by_core(tails[1::2], tails[0::2])
    received = lax.ppermute(sent, "fsdp", TO_NEXT)
    nothing = jnp.zeros_like(received[0])
    shifted = jnp.where(
        z == 0, jnp.stack([nothing, received[0]]), jnp.stack([received[1], nothing])
    )
    before = jnp.where(plane == 0, shifted, received)
    own_before = by_core(before, tails[1::2])
    other_before = by_core(tails[0::2], before)
    earlier = jnp.stack([own_before[0], other_before[0], own_before[1], other_before[1]])
    extended = jnp.concatenate([earlier, mixed], 1).astype(wide)
    lagged = (extended[:, 2:], extended[:, 1 : length + 1], extended[:, :length])
    convolved = kernel[0] * lagged[0] + kernel[1] * lagged[1] + kernel[2] * lagged[2]
    gated = (out_gate * convolved).astype(low).reshape(4 * length, channels)
    branch = jnp.dot(gated, out_full, preferred_element_type=wide)
    middle = jnp.stack([inputs[0], inputs[2]]) + team_sum(
        branch.reshape(4, length, model_width)
    )
    scale_two = norm_scale(middle)
    normed_two = with_core((middle * scale_two * gain_two).astype(low))
    normed_two = normed_two.reshape(4 * length, model_width)
    gate_value = jnp.dot(normed_two, gate_full, preferred_element_type=wide)
    up_value = jnp.dot(normed_two, up_full, preferred_element_type=wide)
    sigmoid_gate = jax.nn.sigmoid(gate_value)
    silu_gate = gate_value * sigmoid_gate
    hidden = (silu_gate * up_value).astype(low)

    grad_hidden = contract_cols(outer_flat, down_full)
    grad_gate = (
        grad_hidden * up_value * sigmoid_gate * (1.0 + gate_value * (1.0 - sigmoid_gate))
    ).astype(low)
    grad_upper = (grad_hidden * silu_gate).astype(low)
    grad_down = contract_rows(hidden, outer_flat).astype(low)
    grad_gate_w = contract_rows(normed_two, grad_gate).astype(low)
    grad_up_w = contract_rows(normed_two, grad_upper).astype(low)
    down_share = plane_scatter(grad_down, 0)
    ff_share = scatter_rows(jnp.concatenate([grad_gate_w, grad_up_w], 1))

    grad_normed_two = contract_cols(grad_gate, gate_full) + contract_cols(grad_upper, up_full)
    grad_normed_two = team_sum(grad_normed_two.reshape(4, length, model_width))
    grad_gain_two = jnp.sum(grad_normed_two[0] * middle[0] * scale_two[0], axis=0)
    outer = jnp.stack([team_outer[0], team_outer[2]]).astype(wide)
    grad_middle = outer + norm_back(grad_normed_two * gain_two, middle, scale_two)
    grad_branch = with_core(grad_middle.astype(low)).reshape(4 * length, model_width)

    down_term = jnp.dot(hidden, down_full, preferred_element_type=wide)
    result = middle[0] + own_sum(down_term.reshape(4, length, model_width))

    grad_out_w = contract_rows(gated, grad_branch)
    grad_gated = contract_cols(grad_branch, out_full).reshape(4, length, channels)
    grad_out_gate = grad_gated * convolved
    grad_conv = grad_gated * out_gate
    grad_kernel = jnp.stack([jnp.sum(grad_conv * rows_of, axis=(0, 1)) for rows_of in lagged], 1)

    heads = grad_conv[:, :2]
    sent = by_core(heads[0::2], heads[1::2])
    received = lax.ppermute(sent, "fsdp", TO_PREVIOUS)
    nothing = jnp.zeros_like(received[0])
    shifted = jnp.where(
        z == 0, jnp.stack([received[1], nothing]), jnp.stack([nothing, received[0]])
    )
    after = jnp.where(plane == PLANE - 1, shifted, received)
    own_after = by_core(heads[1::2], after)
    other_after = by_core(after, heads[0::2])
    later = jnp.stack([own_after[0], other_after[0], own_after[1], other_after[1]])
    grad_long = jnp.concatenate([grad_conv, later], 1)
    grad_mixed = (
        kernel[0] * grad_long[:, :length]
        + kernel[1] * grad_long[:, 1 : length + 1]
        + kernel[2] * grad_long[:, 2:]
    )
    grad_projected = jnp.concatenate(
        [
            (grad_mixed * carried).astype(low),
            grad_out_gate.astype(low),
            (grad_mixed * in_gate).astype(low),
        ],
        2,
    ).reshape(4 * length, 3 * channels)
    grad_in_w = contract_rows(normed, grad_projected)
    grad_normed = contract_cols(grad_projected, in_full).reshape(4, length, model_width)
    grad_gain_one = jnp.sum(grad_normed * inputs * scale_one, axis=(0, 1))

    in_grads = jnp.concatenate(
        [
            grad_in_w,
            jnp.pad(jnp.stack([grad_gain_one, grad_gain_two], 1), ((0, 0), (0, 126))),
        ],
        1,
    ).astype(low)
    out_grads = jnp.concatenate(
        [grad_out_w, jnp.pad(grad_kernel, ((0, 0), (0, 125)))], 1
    ).astype(low)
    in_share = scatter_rows(in_grads)
    out_share = plane_scatter(out_grads, 0)

    grad_normed_own = own_sum(grad_normed)
    grad_inputs = grad_middle[0] + norm_back(
        grad_normed_own * gain_one, inputs[0], scale_one[0]
    )

    def all_reps(blocks):
        swapped = lax.all_to_all(
            jnp.concatenate([blocks, blocks]),
            ("rep", "fsdp"),
            0,
            0,
            tiled=True,
            axis_index_groups=BOTH_TEAMS,
        )
        return swapped[:4].astype(wide) + swapped[4:].astype(wide)

    def both_reps(value):
        other = lax.ppermute(value, "rep", [(0, 1), (1, 0)])
        return value.astype(wide) + other.astype(wide)

    in_total = all_reps(in_share)
    ff_total = all_reps(ff_share)
    out_total = both_reps(out_share)
    down_total = both_reps(down_share)
    gain_total = jnp.sum(in_total[:, :, 3 * channels : 3 * channels + 2], axis=0)

    return (
        result.astype(low),
        grad_inputs,
        gain_total[:, 0],
        from_members(in_total[:, :, : 3 * channels], 3),
        out_total[:, model_width : model_width + 3],
        out_total[:, :model_width],
        gain_total[:, 1],
        from_members(ff_total[:, :, :units], 1),
        from_members(ff_total[:, :, units:], 1),
        down_total,
    )


def solution(mesh):
    return jax.shard_map(
        body,
        mesh=mesh,
        in_specs=(
            P(("rep", "fsdp"), None),
            P("fsdp"),
            P("fsdp", None),
            P("fsdp", None),
            P("fsdp", None),
            P("fsdp"),
            P("fsdp", None),
            P("fsdp", None),
            P("fsdp", None),
            P(("rep", "fsdp"), None),
        ),
        out_specs=(
            P(("rep", "fsdp"), None),
            P(("rep", "fsdp"), None),
            P("fsdp"),
            P("fsdp", None),
            P("fsdp", None),
            P("fsdp", None),
            P("fsdp"),
            P("fsdp", None),
            P("fsdp", None),
            P("fsdp", None),
        ),
        check_vma=False,
    )
```

```python
import jax
import jax.numpy as jnp
from jax import lax
from jax.sharding import PartitionSpec as P

epsilon = 1e-05

SIDE = 4
PLANE = SIDE * SIDE
HALF = PLANE * 2


def place(z, plane, core):
    return (z * PLANE + plane) * 2 + core


def moves(target):
    return [
        (place(z, plane, core), place(*target(z, plane, core)))
        for z in range(2)
        for plane in range(PLANE)
        for core in range(2)
    ]


TO_CORE = moves(lambda z, plane, core: (z, plane, 1 - core))
TO_Z = moves(lambda z, plane, core: (1 - z, plane, core))
TO_NEXT = moves(lambda z, plane, core: (z, (plane + 1) % PLANE, core))
TO_PREVIOUS = moves(lambda z, plane, core: (z, (plane - 1) % PLANE, core))
TEAMS = [
    [place(z, plane, core) for z in range(2) for core in range(2)] for plane in range(PLANE)
]
PLANES = [
    [place(z, plane, core) for plane in range(PLANE)] for z in range(2) for core in range(2)
]
BOTH_TEAMS = [[rep * 2 * HALF + member for rep in range(2) for member in team] for team in TEAMS]


def to_core(value):
    return lax.ppermute(value, "fsdp", TO_CORE)


def to_z(value):
    return lax.ppermute(value, "fsdp", TO_Z)


def norm_scale(values):
    return lax.rsqrt(jnp.mean(values * values, axis=-1, keepdims=True) + epsilon)


def norm_back(grad_normed, values, scale):
    inner = jnp.mean(grad_normed * values, axis=-1, keepdims=True)
    return scale * (grad_normed - values * scale * scale * inner)


def contract_rows(left, right):
    return lax.dot_general(
        left, right, (((0,), (0,)), ((), ())), preferred_element_type=jnp.float32
    )


def contract_cols(left, right):
    return lax.dot_general(
        left, right, (((1,), (1,)), ((), ())), preferred_element_type=jnp.float32
    )


def by_member(shard):
    rows, columns = shard.shape
    split = shard.reshape(rows, 3, 2, PLANE, 2, -1)
    return split.transpose(2, 4, 0, 1, 3, 5).reshape(4, rows, columns // 4)


def from_members(blocks):
    members, rows, columns = blocks.shape
    split = blocks.reshape(2, 2, rows, 3, PLANE, -1)
    return split.transpose(2, 3, 0, 4, 1, 5).reshape(rows, 4 * columns)


def units_by_member(shard, block):
    rows, columns = shard.shape
    split = shard.reshape(rows, 2, PLANE, 2, -1)
    main = split[..., :block].reshape(rows, 2, PLANE, 2, 2, 2, block // 4)
    main = main.transpose(1, 3, 0, 4, 2, 5, 6).reshape(4, rows, PLANE * block)
    rest = split[..., block:].transpose(1, 3, 0, 2, 4).reshape(4, rows, -1)
    return jnp.concatenate([main, rest], 2)


def units_from_members(blocks, block):
    members, rows, columns = blocks.shape
    main = blocks[:, :, : PLANE * block].reshape(2, 2, rows, 2, PLANE, 2, block // 4)
    main = main.transpose(2, 0, 4, 1, 3, 5, 6).reshape(rows, 2, PLANE, 2, block)
    rest = blocks[:, :, PLANE * block :].reshape(2, 2, rows, PLANE, -1)
    return jnp.concatenate([main, rest.transpose(2, 0, 3, 1, 4)], 4).reshape(rows, 4 * columns)


def team_swap(blocks):
    return lax.all_to_all(blocks, "fsdp", 0, 0, tiled=True, axis_index_groups=TEAMS)


def plane_swap(blocks):
    return lax.all_to_all(blocks, "fsdp", 0, 0, tiled=True, axis_index_groups=PLANES)


def gather_rows(blocks):
    members, rows, columns = blocks.shape
    return lax.all_gather(
        blocks.reshape(2, 2 * rows, columns),
        "fsdp",
        axis=1,
        tiled=True,
        axis_index_groups=PLANES,
    ).reshape(-1, columns)


def scatter_rows(value):
    total, columns = value.shape
    return lax.psum_scatter(
        value.reshape(2, total // 2, columns),
        "fsdp",
        scatter_dimension=1,
        tiled=True,
        axis_index_groups=PLANES,
    ).reshape(4, -1, columns)


def team_tokens(own):
    pair = jnp.stack([own, to_z(own)])
    return with_core(pair)


def with_core(pair):
    other = to_core(pair)
    return jnp.stack([pair[0], other[0], pair[1], other[1]])


def core_sum(partial):
    sent = jnp.stack([partial[1], partial[3]]).astype(jnp.bfloat16)
    return jnp.stack([partial[0], partial[2]]) + to_core(sent).astype(jnp.float32)


def team_sum(partial):
    pair = core_sum(partial)
    other = to_z(pair.astype(jnp.bfloat16)).astype(jnp.float32)
    return pair + other[::-1]


def own_sum(partial):
    pair = core_sum(partial)
    return pair[0] + to_z(pair[1].astype(jnp.bfloat16)).astype(jnp.float32)


def body(
    tokens, gain_first, w_in, conv_weight, w_out, gain_second, w_gate, w_up, w_down, cotangent
):
    low, wide = jnp.bfloat16, jnp.float32
    length, model_width = tokens.shape
    position = lax.axis_index("fsdp")
    core, plane, z = position % 2, position // 2 % PLANE, position // HALF
    rows = w_in.shape[0]
    channels = model_width // 4

    block = 4 * rows
    rest = w_down.shape[0] - block
    down_main = w_down[:block].reshape(4, rows, model_width)
    down_rest = w_down[block:].reshape(rest, block // rest, -1).transpose(1, 0, 2)
    ff_pack = jnp.concatenate(
        [units_by_member(w_gate, block), units_by_member(w_up, block)], 2
    )
    ff_swapped = team_swap(ff_pack)
    ff_all = gather_rows(
        jnp.concatenate([ff_swapped, down_main, down_rest.reshape(4, rows, -1)], 2)
    )

    gains = jnp.pad(jnp.stack([gain_first, gain_second], 1), ((0, 0), (0, 126)))
    in_pack = jnp.concatenate(
        [by_member(w_in), jnp.broadcast_to(gains, (4,) + gains.shape)], 2
    )
    in_pack = lax.optimization_barrier((in_pack, ff_swapped))[0]
    in_pack = jnp.broadcast_to(
        in_pack.reshape(2, 1, 2, rows, -1), (2, PLANE, 2, rows, in_pack.shape[2])
    ).reshape(2 * HALF, rows, -1)
    in_all = lax.all_to_all(in_pack, "fsdp", 0, 0, tiled=True).reshape(model_width, -1)
    out_pack = jnp.concatenate([w_out, jnp.pad(conv_weight, ((0, 0), (0, 125)))], 1)
    out_all = plane_swap(jnp.broadcast_to(out_pack, (PLANE,) + out_pack.shape))
    out_all = out_all.reshape(channels, -1)

    in_full = in_all[:, : 3 * channels]
    gain_one = in_all[:, 3 * channels].astype(wide)
    gain_two = in_all[:, 3 * channels + 1].astype(wide)
    out_full = out_all[:, :model_width]
    kernel = out_all[:, model_width : model_width + 3].astype(wide).T
    units = w_down.shape[0] * PLANE
    gate_up_full = ff_all[:, : 2 * units]
    rest_rows = ff_all[:, 2 * units + model_width :].reshape(2, PLANE, 2 * rows, -1)
    rest_rows = rest_rows.transpose(1, 0, 2, 3).reshape(PLANE, block // rest, rest, -1)
    rest_rows = rest_rows.transpose(0, 2, 1, 3).reshape(PLANE * rest, model_width)
    down_full = jnp.concatenate([ff_all[:, 2 * units : 2 * units + model_width], rest_rows], 0)

    team_inputs = team_tokens(tokens)
    team_outer = team_tokens(lax.optimization_barrier((cotangent, in_all))[0])
    outer_flat = team_outer.reshape(4 * length, model_width)

    inputs = team_inputs.astype(wide)
    scale_one = norm_scale(inputs)
    normed = (inputs * scale_one * gain_one).astype(low).reshape(4 * length, model_width)
    projected = jnp.dot(normed, in_full, preferred_element_type=wide)
    in_gate = projected[:, :channels].reshape(4, length, channels)
    out_gate = projected[:, channels : 2 * channels].reshape(4, length, channels)
    carried = projected[:, 2 * channels :].reshape(4, length, channels)
    mixed = (in_gate * carried).astype(low)

    def by_core(first, second):
        return jnp.where(core == 0, first, second)

    tails = mixed[:, length - 2 :]
    sent = by_core(tails[1::2], tails[0::2])
    received = lax.ppermute(sent, "fsdp", TO_NEXT)
    nothing = jnp.zeros_like(received[0])
    shifted = jnp.where(
        z == 0, jnp.stack([nothing, received[0]]), jnp.stack([received[1], nothing])
    )
    before = jnp.where(plane == 0, shifted, received)
    own_before = by_core(before, tails[1::2])
    other_before = by_core(tails[0::2], before)
    earlier = jnp.stack([own_before[0], other_before[0], own_before[1], other_before[1]])
    extended = jnp.concatenate([earlier, mixed], 1).astype(wide)
    lagged = (extended[:, 2:], extended[:, 1 : length + 1], extended[:, :length])
    convolved = kernel[0] * lagged[0] + kernel[1] * lagged[1] + kernel[2] * lagged[2]
    gated = (out_gate * convolved).astype(low).reshape(4 * length, channels)
    branch = jnp.dot(gated, out_full, preferred_element_type=wide)
    middle = jnp.stack([inputs[0], inputs[2]]) + team_sum(
        branch.reshape(4, length, model_width)
    )
    scale_two = norm_scale(middle)
    normed_two = with_core((middle * scale_two * gain_two).astype(low))
    normed_two = normed_two.reshape(4 * length, model_width)
    gate_up = jnp.dot(normed_two, gate_up_full, preferred_element_type=wide)
    gate_value, up_value = gate_up[:, :units], gate_up[:, units:]
    sigmoid_gate = jax.nn.sigmoid(gate_value)
    silu_gate = gate_value * sigmoid_gate
    hidden = (silu_gate * up_value).astype(low)

    grad_hidden = contract_cols(outer_flat, down_full)
    grad_gate = (
        grad_hidden * up_value * sigmoid_gate * (1.0 + gate_value * (1.0 - sigmoid_gate))
    ).astype(low)
    grad_upper = (grad_hidden * silu_gate).astype(low)
    grad_gate_up = jnp.concatenate([grad_gate, grad_upper], 1)
    grad_normed_two = contract_cols(grad_gate_up, gate_up_full)
    grad_down = contract_rows(hidden, outer_flat).astype(low)
    grad_gate_up_w = contract_rows(normed_two, grad_gate_up).astype(low)
    grad_rest = grad_down[model_width:].reshape(PLANE, rest, block // rest, -1)
    grad_rest = grad_rest.transpose(0, 2, 1, 3).reshape(PLANE, 2, 2 * rows, -1)
    grad_rest = grad_rest.transpose(1, 0, 2, 3).reshape(model_width, -1)
    ff_grads = jnp.concatenate([grad_gate_up_w, grad_down[:model_width], grad_rest], 1)
    down_term = jnp.dot(hidden, down_full, preferred_element_type=wide)

    grad_pair = core_sum(grad_normed_two.reshape(4, length, model_width))
    grad_other = to_z(grad_pair.astype(low))
    grad_other, ff_grads, down_term = lax.optimization_barrier((grad_other, ff_grads, down_term))
    ff_share = scatter_rows(ff_grads)
    grad_normed_two = grad_pair + grad_other.astype(wide)[::-1]
    grad_gain_two = jnp.sum(grad_normed_two[0] * middle[0] * scale_two[0], axis=0)
    outer = jnp.stack([team_outer[0], team_outer[2]]).astype(wide)
    grad_middle = outer + norm_back(grad_normed_two * gain_two, middle, scale_two)
    grad_branch = with_core(grad_middle.astype(low)).reshape(4 * length, model_width)

    result = middle[0] + own_sum(down_term.reshape(4, length, model_width))

    grad_out_w = contract_rows(gated, grad_branch)
    grad_gated = contract_cols(grad_branch, out_full).reshape(4, length, channels)
    grad_out_gate = grad_gated * convolved
    grad_conv = grad_gated * out_gate
    grad_kernel = jnp.stack([jnp.sum(grad_conv * rows_of, axis=(0, 1)) for rows_of in lagged], 1)

    heads = grad_conv[:, :2]
    sent = by_core(heads[0::2], heads[1::2])
    received = lax.ppermute(sent, "fsdp", TO_PREVIOUS)
    nothing = jnp.zeros_like(received[0])
    shifted = jnp.where(
        z == 0, jnp.stack([received[1], nothing]), jnp.stack([nothing, received[0]])
    )
    after = jnp.where(plane == PLANE - 1, shifted, received)
    own_after = by_core(heads[1::2], after)
    other_after = by_core(after, heads[0::2])
    later = jnp.stack([own_after[0], other_after[0], own_after[1], other_after[1]])
    grad_long = jnp.concatenate([grad_conv, later], 1)
    grad_mixed = (
        kernel[0] * grad_long[:, :length]
        + kernel[1] * grad_long[:, 1 : length + 1]
        + kernel[2] * grad_long[:, 2:]
    )
    grad_projected = jnp.concatenate(
        [
            (grad_mixed * carried).astype(low),
            grad_out_gate.astype(low),
            (grad_mixed * in_gate).astype(low),
        ],
        2,
    ).reshape(4 * length, 3 * channels)
    grad_in_w = contract_rows(normed, grad_projected)
    grad_normed = contract_cols(grad_projected, in_full).reshape(4, length, model_width)
    grad_gain_one = jnp.sum(grad_normed * inputs * scale_one, axis=(0, 1))

    in_grads = jnp.concatenate(
        [
            grad_in_w,
            jnp.pad(jnp.stack([grad_gain_one, grad_gain_two], 1), ((0, 0), (0, 126))),
        ],
        1,
    ).astype(low)
    out_grads = jnp.concatenate(
        [grad_out_w, jnp.pad(grad_kernel, ((0, 0), (0, 125)))], 1
    ).astype(low)
    in_share = lax.all_to_all(
        in_grads.reshape(2 * HALF, rows, -1), "fsdp", 0, 0, tiled=True
    ).reshape(2, PLANE, 2, rows, -1)
    in_share = jnp.sum(in_share.astype(wide), axis=1).astype(low).reshape(4, rows, -1)
    out_share = plane_swap(out_grads.reshape(PLANE, rows, -1))
    out_share = jnp.sum(out_share.astype(wide), axis=0).astype(low)

    grad_normed_own = own_sum(grad_normed)
    grad_inputs = grad_middle[0] + norm_back(
        grad_normed_own * gain_one, inputs[0], scale_one[0]
    )

    def all_reps(blocks):
        swapped = lax.all_to_all(
            jnp.concatenate([blocks, blocks]),
            ("rep", "fsdp"),
            0,
            0,
            tiled=True,
            axis_index_groups=BOTH_TEAMS,
        )
        return swapped[:4].astype(wide) + swapped[4:].astype(wide)

    def both_reps(value):
        other = lax.ppermute(value, "rep", [(0, 1), (1, 0)])
        return value.astype(wide) + other.astype(wide)

    in_total = both_reps(in_share)
    out_total = both_reps(out_share)
    ff_total = all_reps(ff_share[:, :, : 2 * units])
    down_total = both_reps(ff_share[:, :, 2 * units :])
    down_rest = down_total[:, :, model_width:].reshape(block // rest, rest, -1)
    down_rest = down_rest.transpose(1, 0, 2).reshape(rest, model_width)
    down_total = jnp.concatenate(
        [down_total[:, :, :model_width].reshape(block, model_width), down_rest], 0
    )
    gain_total = jnp.sum(in_total[:, :, 3 * channels : 3 * channels + 2], axis=0)

    return (
        result.astype(low),
        grad_inputs,
        gain_total[:, 0],
        from_members(in_total[:, :, : 3 * channels]),
        out_total[:, model_width : model_width + 3],
        out_total[:, :model_width],
        gain_total[:, 1],
        units_from_members(ff_total[:, :, :units], block),
        units_from_members(ff_total[:, :, units:], block),
        down_total,
    )


def solution(mesh):
    return jax.shard_map(
        body,
        mesh=mesh,
        in_specs=(
            P(("rep", "fsdp"), None),
            P("fsdp"),
            P("fsdp", None),
            P("fsdp", None),
            P("fsdp", None),
            P("fsdp"),
            P("fsdp", None),
            P("fsdp", None),
            P("fsdp", None),
            P(("rep", "fsdp"), None),
        ),
        out_specs=(
            P(("rep", "fsdp"), None),
            P(("rep", "fsdp"), None),
            P("fsdp"),
            P("fsdp", None),
            P("fsdp", None),
            P("fsdp", None),
            P("fsdp"),
            P("fsdp", None),
            P("fsdp", None),
            P("fsdp", None),
        ),
        check_vma=False,
    )
```

```python
import jax
import jax.numpy as jnp
from jax import lax
from jax.sharding import PartitionSpec as P

epsilon = 1e-05

SIDE = 4
PLANE = SIDE * SIDE
HALF = PLANE * 2


def place(z, plane, core):
    return (z * PLANE + plane) * 2 + core


def moves(target):
    return [
        (place(z, plane, core), place(*target(z, plane, core)))
        for z in range(2)
        for plane in range(PLANE)
        for core in range(2)
    ]


TO_CORE = moves(lambda z, plane, core: (z, plane, 1 - core))
TO_Z = moves(lambda z, plane, core: (1 - z, plane, core))
TO_NEXT = moves(lambda z, plane, core: (z, (plane + 1) % PLANE, core))
TO_PREVIOUS = moves(lambda z, plane, core: (z, (plane - 1) % PLANE, core))
TEAMS = [
    [place(z, plane, core) for z in range(2) for core in range(2)] for plane in range(PLANE)
]
PLANES = [
    [place(z, plane, core) for plane in range(PLANE)] for z in range(2) for core in range(2)
]
BOTH_TEAMS = [[rep * 2 * HALF + member for rep in range(2) for member in team] for team in TEAMS]


def to_core(value):
    return lax.ppermute(value, "fsdp", TO_CORE)


def to_z(value):
    return lax.ppermute(value, "fsdp", TO_Z)


def norm_scale(values):
    return lax.rsqrt(jnp.mean(values * values, axis=-1, keepdims=True) + epsilon)


def norm_back(grad_normed, values, scale):
    inner = jnp.mean(grad_normed * values, axis=-1, keepdims=True)
    return scale * (grad_normed - values * scale * scale * inner)


def contract_rows(left, right):
    return lax.dot_general(
        left, right, (((0,), (0,)), ((), ())), preferred_element_type=jnp.float32
    )


def contract_cols(left, right):
    return lax.dot_general(
        left, right, (((1,), (1,)), ((), ())), preferred_element_type=jnp.float32
    )


def by_member(shard, parts):
    rows, columns = shard.shape
    split = shard.reshape(rows, parts, 2, PLANE, 2, -1)
    return split.transpose(2, 4, 0, 1, 3, 5).reshape(4, rows, columns // 4)


def from_members(blocks, parts):
    members, rows, columns = blocks.shape
    split = blocks.reshape(2, 2, rows, parts, PLANE, -1)
    return split.transpose(2, 3, 0, 4, 1, 5).reshape(rows, 4 * columns)


def team_swap(blocks):
    return lax.all_to_all(blocks, "fsdp", 0, 0, tiled=True, axis_index_groups=TEAMS)


def plane_swap(blocks):
    return lax.all_to_all(blocks, "fsdp", 0, 0, tiled=True, axis_index_groups=PLANES)


def gather_rows(blocks):
    members, rows, columns = blocks.shape
    return lax.all_gather(
        blocks.reshape(2, 2 * rows, columns),
        "fsdp",
        axis=1,
        tiled=True,
        axis_index_groups=PLANES,
    ).reshape(-1, columns)


def scatter_rows(value):
    total, columns = value.shape
    return lax.psum_scatter(
        value.reshape(2, total // 2, columns),
        "fsdp",
        scatter_dimension=1,
        tiled=True,
        axis_index_groups=PLANES,
    ).reshape(4, -1, columns)


def team_tokens(own):
    return with_core(jnp.stack([own, to_z(own)]))


def with_core(pair):
    other = to_core(pair)
    return jnp.stack([pair[0], other[0], pair[1], other[1]])


def core_sum(partial):
    sent = jnp.stack([partial[1], partial[3]]).astype(jnp.bfloat16)
    return jnp.stack([partial[0], partial[2]]) + to_core(sent).astype(jnp.float32)


def team_sum(partial):
    pair = core_sum(partial)
    other = to_z(pair.astype(jnp.bfloat16)).astype(jnp.float32)
    return pair + other[::-1]


def own_sum(partial):
    pair = core_sum(partial)
    return pair[0] + to_z(pair[1].astype(jnp.bfloat16)).astype(jnp.float32)


def body(
    tokens, gain_first, w_in, conv_weight, w_out, gain_second, w_gate, w_up, w_down, cotangent
):
    low, wide = jnp.bfloat16, jnp.float32
    length, model_width = tokens.shape
    position = lax.axis_index("fsdp")
    core, plane, z = position % 2, position // 2 % PLANE, position // HALF
    rows = w_in.shape[0]
    channels = model_width // 4

    block = 4 * rows
    rest = w_down.shape[0] - block
    down_main = w_down[:block].reshape(4, rows, model_width)
    down_rest = w_down[block:].reshape(rest, block // rest, -1).transpose(1, 0, 2)
    ff_pack = jnp.concatenate([by_member(w_gate, 1), by_member(w_up, 1)], 2)
    ff_swapped = team_swap(ff_pack)
    ff_all = gather_rows(
        jnp.concatenate([ff_swapped, down_main, down_rest.reshape(4, rows, -1)], 2)
    )

    gains = jnp.pad(jnp.stack([gain_first, gain_second], 1), ((0, 0), (0, 126)))
    in_pack = jnp.concatenate(
        [by_member(w_in, 3), jnp.broadcast_to(gains, (4,) + gains.shape)], 2
    )
    in_pack = lax.optimization_barrier((in_pack, ff_swapped))[0]
    in_pack = jnp.broadcast_to(
        in_pack.reshape(2, 1, 2, rows, -1), (2, PLANE, 2, rows, in_pack.shape[2])
    ).reshape(2 * HALF, rows, -1)
    in_all = lax.all_to_all(in_pack, "fsdp", 0, 0, tiled=True).reshape(model_width, -1)
    out_pack = jnp.concatenate([w_out, jnp.pad(conv_weight, ((0, 0), (0, 125)))], 1)
    out_pack = lax.optimization_barrier((out_pack, in_all))[0]
    out_all = plane_swap(jnp.broadcast_to(out_pack, (PLANE,) + out_pack.shape))
    out_all = out_all.reshape(channels, -1)

    in_full = in_all[:, : 3 * channels]
    gain_one = in_all[:, 3 * channels].astype(wide)
    gain_two = in_all[:, 3 * channels + 1].astype(wide)
    out_full = out_all[:, :model_width]
    kernel = out_all[:, model_width : model_width + 3].astype(wide).T
    units = w_down.shape[0] * PLANE
    gate_up_full = ff_all[:, : 2 * units]
    main_rows = ff_all[:, 2 * units : 2 * units + model_width].reshape(2, PLANE, 2 * rows, -1)
    main_rows = main_rows.transpose(1, 0, 2, 3).reshape(PLANE, block, model_width)
    rest_rows = ff_all[:, 2 * units + model_width :].reshape(2, PLANE, 2 * rows, -1)
    rest_rows = rest_rows.transpose(1, 0, 2, 3).reshape(PLANE, block // rest, rest, -1)
    rest_rows = rest_rows.transpose(0, 2, 1, 3).reshape(PLANE, rest, model_width)
    down_full = jnp.concatenate([main_rows, rest_rows], 1).reshape(units, model_width)

    team_values = team_tokens(jnp.stack([tokens, cotangent]))
    team_inputs, team_outer = team_values[:, 0], team_values[:, 1]
    outer_flat = team_outer.reshape(4 * length, model_width)

    inputs = team_inputs.astype(wide)
    scale_one = norm_scale(inputs)
    normed = (inputs * scale_one * gain_one).astype(low).reshape(4 * length, model_width)
    projected = jnp.dot(normed, in_full, preferred_element_type=wide)
    in_gate = projected[:, :channels].reshape(4, length, channels)
    out_gate = projected[:, channels : 2 * channels].reshape(4, length, channels)
    carried = projected[:, 2 * channels :].reshape(4, length, channels)
    mixed = (in_gate * carried).astype(low)

    def by_core(first, second):
        return jnp.where(core == 0, first, second)

    tails = mixed[:, length - 2 :]
    sent = by_core(tails[1::2], tails[0::2])
    received = lax.ppermute(sent, "fsdp", TO_NEXT)
    nothing = jnp.zeros_like(received[0])
    shifted = jnp.where(
        z == 0, jnp.stack([nothing, received[0]]), jnp.stack([received[1], nothing])
    )
    before = jnp.where(plane == 0, shifted, received)
    own_before = by_core(before, tails[1::2])
    other_before = by_core(tails[0::2], before)
    earlier = jnp.stack([own_before[0], other_before[0], own_before[1], other_before[1]])
    extended = jnp.concatenate([earlier, mixed], 1).astype(wide)
    lagged = (extended[:, 2:], extended[:, 1 : length + 1], extended[:, :length])
    convolved = kernel[0] * lagged[0] + kernel[1] * lagged[1] + kernel[2] * lagged[2]
    gated = (out_gate * convolved).astype(low).reshape(4 * length, channels)
    branch = jnp.dot(gated, out_full, preferred_element_type=wide)
    middle = jnp.stack([inputs[0], inputs[2]]) + team_sum(
        branch.reshape(4, length, model_width)
    )
    scale_two = norm_scale(middle)
    normed_two = with_core((middle * scale_two * gain_two).astype(low))
    normed_two = normed_two.reshape(4 * length, model_width)
    gate_up = jnp.dot(normed_two, gate_up_full, preferred_element_type=wide)
    gate_value, up_value = gate_up[:, :units], gate_up[:, units:]
    sigmoid_gate = jax.nn.sigmoid(gate_value)
    silu_gate = gate_value * sigmoid_gate
    hidden = (silu_gate * up_value).astype(low)

    grad_hidden = contract_cols(outer_flat, down_full)
    grad_gate = (
        grad_hidden * up_value * sigmoid_gate * (1.0 + gate_value * (1.0 - sigmoid_gate))
    ).astype(low)
    grad_upper = (grad_hidden * silu_gate).astype(low)
    grad_gate_up = jnp.concatenate([grad_gate, grad_upper], 1)
    grad_normed_two = contract_cols(grad_gate_up, gate_up_full)
    grad_down = contract_rows(hidden, outer_flat).astype(low)
    grad_gate_up_w = contract_rows(normed_two, grad_gate_up).astype(low)
    grad_down = grad_down.reshape(PLANE, block + rest, model_width)
    grad_main = grad_down[:, :block].reshape(PLANE, 2, 2 * rows, -1)
    grad_main = grad_main.transpose(1, 0, 2, 3).reshape(model_width, -1)
    grad_rest = grad_down[:, block:].reshape(PLANE, rest, block // rest, -1)
    grad_rest = grad_rest.transpose(0, 2, 1, 3).reshape(PLANE, 2, 2 * rows, -1)
    grad_rest = grad_rest.transpose(1, 0, 2, 3).reshape(model_width, -1)
    ff_grads = jnp.concatenate([grad_gate_up_w, grad_main, grad_rest], 1)
    ff_share = scatter_rows(ff_grads)
    down_term = jnp.dot(hidden, down_full, preferred_element_type=wide)

    grad_pair = core_sum(grad_normed_two.reshape(4, length, model_width))
    grad_other = to_z(grad_pair.astype(low))
    grad_other, ff_grads, down_term = lax.optimization_barrier((grad_other, ff_grads, down_term))
    grad_normed_two = grad_pair + grad_other.astype(wide)[::-1]
    grad_gain_two = jnp.sum(grad_normed_two[0] * middle[0] * scale_two[0], axis=0)
    outer = jnp.stack([team_outer[0], team_outer[2]]).astype(wide)
    grad_middle = outer + norm_back(grad_normed_two * gain_two, middle, scale_two)
    grad_branch = with_core(grad_middle.astype(low)).reshape(4 * length, model_width)

    result = middle[0] + own_sum(down_term.reshape(4, length, model_width))

    grad_out_w = contract_rows(gated, grad_branch)
    grad_gated = contract_cols(grad_branch, out_full).reshape(4, length, channels)
    grad_out_gate = grad_gated * convolved
    grad_conv = grad_gated * out_gate
    grad_kernel = jnp.stack([jnp.sum(grad_conv * rows_of, axis=(0, 1)) for rows_of in lagged], 1)

    heads = grad_conv[:, :2]
    sent = by_core(heads[0::2], heads[1::2])
    received = lax.ppermute(sent, "fsdp", TO_PREVIOUS)
    nothing = jnp.zeros_like(received[0])
    shifted = jnp.where(
        z == 0, jnp.stack([received[1], nothing]), jnp.stack([nothing, received[0]])
    )
    after = jnp.where(plane == PLANE - 1, shifted, received)
    own_after = by_core(heads[1::2], after)
    other_after = by_core(after, heads[0::2])
    later = jnp.stack([own_after[0], other_after[0], own_after[1], other_after[1]])
    grad_long = jnp.concatenate([grad_conv, later], 1)
    grad_mixed = (
        kernel[0] * grad_long[:, :length]
        + kernel[1] * grad_long[:, 1 : length + 1]
        + kernel[2] * grad_long[:, 2:]
    )
    grad_projected = jnp.concatenate(
        [
            (grad_mixed * carried).astype(low),
            grad_out_gate.astype(low),
            (grad_mixed * in_gate).astype(low),
        ],
        2,
    ).reshape(4 * length, 3 * channels)
    grad_in_w = contract_rows(normed, grad_projected)
    grad_normed = contract_cols(grad_projected, in_full).reshape(4, length, model_width)
    grad_gain_one = jnp.sum(grad_normed * inputs * scale_one, axis=(0, 1))

    in_grads = jnp.concatenate(
        [
            grad_in_w,
            jnp.pad(jnp.stack([grad_gain_one, grad_gain_two], 1), ((0, 0), (0, 126))),
        ],
        1,
    ).astype(low)
    out_grads = jnp.concatenate(
        [grad_out_w, jnp.pad(grad_kernel, ((0, 0), (0, 125)))], 1
    ).astype(low)
    in_share = lax.all_to_all(
        in_grads.reshape(2 * HALF, rows, -1), "fsdp", 0, 0, tiled=True
    ).reshape(2, PLANE, 2, rows, -1)
    in_share = jnp.sum(in_share.astype(wide), axis=1).astype(low).reshape(4, rows, -1)
    out_share = plane_swap(out_grads.reshape(PLANE, rows, -1))
    out_share = jnp.sum(out_share.astype(wide), axis=0).astype(low)

    grad_normed_own = own_sum(grad_normed)
    grad_inputs = grad_middle[0] + norm_back(
        grad_normed_own * gain_one, inputs[0], scale_one[0]
    )

    def all_reps(blocks):
        swapped = lax.all_to_all(
            jnp.concatenate([blocks, blocks]),
            ("rep", "fsdp"),
            0,
            0,
            tiled=True,
            axis_index_groups=BOTH_TEAMS,
        )
        return swapped[:4].astype(wide) + swapped[4:].astype(wide)

    def both_reps(value):
        other = lax.ppermute(value, "rep", [(0, 1), (1, 0)])
        return value.astype(wide) + other.astype(wide)

    in_total = both_reps(in_share)
    out_total = both_reps(out_share)
    ff_total = all_reps(ff_share[:, :, : 2 * units])
    down_total = both_reps(ff_share[:, :, 2 * units :])
    down_rest = down_total[:, :, model_width:].reshape(block // rest, rest, -1)
    down_rest = down_rest.transpose(1, 0, 2).reshape(rest, model_width)
    down_total = jnp.concatenate(
        [down_total[:, :, :model_width].reshape(block, model_width), down_rest], 0
    )
    gain_total = jnp.sum(in_total[:, :, 3 * channels : 3 * channels + 2], axis=0)

    return (
        result.astype(low),
        grad_inputs,
        gain_total[:, 0],
        from_members(in_total[:, :, : 3 * channels], 3),
        out_total[:, model_width : model_width + 3],
        out_total[:, :model_width],
        gain_total[:, 1],
        from_members(ff_total[:, :, :units], 1),
        from_members(ff_total[:, :, units:], 1),
        down_total,
    )


def solution(mesh):
    return jax.shard_map(
        body,
        mesh=mesh,
        in_specs=(
            P(("rep", "fsdp"), None),
            P("fsdp"),
            P("fsdp", None),
            P("fsdp", None),
            P("fsdp", None),
            P("fsdp"),
            P("fsdp", None),
            P("fsdp", None),
            P("fsdp", None),
            P(("rep", "fsdp"), None),
        ),
        out_specs=(
            P(("rep", "fsdp"), None),
            P(("rep", "fsdp"), None),
            P("fsdp"),
            P("fsdp", None),
            P("fsdp", None),
            P("fsdp", None),
            P("fsdp"),
            P("fsdp", None),
            P("fsdp", None),
            P("fsdp", None),
        ),
        check_vma=False,
    )
```

```python
import jax
import jax.numpy as jnp
from jax import lax
from jax.sharding import PartitionSpec as P

epsilon = 1e-05

SIDE = 4
PLANE = SIDE * SIDE
HALF = PLANE * 2
SPARE = 128


def place(z, plane, core):
    return (z * PLANE + plane) * 2 + core


def moves(target):
    return [
        (place(z, plane, core), place(*target(z, plane, core)))
        for z in range(2)
        for plane in range(PLANE)
        for core in range(2)
    ]


TO_CORE = moves(lambda z, plane, core: (z, plane, 1 - core))
TO_Z = moves(lambda z, plane, core: (1 - z, plane, core))
TO_NEXT = moves(lambda z, plane, core: (z, (plane + 1) % PLANE, core))
TO_PREVIOUS = moves(lambda z, plane, core: (z, (plane - 1) % PLANE, core))
TEAMS = [
    [place(z, plane, core) for z in range(2) for core in range(2)] for plane in range(PLANE)
]
PLANES = [
    [place(z, plane, core) for plane in range(PLANE)] for z in range(2) for core in range(2)
]
BOTH_TEAMS = [[rep * 2 * HALF + member for rep in range(2) for member in team] for team in TEAMS]


def to_core(value):
    return lax.ppermute(value, "fsdp", TO_CORE)


def to_z(value):
    return lax.ppermute(value, "fsdp", TO_Z)


def norm_scale(values):
    return lax.rsqrt(jnp.mean(values * values, axis=-1, keepdims=True) + epsilon)


def norm_back(grad_normed, values, scale):
    inner = jnp.mean(grad_normed * values, axis=-1, keepdims=True)
    return scale * (grad_normed - values * scale * scale * inner)


def contract_rows(left, right):
    return lax.dot_general(
        left, right, (((0,), (0,)), ((), ())), preferred_element_type=jnp.float32
    )


def contract_cols(left, right):
    return lax.dot_general(
        left, right, (((1,), (1,)), ((), ())), preferred_element_type=jnp.float32
    )


def by_member(shard, parts):
    rows, columns = shard.shape
    split = shard.reshape(rows, parts, 2, PLANE, 2, -1)
    return split.transpose(2, 4, 0, 1, 3, 5).reshape(4, rows, columns // 4)


def from_members(blocks, parts):
    members, rows, columns = blocks.shape
    split = blocks.reshape(2, 2, rows, parts, PLANE, -1)
    return split.transpose(2, 3, 0, 4, 1, 5).reshape(rows, 4 * columns)


def team_swap(blocks):
    return lax.all_to_all(blocks, "fsdp", 0, 0, tiled=True, axis_index_groups=TEAMS)


def plane_swap(blocks):
    return lax.all_to_all(blocks, "fsdp", 0, 0, tiled=True, axis_index_groups=PLANES)


def gather_rows(blocks):
    members, rows, columns = blocks.shape
    return lax.all_gather(
        blocks.reshape(2, 2 * rows, columns),
        "fsdp",
        axis=1,
        tiled=True,
        axis_index_groups=PLANES,
    ).reshape(-1, columns)


def scatter_rows(value):
    total, columns = value.shape
    return lax.psum_scatter(
        value.reshape(2, total // 2, columns),
        "fsdp",
        scatter_dimension=1,
        tiled=True,
        axis_index_groups=PLANES,
    ).reshape(4, -1, columns)


def team_tokens(own):
    return with_core(jnp.stack([own, to_z(own)]))


def with_core(pair):
    other = to_core(pair)
    return jnp.stack([pair[0], other[0], pair[1], other[1]])


def core_sum(partial):
    sent = jnp.stack([partial[1], partial[3]]).astype(jnp.bfloat16)
    return jnp.stack([partial[0], partial[2]]) + to_core(sent).astype(jnp.float32)


def own_sum(partial):
    pair = core_sum(partial)
    return pair[0] + to_z(pair[1].astype(jnp.bfloat16)).astype(jnp.float32)


def body(
    tokens, gain_first, w_in, conv_weight, w_out, gain_second, w_gate, w_up, w_down, cotangent
):
    low, wide = jnp.bfloat16, jnp.float32
    length, model_width = tokens.shape
    position = lax.axis_index("fsdp")
    core, plane, z = position % 2, position // 2 % PLANE, position // HALF
    rows = w_in.shape[0]
    channels = model_width // 4

    block = 4 * rows
    rest = w_down.shape[0] - block
    units = w_down.shape[0] * PLANE
    gains = jnp.pad(jnp.stack([gain_first, gain_second], 1), ((0, 0), (0, SPARE - 2)))
    gains = jnp.broadcast_to(gains, (4, rows, SPARE))
    swapped = team_swap(
        jnp.concatenate(
            [by_member(w_gate, 1), by_member(w_up, 1), by_member(w_in, 3), gains], 2
        )
    )
    down_main = w_down[:block].reshape(4, rows, model_width)
    down_rest = w_down[block:].reshape(rest, block // rest, -1).transpose(1, 0, 2)
    ff_all = gather_rows(
        jnp.concatenate(
            [swapped[:, :, : 2 * units], down_main, down_rest.reshape(4, rows, -1)], 2
        )
    )

    in_width = 3 * channels
    conv_lanes = jnp.pad(conv_weight, ((0, 0), (2, SPARE - 5)))
    first_pack = jnp.concatenate(
        [
            swapped[:, :, 2 * units : 2 * units + in_width],
            w_out.reshape(rows, 4, channels).transpose(1, 0, 2),
            swapped[:, :, 2 * units + in_width :] + conv_lanes,
        ],
        2,
    )
    first_all = plane_swap(jnp.broadcast_to(first_pack, (PLANE,) + first_pack.shape))
    in_full = first_all[..., :in_width].reshape(PLANE, 2, 2 * rows, in_width)
    in_full = in_full.transpose(1, 0, 2, 3).reshape(model_width, in_width)
    out_full = first_all[..., in_width : in_width + channels]
    out_full = out_full.transpose(0, 2, 1, 3).reshape(channels, model_width)
    spare = first_all[..., in_width + channels :]
    gain_both = spare[..., :2].reshape(PLANE, 2, 2 * rows, 2).transpose(3, 1, 0, 2)
    gain_one, gain_two = gain_both.astype(wide).reshape(2, model_width)
    kernel = spare[:, 0, :, 2:5].transpose(2, 0, 1).astype(wide).reshape(3, channels)

    gate_up_full = ff_all[:, : 2 * units]
    main_rows = ff_all[:, 2 * units : 2 * units + model_width].reshape(2, PLANE, 2 * rows, -1)
    main_rows = main_rows.transpose(1, 0, 2, 3).reshape(PLANE, block, model_width)
    rest_rows = ff_all[:, 2 * units + model_width :].reshape(2, PLANE, 2 * rows, -1)
    rest_rows = rest_rows.transpose(1, 0, 2, 3).reshape(PLANE, block // rest, rest, -1)
    rest_rows = rest_rows.transpose(0, 2, 1, 3).reshape(PLANE, rest, model_width)
    down_full = jnp.concatenate([main_rows, rest_rows], 1).reshape(units, model_width)

    team_values = team_tokens(jnp.stack([tokens, cotangent]))
    team_inputs, team_outer = team_values[:, 0], team_values[:, 1]
    outer_flat = team_outer.reshape(4 * length, model_width)

    inputs = team_inputs.astype(wide)
    scale_one = norm_scale(inputs)
    normed = (inputs * scale_one * gain_one).astype(low).reshape(4 * length, model_width)
    projected = jnp.dot(normed, in_full, preferred_element_type=wide)
    in_gate = projected[:, :channels].reshape(4, length, channels)
    out_gate = projected[:, channels : 2 * channels].reshape(4, length, channels)
    carried = projected[:, 2 * channels :].reshape(4, length, channels)
    mixed = (in_gate * carried).astype(low)

    def by_core(first, second):
        return jnp.where(core == 0, first, second)

    tails = mixed[:, length - 2 :]
    sent = by_core(tails[1::2], tails[0::2])
    received = lax.ppermute(sent, "fsdp", TO_NEXT)
    nothing = jnp.zeros_like(received[0])
    shifted = jnp.where(
        z == 0, jnp.stack([nothing, received[0]]), jnp.stack([received[1], nothing])
    )
    before = jnp.where(plane == 0, shifted, received)
    own_before = by_core(before, tails[1::2])
    other_before = by_core(tails[0::2], before)
    earlier = jnp.stack([own_before[0], other_before[0], own_before[1], other_before[1]])
    extended = jnp.concatenate([earlier, mixed], 1).astype(wide)
    lagged = (extended[:, 2:], extended[:, 1 : length + 1], extended[:, :length])
    convolved = kernel[0] * lagged[0] + kernel[1] * lagged[1] + kernel[2] * lagged[2]
    gated = (out_gate * convolved).astype(low).reshape(4 * length, channels)
    branch = jnp.dot(gated, out_full, preferred_element_type=wide)
    branch_pair = core_sum(branch.reshape(4, length, model_width))
    branch_other = to_z(branch_pair.astype(low))
    branch_other, down_full, gate_up_full = lax.optimization_barrier(
        (branch_other, down_full, gate_up_full)
    )
    middle = jnp.stack([inputs[0], inputs[2]]) + branch_pair + branch_other.astype(wide)[::-1]
    scale_two = norm_scale(middle)
    normed_two = with_core((middle * scale_two * gain_two).astype(low))
    normed_two = normed_two.reshape(4 * length, model_width)
    gate_up = jnp.dot(normed_two, gate_up_full, preferred_element_type=wide)
    gate_value, up_value = gate_up[:, :units], gate_up[:, units:]
    sigmoid_gate = jax.nn.sigmoid(gate_value)
    silu_gate = gate_value * sigmoid_gate
    hidden = (silu_gate * up_value).astype(low)

    grad_hidden = contract_cols(outer_flat, down_full)
    grad_gate = (
        grad_hidden * up_value * sigmoid_gate * (1.0 + gate_value * (1.0 - sigmoid_gate))
    ).astype(low)
    grad_upper = (grad_hidden * silu_gate).astype(low)
    grad_gate_up = jnp.concatenate([grad_gate, grad_upper], 1)
    grad_normed_two = contract_cols(grad_gate_up, gate_up_full)
    grad_pair = core_sum(grad_normed_two.reshape(4, length, model_width))
    grad_sent = grad_pair.astype(low)
    grad_other = to_z(grad_sent)

    grad_sent, hidden_now, grad_gate_up = lax.optimization_barrier(
        (grad_sent, hidden, grad_gate_up)
    )
    grad_down = contract_rows(hidden_now, outer_flat).astype(low)
    grad_gate_up_w = contract_rows(normed_two, grad_gate_up).astype(low)
    grad_down = grad_down.reshape(PLANE, block + rest, model_width)
    grad_main = grad_down[:, :block].reshape(PLANE, 2, 2 * rows, -1)
    grad_main = grad_main.transpose(1, 0, 2, 3).reshape(model_width, -1)
    grad_rest = grad_down[:, block:].reshape(PLANE, rest, block // rest, -1)
    grad_rest = grad_rest.transpose(0, 2, 1, 3).reshape(PLANE, 2, 2 * rows, -1)
    grad_rest = grad_rest.transpose(1, 0, 2, 3).reshape(model_width, -1)
    ff_grads = jnp.concatenate([grad_gate_up_w, grad_main, grad_rest], 1)
    ff_share = scatter_rows(ff_grads)
    down_term = jnp.dot(hidden_now, down_full, preferred_element_type=wide)
    grad_other, ff_grads, down_term = lax.optimization_barrier((grad_other, ff_grads, down_term))
    grad_normed_two = grad_pair + grad_other.astype(wide)[::-1]
    grad_gain_two = jnp.sum(grad_normed_two[0] * middle[0] * scale_two[0], axis=0)
    outer = jnp.stack([team_outer[0], team_outer[2]]).astype(wide)
    grad_middle = outer + norm_back(grad_normed_two * gain_two, middle, scale_two)
    grad_branch = with_core(grad_middle.astype(low)).reshape(4 * length, model_width)

    result = middle[0] + own_sum(down_term.reshape(4, length, model_width))

    grad_out_w = contract_rows(gated, grad_branch)
    grad_gated = contract_cols(grad_branch, out_full).reshape(4, length, channels)
    grad_out_gate = grad_gated * convolved
    grad_conv = grad_gated * out_gate
    grad_kernel = jnp.stack([jnp.sum(grad_conv * rows_of, axis=(0, 1)) for rows_of in lagged], 1)

    heads = grad_conv[:, :2]
    sent = by_core(heads[0::2], heads[1::2])
    received = lax.ppermute(sent, "fsdp", TO_PREVIOUS)
    nothing = jnp.zeros_like(received[0])
    shifted = jnp.where(
        z == 0, jnp.stack([received[1], nothing]), jnp.stack([nothing, received[0]])
    )
    after = jnp.where(plane == PLANE - 1, shifted, received)
    own_after = by_core(heads[1::2], after)
    other_after = by_core(after, heads[0::2])
    later = jnp.stack([own_after[0], other_after[0], own_after[1], other_after[1]])
    grad_long = jnp.concatenate([grad_conv, later], 1)
    grad_mixed = (
        kernel[0] * grad_long[:, :length]
        + kernel[1] * grad_long[:, 1 : length + 1]
        + kernel[2] * grad_long[:, 2:]
    )
    grad_projected = jnp.concatenate(
        [
            (grad_mixed * carried).astype(low),
            grad_out_gate.astype(low),
            (grad_mixed * in_gate).astype(low),
        ],
        2,
    ).reshape(4 * length, 3 * channels)
    grad_in_w = contract_rows(normed, grad_projected)
    grad_normed = contract_cols(grad_projected, in_full).reshape(4, length, model_width)
    grad_gain_one = jnp.sum(grad_normed * inputs * scale_one, axis=(0, 1))

    spare_grads = jnp.pad(
        jnp.stack([grad_gain_one, grad_gain_two], 1).reshape(2, PLANE, 2, rows, 2),
        ((0, 0),) * 4 + ((0, SPARE - 2),),
    ).transpose(1, 0, 2, 3, 4)
    spare_grads = spare_grads.reshape(PLANE, 4, rows, SPARE) + jnp.pad(
        grad_kernel.reshape(PLANE, 1, rows, 3), ((0, 0),) * 3 + ((2, SPARE - 5),)
    )
    first_grads = jnp.concatenate(
        [
            grad_in_w.reshape(2, PLANE, 2 * rows, in_width)
            .transpose(1, 0, 2, 3)
            .reshape(PLANE, 4, rows, in_width)
            .astype(low),
            grad_out_w.reshape(PLANE, rows, 4, channels).transpose(0, 2, 1, 3).astype(low),
            spare_grads.astype(low),
        ],
        3,
    )
    first_share = jnp.sum(plane_swap(first_grads).astype(wide), axis=0).astype(low)

    grad_normed_own = own_sum(grad_normed)
    grad_inputs = grad_middle[0] + norm_back(
        grad_normed_own * gain_one, inputs[0], scale_one[0]
    )

    def all_reps(blocks):
        swapped = lax.all_to_all(
            jnp.concatenate([blocks, blocks]),
            ("rep", "fsdp"),
            0,
            0,
            tiled=True,
            axis_index_groups=BOTH_TEAMS,
        )
        return swapped[:4].astype(wide) + swapped[4:].astype(wide)

    def both_reps(value):
        other = lax.ppermute(value, "rep", [(0, 1), (1, 0)])
        return value.astype(wide) + other.astype(wide)

    down_total = both_reps(ff_share[:, :, 2 * units :])
    down_rest = down_total[:, :, model_width:].reshape(block // rest, rest, -1)
    down_rest = down_rest.transpose(1, 0, 2).reshape(rest, model_width)
    down_total = jnp.concatenate(
        [down_total[:, :, :model_width].reshape(block, model_width), down_rest], 0
    )
    out_total = both_reps(first_share[:, :, in_width:])
    conv_total = out_total[0, :, channels + 2 : channels + 5]
    out_total = out_total[:, :, :channels].transpose(1, 0, 2).reshape(rows, model_width)
    totals = all_reps(
        jnp.concatenate(
            [
                ff_share[:, :, : 2 * units],
                first_share[:, :, :in_width],
                first_share[:, :, in_width + channels :],
            ],
            2,
        )
    )
    gain_total = jnp.sum(totals[:, :, 2 * units + in_width : 2 * units + in_width + 2], axis=0)

    return (
        result.astype(low),
        grad_inputs,
        gain_total[:, 0],
        from_members(totals[:, :, 2 * units : 2 * units + in_width], 3),
        conv_total,
        out_total,
        gain_total[:, 1],
        from_members(totals[:, :, :units], 1),
        from_members(totals[:, :, units : 2 * units], 1),
        down_total,
    )


def solution(mesh):
    return jax.shard_map(
        body,
        mesh=mesh,
        in_specs=(
            P(("rep", "fsdp"), None),
            P("fsdp"),
            P("fsdp", None),
            P("fsdp", None),
            P("fsdp", None),
            P("fsdp"),
            P("fsdp", None),
            P("fsdp", None),
            P("fsdp", None),
            P(("rep", "fsdp"), None),
        ),
        out_specs=(
            P(("rep", "fsdp"), None),
            P(("rep", "fsdp"), None),
            P("fsdp"),
            P("fsdp", None),
            P("fsdp", None),
            P("fsdp", None),
            P("fsdp"),
            P("fsdp", None),
            P("fsdp", None),
            P("fsdp", None),
        ),
        check_vma=False,
    )
```

```python
import jax
import jax.numpy as jnp
from jax import lax
from jax.experimental import pallas as pl
from jax.experimental.pallas import tpu as pltpu
from jax.sharding import PartitionSpec as P

epsilon = 1e-05

SIDE = 4
PLANE = SIDE * SIDE
HALF = PLANE * 2
SPARE = 128
VMEM_BYTES = 50 * 1024 * 1024


def place(z, plane, core):
    return (z * PLANE + plane) * 2 + core


def moves(target):
    return [
        (place(z, plane, core), place(*target(z, plane, core)))
        for z in range(2)
        for plane in range(PLANE)
        for core in range(2)
    ]


TO_CORE = moves(lambda z, plane, core: (z, plane, 1 - core))
TO_Z = moves(lambda z, plane, core: (1 - z, plane, core))
TO_NEXT = moves(lambda z, plane, core: (z, (plane + 1) % PLANE, core))
TO_PREVIOUS = moves(lambda z, plane, core: (z, (plane - 1) % PLANE, core))
TEAMS = [
    [place(z, plane, core) for z in range(2) for core in range(2)] for plane in range(PLANE)
]
PLANES = [
    [place(z, plane, core) for plane in range(PLANE)] for z in range(2) for core in range(2)
]
BOTH_TEAMS = [[rep * 2 * HALF + member for rep in range(2) for member in team] for team in TEAMS]


def to_core(value):
    return lax.ppermute(value, "fsdp", TO_CORE)


def to_z(value):
    return lax.ppermute(value, "fsdp", TO_Z)


def norm_scale(values):
    return lax.rsqrt(jnp.mean(values * values, axis=-1, keepdims=True) + epsilon)


def norm_back(grad_normed, values, scale):
    inner = jnp.mean(grad_normed * values, axis=-1, keepdims=True)
    return scale * (grad_normed - values * scale * scale * inner)


def contract_rows(left, right):
    return lax.dot_general(
        left, right, (((0,), (0,)), ((), ())), preferred_element_type=jnp.float32
    )


def contract_cols(left, right):
    return lax.dot_general(
        left, right, (((1,), (1,)), ((), ())), preferred_element_type=jnp.float32
    )


def by_member(shard, parts):
    rows, columns = shard.shape
    split = shard.reshape(rows, parts, 2, PLANE, 2, -1)
    return split.transpose(2, 4, 0, 1, 3, 5).reshape(4, rows, columns // 4)


def from_members(blocks, parts):
    members, rows, columns = blocks.shape
    split = blocks.reshape(2, 2, rows, parts, PLANE, -1)
    return split.transpose(2, 3, 0, 4, 1, 5).reshape(rows, 4 * columns)


def team_swap(blocks):
    return lax.all_to_all(blocks, "fsdp", 0, 0, tiled=True, axis_index_groups=TEAMS)


def plane_swap(blocks):
    return lax.all_to_all(blocks, "fsdp", 0, 0, tiled=True, axis_index_groups=PLANES)


def gather_rows(blocks):
    members, rows, columns = blocks.shape
    return lax.all_gather(
        blocks.reshape(2, 2 * rows, columns),
        "fsdp",
        axis=1,
        tiled=True,
        axis_index_groups=PLANES,
    ).reshape(-1, columns)


def scatter_rows(value):
    total, columns = value.shape
    return lax.psum_scatter(
        value.reshape(2, total // 2, columns),
        "fsdp",
        scatter_dimension=1,
        tiled=True,
        axis_index_groups=PLANES,
    ).reshape(4, -1, columns)


def slots_of(pair, other):
    return jnp.stack([pair[0], other[0], pair[1], other[1]])


def core_sum(keep, sent):
    return keep + to_core(sent).astype(jnp.float32)


def own_sum(keep, sent):
    pair = core_sum(keep, sent)
    return pair[0] + to_z(pair[1].astype(jnp.bfloat16)).astype(jnp.float32)


def whole(*shape):
    return pl.BlockSpec(shape, lambda *_: (0,) * len(shape))


def per_slot(length, width, column=0):
    return pl.BlockSpec((1, length, width), lambda slot: (slot, 0, column))


def per_pair(length, width):
    return pl.BlockSpec((1, length, width), lambda slot: (slot // 2, 0, 0))


def pair_of_values(length, width, which):
    return pl.BlockSpec((1, 1, length, width), lambda slot: (slot // 2, which, 0, 0))


def run(kernel, grid, in_specs, out_specs, out_shape, scratch, flops, values):
    moved = sum(value.size * value.dtype.itemsize for value in values)
    moved += sum(value.size * value.dtype.itemsize for value in out_shape)
    return pl.pallas_call(
        kernel,
        grid=grid,
        in_specs=in_specs,
        out_specs=out_specs,
        out_shape=out_shape,
        scratch_shapes=scratch,
        compiler_params=pltpu.CompilerParams(vmem_limit_bytes=VMEM_BYTES),
        cost_estimate=pl.CostEstimate(flops=flops, bytes_accessed=moved, transcendentals=0),
    )(*values)


def array(shape, kind):
    return jax.ShapeDtypeStruct(shape, kind)


def pick(slot, even, odd):
    return jnp.where(slot % 2 == 0, even, odd)


def shifted_in(values, first_rows, steps):
    moved = pltpu.roll(values, steps, 0)
    row = lax.broadcasted_iota(jnp.int32, values.shape, 0)
    for index in range(steps):
        moved = jnp.where(row == index, first_rows[2 - steps + index :][:1], moved)
    return moved


def shifted_out(values, next_rows, steps):
    length = values.shape[0]
    moved = pltpu.roll(values, length - steps, 0)
    row = lax.broadcasted_iota(jnp.int32, values.shape, 0)
    for index in range(steps):
        moved = jnp.where(row == length - steps + index, next_rows[index : index + 1], moved)
    return moved


def store_pair(slot, value, keep_ref, sent_ref):
    @pl.when(slot % 2 == 0)
    def _():
        keep_ref[0] = value

    @pl.when(slot % 2 == 1)
    def _():
        sent_ref[0] = value.astype(sent_ref.dtype)


def project_kernel(
    pair_ref, other_ref, first_ref,
    normed_ref, proj_ref, mixed_ref, in_ref, out_ref, gains_ref, taps_ref,
    column, taps_column,
):
    slot = pl.program_id(0)
    width = in_ref.shape[1]
    channels = width // 3
    rows = channels // PLANE

    @pl.when(slot == 0)
    def _():
        for plane in range(PLANE):
            for z in range(2):
                at = pl.ds((z * PLANE + plane) * 2 * rows, 2 * rows)
                source = pl.ds(z * 2 * rows, 2 * rows)
                in_ref[at, :] = first_ref[plane, source, :width]
                column[at, :] = first_ref[plane, source, width + channels :].astype(jnp.float32)
            at = pl.ds(plane * rows, rows)
            for part in range(4):
                out_ref[at, part * channels : (part + 1) * channels] = first_ref[
                    plane, pl.ds(part * rows, rows), width : width + channels
                ]
            taps_column[at, :] = first_ref[plane, :rows, width + channels :].astype(jnp.float32)
        gains_ref[...] = column[...].T[:8]
        taps_ref[...] = taps_column[...].T[:8]

    values = pick(slot, pair_ref[0, 0], other_ref[0, 0]).astype(jnp.float32)
    normed = (values * norm_scale(values) * gains_ref[0:1]).astype(jnp.bfloat16)
    normed_ref[0] = normed
    projected = jnp.dot(normed, in_ref[...], preferred_element_type=jnp.float32)
    proj_ref[0] = projected
    mixed = projected[:, :channels] * projected[:, 2 * channels :]
    mixed_ref[0] = mixed.astype(jnp.bfloat16)


def branch_kernel(
    mixed_ref, earlier_ref, out_gate_ref, taps_ref, out_ref,
    convolved_ref, gated_ref, keep_ref, sent_ref,
):
    slot = pl.program_id(0)
    mixed = mixed_ref[0].astype(jnp.float32)
    earlier = earlier_ref[0]
    convolved = (
        taps_ref[2:3] * mixed
        + taps_ref[3:4] * shifted_in(mixed, earlier, 1)
        + taps_ref[4:5] * shifted_in(mixed, earlier, 2)
    )
    convolved_ref[0] = convolved
    gated = (out_gate_ref[0] * convolved).astype(jnp.bfloat16)
    gated_ref[0] = gated
    branch = jnp.dot(gated, out_ref[...], preferred_element_type=jnp.float32)
    store_pair(slot, branch, keep_ref, sent_ref)


def ff_kernel(
    own_ref, swap_ref, pair_ref, other_ref, gate_ref, up_ref, down_ref,
    hidden_ref, grad_gate_ref, grad_up_ref, keep_ref, sent_ref,
    total,
):
    step, slot = pl.program_id(0), pl.program_id(1)
    normed = pick(slot, own_ref[0], swap_ref[0])
    outer = pick(slot, pair_ref[0, 0], other_ref[0, 0])
    gate = jnp.dot(normed, gate_ref[...], preferred_element_type=jnp.float32)
    up = jnp.dot(normed, up_ref[...], preferred_element_type=jnp.float32)
    grad = contract_cols(outer, down_ref[...])
    sigmoid = jax.nn.sigmoid(gate)
    silu = gate * sigmoid
    hidden_ref[0] = (silu * up).astype(jnp.bfloat16)
    grad_gate = (grad * up * sigmoid * (1.0 + gate * (1.0 - sigmoid))).astype(jnp.bfloat16)
    grad_up = (grad * silu).astype(jnp.bfloat16)
    grad_gate_ref[0] = grad_gate
    grad_up_ref[0] = grad_up
    term = contract_cols(grad_gate, gate_ref[...]) + contract_cols(grad_up, up_ref[...])

    @pl.when(step == 0)
    def _():
        total[slot] = term

    @pl.when(step > 0)
    def _():
        total[slot] += term

    @pl.when(step == pl.num_programs(0) - 1)
    def _():
        store_pair(slot, total[slot], keep_ref, sent_ref)


def gated_back_kernel(
    own_ref, swap_ref, out_ref, convolved_ref, out_gate_ref, grad_out_ref, grad_conv_ref
):
    slot = pl.program_id(0)
    grad_gated = contract_cols(pick(slot, own_ref[0], swap_ref[0]), out_ref[...])
    grad_out_ref[0] = (grad_gated * convolved_ref[0]).astype(jnp.bfloat16)
    grad_conv_ref[0] = grad_gated * out_gate_ref[0]


def out_grads_kernel(
    own_ref, swap_ref, gated_ref, grad_conv_ref, mixed_ref, earlier_ref, gain_ref,
    part_ref, spare_ref,
    total, taps_rows, gain_rows,
):
    slot = pl.program_id(0)
    rows = spare_ref.shape[1] // 4
    channels = gated_ref.shape[2]

    @pl.when(slot == 0)
    def _():
        total[...] = jnp.zeros_like(total)
        taps_rows[...] = jnp.zeros_like(taps_rows)
        gain_rows[...] = jnp.zeros_like(gain_rows)
        gain_rows[1:2] = gain_ref[...]

    total[...] += contract_rows(gated_ref[0], pick(slot, own_ref[0], swap_ref[0]))
    grad_conv = grad_conv_ref[0]
    mixed = mixed_ref[0].astype(jnp.float32)
    earlier = earlier_ref[0]
    lagged = (mixed, shifted_in(mixed, earlier, 1), shifted_in(mixed, earlier, 2))
    for lag, value in enumerate(lagged):
        taps_rows[2 + lag : 3 + lag] += jnp.sum(grad_conv * value, axis=0, keepdims=True)

    @pl.when(slot == 3)
    def _():
        gain_column = gain_rows[...].T
        taps_column = taps_rows[...].T
        for plane in range(PLANE):
            at = slice(plane * rows, (plane + 1) * rows)
            for part in range(4):
                part_ref[plane, part * rows : (part + 1) * rows, :] = total[
                    at, part * channels : (part + 1) * channels
                ].astype(jnp.bfloat16)
            for z in range(2):
                start = (z * PLANE + plane) * 2 * rows
                spare_ref[plane, z * 2 * rows : (z + 1) * 2 * rows, :] = gain_column[
                    start : start + 2 * rows
                ]
            spare_ref[plane, :rows, :] += taps_column[at]


def project_back_kernel(
    grad_conv_ref, later_ref, proj_ref, grad_out_ref, normed_ref, in_ref, taps_ref,
    pair_ref, other_ref, part_ref, spare_ref,
    pack_ref, keep_ref, sent_ref,
    total, gain_rows,
):
    slot = pl.program_id(0)
    width = in_ref.shape[1]
    channels = width // 3
    rows = channels // PLANE

    @pl.when(slot == 0)
    def _():
        total[...] = jnp.zeros_like(total)
        gain_rows[...] = jnp.zeros_like(gain_rows)

    grad_conv, later = grad_conv_ref[0], later_ref[0]
    grad_mixed = (
        taps_ref[2:3] * grad_conv
        + taps_ref[3:4] * shifted_out(grad_conv, later, 1)
        + taps_ref[4:5] * shifted_out(grad_conv, later, 2)
    )
    grad_projected = jnp.concatenate(
        [
            (grad_mixed * proj_ref[0, :, 2 * channels :]).astype(jnp.bfloat16),
            grad_out_ref[0],
            (grad_mixed * proj_ref[0, :, :channels]).astype(jnp.bfloat16),
        ],
        1,
    )
    total[...] += contract_rows(normed_ref[0], grad_projected)
    grad_normed = contract_cols(grad_projected, in_ref[...])
    store_pair(slot, grad_normed, keep_ref, sent_ref)
    values = pick(slot, pair_ref[0, 0], other_ref[0, 0]).astype(jnp.float32)
    gain_rows[0:1] += jnp.sum(grad_normed * values * norm_scale(values), axis=0, keepdims=True)

    @pl.when(slot == 3)
    def _():
        gain_column = gain_rows[...].T
        for plane in range(PLANE):
            for z in range(2):
                start = (z * PLANE + plane) * 2 * rows
                to = slice(z * 2 * rows, (z + 1) * 2 * rows)
                pack_ref[plane, to, :width] = total[start : start + 2 * rows].astype(jnp.bfloat16)
                pack_ref[plane, to, width + channels :] = (
                    spare_ref[plane, to] + gain_column[start : start + 2 * rows]
                ).astype(jnp.bfloat16)
            pack_ref[plane, :, width : width + channels] = part_ref[plane]


def body(
    tokens, gain_first, w_in, conv_weight, w_out, gain_second, w_gate, w_up, w_down, cotangent
):
    low, wide = jnp.bfloat16, jnp.float32
    length, model_width = tokens.shape
    position = lax.axis_index("fsdp")
    core, plane, z = position % 2, position // 2 % PLANE, position // HALF
    rows = w_in.shape[0]
    channels = model_width // 4

    block = 4 * rows
    rest = w_down.shape[0] - block
    units = w_down.shape[0] * PLANE
    gains = jnp.pad(jnp.stack([gain_first, gain_second], 1), ((0, 0), (0, SPARE - 2)))
    gains = jnp.broadcast_to(gains, (4, rows, SPARE))
    swapped = team_swap(
        jnp.concatenate(
            [by_member(w_gate, 1), by_member(w_up, 1), by_member(w_in, 3), gains], 2
        )
    )
    down_main = w_down[:block].reshape(4, rows, model_width)
    down_rest = w_down[block:].reshape(rest, block // rest, -1).transpose(1, 0, 2)
    ff_all = gather_rows(
        jnp.concatenate(
            [swapped[:, :, : 2 * units], down_main, down_rest.reshape(4, rows, -1)], 2
        )
    )

    in_width = 3 * channels
    conv_lanes = jnp.pad(conv_weight, ((0, 0), (2, SPARE - 5)))
    first_pack = jnp.concatenate(
        [
            swapped[:, :, 2 * units : 2 * units + in_width],
            w_out.reshape(rows, 4, channels).transpose(1, 0, 2),
            swapped[:, :, 2 * units + in_width :] + conv_lanes,
        ],
        2,
    )
    first_all = plane_swap(jnp.broadcast_to(first_pack, (PLANE,) + first_pack.shape))
    first_all = first_all.reshape(PLANE, 4 * rows, -1)

    main_rows = ff_all[:, 2 * units : 2 * units + model_width].reshape(2, PLANE, 2 * rows, -1)
    main_rows = main_rows.transpose(1, 0, 2, 3).reshape(PLANE, block, model_width)
    rest_rows = ff_all[:, 2 * units + model_width :].reshape(2, PLANE, 2 * rows, -1)
    rest_rows = rest_rows.transpose(1, 0, 2, 3).reshape(PLANE, block // rest, rest, -1)
    rest_rows = rest_rows.transpose(0, 2, 1, 3).reshape(PLANE, rest, model_width)
    down_full = jnp.concatenate([main_rows, rest_rows], 1).reshape(units, model_width)

    pair = jnp.stack([tokens, cotangent])
    pair = jnp.stack([pair, to_z(pair)])
    other = to_core(pair)
    team_pairs = [pair_of_values(length, model_width, 0)] * 2
    slot_wide, slot_narrow = (4, length, model_width), (4, length, channels)
    pair_wide = (2, length, model_width)
    pairs = [per_pair(length, model_width)] * 2
    narrow = per_slot(length, channels)
    out_gate = per_slot(length, channels, 1)
    edge = per_slot(8, channels)
    out_matrix, in_matrix = whole(channels, model_width), whole(model_width, in_width)
    taps = whole(8, channels)
    unit = 2 * 4 * length * model_width * channels

    normed, projected, mixed, in_full, out_full, gains, kernel = run(
        project_kernel,
        (4,),
        team_pairs + [whole(*first_all.shape)],
        [
            per_slot(length, model_width),
            per_slot(length, in_width),
            narrow,
            in_matrix,
            out_matrix,
            whole(8, model_width),
            taps,
        ],
        [
            array(slot_wide, low),
            array((4, length, in_width), wide),
            array(slot_narrow, low),
            array((model_width, in_width), low),
            array((channels, model_width), low),
            array((8, model_width), wide),
            array((8, channels), wide),
        ],
        [pltpu.VMEM((model_width, SPARE), wide), pltpu.VMEM((channels, SPARE), wide)],
        3 * unit,
        [pair, other, first_all],
    )
    gain_one, gain_two = gains[0], gains[1]

    def by_core(first, second):
        return jnp.where(core == 0, first, second)

    tails = mixed[:, length - 2 :]
    sent = by_core(tails[1::2], tails[0::2])
    received = lax.ppermute(sent, "fsdp", TO_NEXT)
    nothing = jnp.zeros_like(received[0])
    shifted = jnp.where(
        z == 0, jnp.stack([nothing, received[0]]), jnp.stack([received[1], nothing])
    )
    before = jnp.where(plane == 0, shifted, received)
    own_before = by_core(before, tails[1::2])
    other_before = by_core(tails[0::2], before)
    earlier = jnp.stack([own_before[0], other_before[0], own_before[1], other_before[1]])
    earlier = jnp.pad(earlier.astype(wide), ((0, 0), (0, 6), (0, 0)))
    convolved, gated, branch_keep, branch_sent = run(
        branch_kernel,
        (4,),
        [narrow, edge, out_gate, taps, out_matrix],
        [narrow, narrow] + pairs,
        [
            array(slot_narrow, wide),
            array(slot_narrow, low),
            array(pair_wide, wide),
            array(pair_wide, low),
        ],
        [],
        unit,
        [mixed, earlier, projected, kernel, out_full],
    )
    branch_pair = core_sum(branch_keep, branch_sent)
    branch_other = to_z(branch_pair.astype(low))
    branch_other, down_full = lax.optimization_barrier((branch_other, down_full))
    inputs = pair[:, 0].astype(wide)
    middle = inputs + branch_pair + branch_other.astype(wide)[::-1]
    scale_two = norm_scale(middle)
    normed_two = (middle * scale_two * gain_two).astype(low)
    normed_swap = to_core(normed_two)

    steps = 3
    tile = units // steps
    pair_now = pl.BlockSpec((1, length, model_width), lambda step, slot: (slot // 2, 0, 0))
    outer_now = pl.BlockSpec(
        (1, 1, length, model_width), lambda step, slot: (slot // 2, 1, 0, 0)
    )
    pair_last = pl.BlockSpec(
        (1, length, model_width),
        lambda step, slot: (jnp.where(step == steps - 1, slot // 2, 0), 0, 0),
    )
    tile_now = pl.BlockSpec((1, length, tile), lambda step, slot: (slot, 0, step))
    hidden, grad_gate, grad_upper, grad_keep, grad_sent = run(
        ff_kernel,
        (steps, 4),
        [
            pair_now,
            pair_now,
            outer_now,
            outer_now,
            pl.BlockSpec((model_width, tile), lambda step, slot: (0, step)),
            pl.BlockSpec((model_width, tile), lambda step, slot: (0, steps + step)),
            pl.BlockSpec((tile, model_width), lambda step, slot: (step, 0)),
        ],
        [tile_now] * 3 + [pair_last] * 2,
        [array((4, length, units), low)] * 3 + [array(pair_wide, wide), array(pair_wide, low)],
        [pltpu.VMEM(slot_wide, wide)],
        5 * 2 * 4 * length * model_width * units,
        [normed_two, normed_swap, pair, other, ff_all, ff_all, down_full],
    )
    hidden, grad_gate, grad_upper = (
        value.reshape(4 * length, units) for value in (hidden, grad_gate, grad_upper)
    )
    grad_pair = core_sum(grad_keep, grad_sent)
    grad_sent = grad_pair.astype(low)
    grad_other = to_z(grad_sent)

    grad_sent, hidden, grad_gate, grad_upper = lax.optimization_barrier(
        (grad_sent, hidden, grad_gate, grad_upper)
    )
    outer_flat = slots_of(pair[:, 1], other[:, 1]).reshape(4 * length, model_width)
    normed_flat = slots_of(normed_two, normed_swap).reshape(4 * length, model_width)
    grad_down = contract_rows(hidden, outer_flat).astype(low)
    grad_gate_w = contract_rows(normed_flat, grad_gate).astype(low)
    grad_up_w = contract_rows(normed_flat, grad_upper).astype(low)
    grad_down = grad_down.reshape(PLANE, block + rest, model_width)
    grad_main = grad_down[:, :block].reshape(PLANE, 2, 2 * rows, -1)
    grad_main = grad_main.transpose(1, 0, 2, 3).reshape(model_width, -1)
    grad_rest = grad_down[:, block:].reshape(PLANE, rest, block // rest, -1)
    grad_rest = grad_rest.transpose(0, 2, 1, 3).reshape(PLANE, 2, 2 * rows, -1)
    grad_rest = grad_rest.transpose(1, 0, 2, 3).reshape(model_width, -1)
    ff_grads = jnp.concatenate([grad_gate_w, grad_up_w, grad_main, grad_rest], 1)
    ff_share = scatter_rows(ff_grads)
    down_term = jnp.dot(hidden, down_full, preferred_element_type=wide)
    grad_other, ff_grads, down_term = lax.optimization_barrier((grad_other, ff_grads, down_term))
    grad_normed_two = grad_pair + grad_other.astype(wide)[::-1]
    grad_gain_two = jnp.sum(grad_normed_two[0] * middle[0] * scale_two[0], axis=0)
    outer = pair[:, 1].astype(wide)
    grad_middle = outer + norm_back(grad_normed_two * gain_two, middle, scale_two)
    grad_branch = grad_middle.astype(low)
    grad_swap = to_core(grad_branch)

    down_term = down_term.reshape(4, length, model_width)
    result = middle[0] + own_sum(down_term[0::2], down_term[1::2].astype(low))

    grad_out, grad_conv = run(
        gated_back_kernel,
        (4,),
        pairs + [out_matrix, narrow, out_gate],
        [narrow, narrow],
        [array(slot_narrow, low), array(slot_narrow, wide)],
        [],
        unit,
        [grad_branch, grad_swap, out_full, convolved, projected],
    )
    heads = grad_conv[:, :2]
    sent = by_core(heads[0::2], heads[1::2])
    received = lax.ppermute(sent, "fsdp", TO_PREVIOUS)
    nothing = jnp.zeros_like(received[0])
    shifted = jnp.where(
        z == 0, jnp.stack([received[1], nothing]), jnp.stack([nothing, received[0]])
    )
    after = jnp.where(plane == PLANE - 1, shifted, received)
    own_after = by_core(heads[1::2], after)
    other_after = by_core(after, heads[0::2])
    later = jnp.stack([own_after[0], other_after[0], own_after[1], other_after[1]])
    later = jnp.pad(later, ((0, 0), (0, 6), (0, 0)))
    part_shape, spare_shape = (PLANE, 4 * rows, channels), (PLANE, 4 * rows, SPARE)
    out_part, spare_part = run(
        out_grads_kernel,
        (4,),
        pairs + [narrow, narrow, narrow, edge, whole(1, model_width)],
        [whole(*part_shape), whole(*spare_shape)],
        [array(part_shape, low), array(spare_shape, wide)],
        [
            pltpu.VMEM((channels, model_width), wide),
            pltpu.VMEM((SPARE, channels), wide),
            pltpu.VMEM((SPARE, model_width), wide),
        ],
        unit,
        [grad_branch, grad_swap, gated, grad_conv, mixed, earlier, grad_gain_two[None]],
    )
    first_grads, normed_keep, normed_sent = run(
        project_back_kernel,
        (4,),
        [
            narrow,
            edge,
            per_slot(length, in_width),
            narrow,
            per_slot(length, model_width),
            in_matrix,
            taps,
        ]
        + team_pairs
        + [whole(*part_shape), whole(*spare_shape)],
        [whole(*first_all.shape)] + pairs,
        [array(first_all.shape, low), array(pair_wide, wide), array(pair_wide, low)],
        [pltpu.VMEM((model_width, in_width), wide), pltpu.VMEM((SPARE, model_width), wide)],
        6 * unit,
        [
            grad_conv,
            later,
            projected,
            grad_out,
            normed,
            in_full,
            kernel,
            pair,
            other,
            out_part,
            spare_part,
        ],
    )
    first_grads = first_grads.reshape(PLANE, 4, rows, -1)
    first_share = jnp.sum(plane_swap(first_grads).astype(wide), axis=0).astype(low)

    grad_normed_own = own_sum(normed_keep, normed_sent)
    grad_inputs = grad_middle[0] + norm_back(
        grad_normed_own * gain_one, inputs[0], norm_scale(inputs[0])
    )

    def all_reps(blocks):
        swapped = lax.all_to_all(
            jnp.concatenate([blocks, blocks]),
            ("rep", "fsdp"),
            0,
            0,
            tiled=True,
            axis_index_groups=BOTH_TEAMS,
        )
        return swapped[:4].astype(wide) + swapped[4:].astype(wide)

    def both_reps(value):
        other = lax.ppermute(value, "rep", [(0, 1), (1, 0)])
        return value.astype(wide) + other.astype(wide)

    down_total = both_reps(ff_share[:, :, 2 * units :])
    down_rest = down_total[:, :, model_width:].reshape(block // rest, rest, -1)
    down_rest = down_rest.transpose(1, 0, 2).reshape(rest, model_width)
    down_total = jnp.concatenate(
        [down_total[:, :, :model_width].reshape(block, model_width), down_rest], 0
    )
    out_total = both_reps(first_share[:, :, in_width:])
    conv_total = out_total[0, :, channels + 2 : channels + 5]
    out_total = out_total[:, :, :channels].transpose(1, 0, 2).reshape(rows, model_width)
    totals = all_reps(
        jnp.concatenate(
            [
                ff_share[:, :, : 2 * units],
                first_share[:, :, :in_width],
                first_share[:, :, in_width + channels :],
            ],
            2,
        )
    )
    gain_total = jnp.sum(totals[:, :, 2 * units + in_width : 2 * units + in_width + 2], axis=0)

    return (
        result.astype(low),
        grad_inputs,
        gain_total[:, 0],
        from_members(totals[:, :, 2 * units : 2 * units + in_width], 3),
        conv_total,
        out_total,
        gain_total[:, 1],
        from_members(totals[:, :, :units], 1),
        from_members(totals[:, :, units : 2 * units], 1),
        down_total,
    )


def solution(mesh):
    return jax.shard_map(
        body,
        mesh=mesh,
        in_specs=(
            P(("rep", "fsdp"), None),
            P("fsdp"),
            P("fsdp", None),
            P("fsdp", None),
            P("fsdp", None),
            P("fsdp"),
            P("fsdp", None),
            P("fsdp", None),
            P("fsdp", None),
            P(("rep", "fsdp"), None),
        ),
        out_specs=(
            P(("rep", "fsdp"), None),
            P(("rep", "fsdp"), None),
            P("fsdp"),
            P("fsdp", None),
            P("fsdp", None),
            P("fsdp", None),
            P("fsdp"),
            P("fsdp", None),
            P("fsdp", None),
            P("fsdp", None),
        ),
        check_vma=False,
    )
```

```python
import jax
import jax.numpy as jnp
from jax import lax
from jax.experimental import pallas as pl
from jax.experimental.pallas import tpu as pltpu
from jax.sharding import PartitionSpec as P

epsilon = 1e-05

SIDE = 4
PLANE = SIDE * SIDE
HALF = PLANE * 2
SPARE = 128
CHUNK = 256
VMEM_BYTES = 56 * 1024 * 1024


def place(z, plane, core):
    return (z * PLANE + plane) * 2 + core


def moves(target):
    return [
        (place(z, plane, core), place(*target(z, plane, core)))
        for z in range(2)
        for plane in range(PLANE)
        for core in range(2)
    ]


TO_CORE = moves(lambda z, plane, core: (z, plane, 1 - core))
TO_Z = moves(lambda z, plane, core: (1 - z, plane, core))
TO_NEXT = moves(lambda z, plane, core: (z, (plane + 1) % PLANE, core))
TO_PREVIOUS = moves(lambda z, plane, core: (z, (plane - 1) % PLANE, core))


def along_x(steps):
    return moves(
        lambda z, plane, core: (z, (plane // SIDE + steps) % SIDE * SIDE + plane % SIDE, core)
    )


def along_y(steps):
    return moves(
        lambda z, plane, core: (z, plane // SIDE * SIDE + (plane + steps) % SIDE, core)
    )


ALONG_X = [along_x(steps) for steps in range(1, SIDE)]
ALONG_Y = [along_y(steps) for steps in range(1, SIDE)]
TEAMS = [
    [place(z, plane, core) for z in range(2) for core in range(2)] for plane in range(PLANE)
]
PLANES = [
    [place(z, plane, core) for plane in range(PLANE)] for z in range(2) for core in range(2)
]
BOTH_TEAMS = [[rep * 2 * HALF + member for rep in range(2) for member in team] for team in TEAMS]


def to_core(value):
    return lax.ppermute(value, "fsdp", TO_CORE)


def to_z(value):
    return lax.ppermute(value, "fsdp", TO_Z)


def norm_scale(values):
    return lax.rsqrt(jnp.mean(values * values, axis=-1, keepdims=True) + epsilon)


def norm_back(grad_normed, values, scale):
    inner = jnp.mean(grad_normed * values, axis=-1, keepdims=True)
    return scale * (grad_normed - values * scale * scale * inner)


def contract_rows(left, right):
    return lax.dot_general(
        left, right, (((0,), (0,)), ((), ())), preferred_element_type=jnp.float32
    )


def contract_cols(left, right):
    return lax.dot_general(
        left, right, (((1,), (1,)), ((), ())), preferred_element_type=jnp.float32
    )


def by_member(shard, parts):
    rows, columns = shard.shape
    split = shard.reshape(rows, parts, 2, PLANE, 2, -1)
    return split.transpose(2, 4, 0, 1, 3, 5).reshape(4, rows, columns // 4)


def from_members(blocks, parts):
    members, rows, columns = blocks.shape
    split = blocks.reshape(2, 2, rows, parts, PLANE, -1)
    return split.transpose(2, 3, 0, 4, 1, 5).reshape(rows, 4 * columns)


def team_swap(blocks):
    return lax.all_to_all(blocks, "fsdp", 0, 0, tiled=True, axis_index_groups=TEAMS)


def fetch(value, along):
    return [value] + [
        lax.ppermute(value, "fsdp", along[SIDE - steps - 1]) for steps in range(1, SIDE)
    ]


def deliver(values, along):
    total = values[0].astype(jnp.float32)
    for steps in range(1, SIDE):
        moved = lax.ppermute(values[steps], "fsdp", along[steps - 1])
        total = total + moved.astype(jnp.float32)
    return total


def gather_rows(blocks):
    members, rows, columns = blocks.shape
    return lax.all_gather(
        blocks.reshape(2, 2 * rows, columns),
        "fsdp",
        axis=1,
        tiled=True,
        axis_index_groups=PLANES,
    ).reshape(-1, columns)


def scatter_rows(value):
    total, columns = value.shape
    return lax.psum_scatter(
        value.reshape(2, total // 2, columns),
        "fsdp",
        scatter_dimension=1,
        tiled=True,
        axis_index_groups=PLANES,
    ).reshape(4, -1, columns)


def slots_of(pair, other):
    return jnp.stack([pair[0], other[0], pair[1], other[1]])


def core_sum(keep, sent):
    return keep + to_core(sent).astype(jnp.float32)


def own_sum(keep, sent):
    pair = core_sum(keep, sent)
    return pair[0] + to_z(pair[1].astype(jnp.bfloat16)).astype(jnp.float32)


def whole(*shape):
    return pl.BlockSpec(shape, lambda *_: (0,) * len(shape))


def per_slot(length, width, column=0):
    return pl.BlockSpec((1, length, width), lambda slot: (slot, 0, column))


def per_pair(length, width):
    return pl.BlockSpec((1, length, width), lambda slot: (slot // 2, 0, 0))


def pair_of_values(length, width, which):
    return pl.BlockSpec((1, 1, length, width), lambda slot: (slot // 2, which, 0, 0))


def run(kernel, grid, in_specs, out_specs, out_shape, scratch, flops, values):
    moved = sum(value.size * value.dtype.itemsize for value in values)
    moved += sum(value.size * value.dtype.itemsize for value in out_shape)
    return pl.pallas_call(
        kernel,
        grid=grid,
        in_specs=in_specs,
        out_specs=out_specs,
        out_shape=out_shape,
        scratch_shapes=scratch,
        compiler_params=pltpu.CompilerParams(vmem_limit_bytes=VMEM_BYTES),
        cost_estimate=pl.CostEstimate(flops=flops, bytes_accessed=moved, transcendentals=0),
    )(*values)


def array(shape, kind):
    return jax.ShapeDtypeStruct(shape, kind)


def pick(slot, even, odd):
    return jnp.where(slot % 2 == 0, even, odd)


def shifted_in(values, first_rows, steps):
    moved = pltpu.roll(values, steps, 0)
    row = lax.broadcasted_iota(jnp.int32, values.shape, 0)
    for index in range(steps):
        moved = jnp.where(row == index, first_rows[2 - steps + index :][:1], moved)
    return moved


def shifted_out(values, next_rows, steps):
    length = values.shape[0]
    moved = pltpu.roll(values, length - steps, 0)
    row = lax.broadcasted_iota(jnp.int32, values.shape, 0)
    for index in range(steps):
        moved = jnp.where(row == length - steps + index, next_rows[index : index + 1], moved)
    return moved


def store_pair(slot, value, keep_ref, sent_ref):
    @pl.when(slot % 2 == 0)
    def _():
        keep_ref[0] = value

    @pl.when(slot % 2 == 1)
    def _():
        sent_ref[0] = value.astype(sent_ref.dtype)


def square_plane(place_ref, dx, dy):
    return (place_ref[0] + dx) % SIDE * SIDE + (place_ref[1] + dy) % SIDE


def project_kernel(place_ref, pair_ref, other_ref, *refs):
    first_refs, refs = refs[: 2 * SIDE], refs[2 * SIDE :]
    normed_ref, proj_ref, mixed_ref, in_ref, out_ref, gains_ref, taps_ref = refs[:7]
    column, taps_column = refs[7:]
    slot = pl.program_id(0)
    width = in_ref.shape[1]
    channels = width // 3
    rows = channels // PLANE

    @pl.when(slot == 0)
    def _():
        for z in range(2):
            for far in range(SIDE):
                source = first_refs[z * SIDE + far]
                for near in range(SIDE):
                    dx, dy = (near, far) if z == 0 else (far, near)
                    plane = square_plane(place_ref, dx, dy)
                    at = pl.ds(pl.multiple_of((z * PLANE + plane) * 2 * rows, 2 * rows), 2 * rows)
                    in_ref[at, :] = source[near, :, :width]
                    column[at, :] = source[near, :, width + channels :].astype(jnp.float32)
                    at = pl.ds(pl.multiple_of(plane * rows, rows), rows)
                    for part in range(2):
                        lanes = slice((2 * z + part) * channels, (2 * z + part + 1) * channels)
                        out_ref[at, lanes] = source[
                            near, part * rows : (part + 1) * rows, width : width + channels
                        ]
                    if z == 0:
                        taps_column[at, :] = source[near, :rows, width + channels :].astype(
                            jnp.float32
                        )
        gains_ref[...] = column[...].T[:8]
        taps_ref[...] = taps_column[...].T[:8]

    values = pick(slot, pair_ref[0, 0], other_ref[0, 0]).astype(jnp.float32)
    normed = (values * norm_scale(values) * gains_ref[0:1]).astype(jnp.bfloat16)
    normed_ref[0] = normed
    projected = jnp.dot(normed, in_ref[...], preferred_element_type=jnp.float32)
    proj_ref[0] = projected
    mixed = projected[:, :channels] * projected[:, 2 * channels :]
    mixed_ref[0] = mixed.astype(jnp.bfloat16)


def branch_kernel(
    mixed_ref, earlier_ref, out_gate_ref, taps_ref, out_ref,
    convolved_ref, gated_ref, keep_ref, sent_ref,
):
    slot = pl.program_id(0)
    mixed = mixed_ref[0].astype(jnp.float32)
    earlier = earlier_ref[0]
    convolved = (
        taps_ref[2:3] * mixed
        + taps_ref[3:4] * shifted_in(mixed, earlier, 1)
        + taps_ref[4:5] * shifted_in(mixed, earlier, 2)
    )
    convolved_ref[0] = convolved
    gated = (out_gate_ref[0] * convolved).astype(jnp.bfloat16)
    gated_ref[0] = gated
    branch = jnp.dot(gated, out_ref[...], preferred_element_type=jnp.float32)
    store_pair(slot, branch, keep_ref, sent_ref)


def ff_kernel(
    own_ref, swap_ref, pair_ref, other_ref, weights_ref, down_ref,
    hidden_ref, grad_gate_ref, grad_up_ref, keep_ref, sent_ref,
):
    slot = pl.program_id(0)
    units = down_ref.shape[0]
    normed = pick(slot, own_ref[0], swap_ref[0])
    outer = pick(slot, pair_ref[0, 0], other_ref[0, 0])
    for start in range(0, units, CHUNK):
        lanes = slice(start, min(start + CHUNK, units))
        up_lanes = slice(units + lanes.start, units + lanes.stop)
        gate = jnp.dot(normed, weights_ref[:, lanes], preferred_element_type=jnp.float32)
        up = jnp.dot(normed, weights_ref[:, up_lanes], preferred_element_type=jnp.float32)
        grad = contract_cols(outer, down_ref[lanes, :])
        sigmoid = jax.nn.sigmoid(gate)
        silu = gate * sigmoid
        hidden_ref[0, :, lanes] = (silu * up).astype(jnp.bfloat16)
        grad_gate = grad * up * sigmoid * (1.0 + gate * (1.0 - sigmoid))
        grad_gate_ref[0, :, lanes] = grad_gate.astype(jnp.bfloat16)
        grad_up_ref[0, :, lanes] = (grad * silu).astype(jnp.bfloat16)
    term = contract_cols(grad_gate_ref[0], weights_ref[:, :units])
    term += contract_cols(grad_up_ref[0], weights_ref[:, units : 2 * units])
    store_pair(slot, term, keep_ref, sent_ref)


def ff_grads_kernel(
    own_ref, swap_ref, pair_ref, other_ref, hidden_ref, grad_gate_ref, grad_up_ref,
    pack_ref,
    gate_total, up_total, down_total,
):
    slot = pl.program_id(0)
    width, units = gate_total.shape
    each = units // PLANE
    block = width // PLANE
    rest = each - block
    normed = pick(slot, own_ref[0], swap_ref[0])
    outer = pick(slot, pair_ref[0, 0], other_ref[0, 0])

    @pl.when(slot == 0)
    def _():
        gate_total[...] = jnp.zeros_like(gate_total)
        up_total[...] = jnp.zeros_like(up_total)
        down_total[...] = jnp.zeros_like(down_total)

    gate_total[...] += contract_rows(normed, grad_gate_ref[0])
    up_total[...] += contract_rows(normed, grad_up_ref[0])
    down_total[...] += contract_rows(hidden_ref[0], outer)

    @pl.when(slot == 3)
    def _():
        pack_ref[:, :units] = gate_total[...].astype(jnp.bfloat16)
        pack_ref[:, units : 2 * units] = up_total[...].astype(jnp.bfloat16)
        for plane in range(PLANE):
            start = plane * each
            for half in range(2):
                to = half * width // 2 + plane * block // 2
                pack_ref[to : to + block // 2, 2 * units : 2 * units + width] = down_total[
                    start + half * block // 2 : start + (half + 1) * block // 2
                ].astype(jnp.bfloat16)
                parts = block // rest // 2
                lanes = width * rest // block
                last = down_total[start + block : start + each]
                pieces = [
                    last[:, (half * parts + part) * lanes : (half * parts + part + 1) * lanes]
                    for part in range(parts)
                ]
                pack_ref[to : to + block // 2, 2 * units + width :] = jnp.concatenate(
                    pieces, 0
                ).astype(jnp.bfloat16)


def gated_back_kernel(
    own_ref, swap_ref, out_ref, convolved_ref, out_gate_ref, grad_out_ref, grad_conv_ref
):
    slot = pl.program_id(0)
    grad_gated = contract_cols(pick(slot, own_ref[0], swap_ref[0]), out_ref[...])
    grad_out_ref[0] = (grad_gated * convolved_ref[0]).astype(jnp.bfloat16)
    grad_conv_ref[0] = grad_gated * out_gate_ref[0]


def out_grads_kernel(
    own_ref, swap_ref, gated_ref, grad_conv_ref, mixed_ref, earlier_ref, gain_ref,
    part_ref, spare_ref,
    total, taps_rows, gain_rows,
):
    slot = pl.program_id(0)
    rows = spare_ref.shape[1] // 4
    channels = gated_ref.shape[2]

    @pl.when(slot == 0)
    def _():
        total[...] = jnp.zeros_like(total)
        taps_rows[...] = jnp.zeros_like(taps_rows)
        gain_rows[...] = jnp.zeros_like(gain_rows)
        gain_rows[1:2] = gain_ref[...]

    total[...] += contract_rows(gated_ref[0], pick(slot, own_ref[0], swap_ref[0]))
    grad_conv = grad_conv_ref[0]
    mixed = mixed_ref[0].astype(jnp.float32)
    earlier = earlier_ref[0]
    lagged = (mixed, shifted_in(mixed, earlier, 1), shifted_in(mixed, earlier, 2))
    for lag, value in enumerate(lagged):
        taps_rows[2 + lag : 3 + lag] += jnp.sum(grad_conv * value, axis=0, keepdims=True)

    @pl.when(slot == 3)
    def _():
        gain_column = gain_rows[...].T
        taps_column = taps_rows[...].T
        for plane in range(PLANE):
            at = slice(plane * rows, (plane + 1) * rows)
            for part in range(4):
                part_ref[plane, part * rows : (part + 1) * rows, :] = total[
                    at, part * channels : (part + 1) * channels
                ].astype(jnp.bfloat16)
            for z in range(2):
                start = (z * PLANE + plane) * 2 * rows
                spare_ref[plane, z * 2 * rows : (z + 1) * 2 * rows, :] = gain_column[
                    start : start + 2 * rows
                ]
            spare_ref[plane, :rows, :] += taps_column[at]


def project_back_kernel(
    place_ref, grad_conv_ref, later_ref, proj_ref, grad_out_ref, normed_ref, in_ref, taps_ref,
    pair_ref, other_ref, part_ref, spare_ref, *refs
):
    pack_refs, (keep_ref, sent_ref, total, gain_rows, gain_column) = refs[: 2 * SIDE], refs[2 * SIDE :]
    slot = pl.program_id(0)
    width = in_ref.shape[1]
    channels = width // 3
    rows = channels // PLANE

    @pl.when(slot == 0)
    def _():
        total[...] = jnp.zeros_like(total)
        gain_rows[...] = jnp.zeros_like(gain_rows)

    grad_conv, later = grad_conv_ref[0], later_ref[0]
    grad_mixed = (
        taps_ref[2:3] * grad_conv
        + taps_ref[3:4] * shifted_out(grad_conv, later, 1)
        + taps_ref[4:5] * shifted_out(grad_conv, later, 2)
    )
    grad_projected = jnp.concatenate(
        [
            (grad_mixed * proj_ref[0, :, 2 * channels :]).astype(jnp.bfloat16),
            grad_out_ref[0],
            (grad_mixed * proj_ref[0, :, :channels]).astype(jnp.bfloat16),
        ],
        1,
    )
    total[...] += contract_rows(normed_ref[0], grad_projected)
    grad_normed = contract_cols(grad_projected, in_ref[...])
    store_pair(slot, grad_normed, keep_ref, sent_ref)
    values = pick(slot, pair_ref[0, 0], other_ref[0, 0]).astype(jnp.float32)
    gain_rows[0:1] += jnp.sum(grad_normed * values * norm_scale(values), axis=0, keepdims=True)

    @pl.when(slot == 3)
    def _():
        gain_column[...] = gain_rows[...].T
        for z in range(2):
            half = slice(z * 2 * rows, (z + 1) * 2 * rows)
            for far in range(SIDE):
                to = pack_refs[z * SIDE + far]
                for near in range(SIDE):
                    dx, dy = (near, far) if z == 0 else (far, near)
                    plane = square_plane(place_ref, dx, dy)
                    at = pl.ds(pl.multiple_of((z * PLANE + plane) * 2 * rows, 2 * rows), 2 * rows)
                    to[near, :, :width] = total[at, :].astype(jnp.bfloat16)
                    to[near, :, width : width + channels] = part_ref[plane, half, :]
                    to[near, :, width + channels :] = (
                        spare_ref[plane, half, :] + gain_column[at, :]
                    ).astype(jnp.bfloat16)


def in_total_kernel(blocks_ref, total_ref, spare_ref):
    members, rows, width = blocks_ref.shape
    channels = (width - SPARE) // 3
    unit = channels // PLANE
    source = lax.broadcasted_iota(jnp.int32, (channels, 2 * channels), 0)
    target = lax.broadcasted_iota(jnp.int32, (channels, 2 * channels), 1)
    for z in range(2):
        for part in range(3):
            total = jnp.zeros((rows, 2 * channels), jnp.float32)
            for core in range(2):
                placed = source // unit * (2 * unit) + core * unit + source % unit == target
                placed = placed.astype(jnp.float32).astype(jnp.bfloat16)
                for rep in range(2):
                    block = blocks_ref[rep * 4 + z * 2 + core]
                    total += jnp.dot(
                        block[:, part * channels : (part + 1) * channels],
                        placed,
                        preferred_element_type=jnp.float32,
                    )
            start = (part * 2 + z) * 2 * channels
            total_ref[:, start : start + 2 * channels] = total
    spare = jnp.zeros((rows, SPARE), jnp.float32)
    for member in range(members):
        spare += blocks_ref[member, :, 3 * channels :].astype(jnp.float32)
    spare_ref[...] = spare


def body(
    tokens, gain_first, w_in, conv_weight, w_out, gain_second, w_gate, w_up, w_down, cotangent
):
    low, wide = jnp.bfloat16, jnp.float32
    length, model_width = tokens.shape
    position = lax.axis_index("fsdp")
    core, plane, z = position % 2, position // 2 % PLANE, position // HALF
    rows = w_in.shape[0]
    channels = model_width // 4

    block = 4 * rows
    rest = w_down.shape[0] - block
    units = w_down.shape[0] * PLANE
    gains = jnp.pad(jnp.stack([gain_first, gain_second], 1), ((0, 0), (0, SPARE - 2)))
    gains = jnp.broadcast_to(gains, (4, rows, SPARE))
    swapped = team_swap(
        jnp.concatenate(
            [by_member(w_gate, 1), by_member(w_up, 1), by_member(w_in, 3), gains], 2
        )
    )
    down_main = w_down[:block].reshape(4, rows, model_width)
    down_rest = w_down[block:].reshape(rest, block // rest, -1).transpose(1, 0, 2)
    ff_all = gather_rows(
        jnp.concatenate(
            [swapped[:, :, : 2 * units], down_main, down_rest.reshape(4, rows, -1)], 2
        )
    )

    in_width = 3 * channels
    conv_lanes = jnp.pad(conv_weight, ((0, 0), (2, SPARE - 5)))
    first_pack = jnp.concatenate(
        [
            swapped[:, :, 2 * units : 2 * units + in_width],
            w_out.reshape(rows, 4, channels).transpose(1, 0, 2),
            swapped[:, :, 2 * units + in_width :] + conv_lanes,
        ],
        2,
    )
    first_pack = first_pack.reshape(2, 2 * rows, -1)
    first_all = fetch(jnp.stack(fetch(first_pack[0], ALONG_X)), ALONG_Y)
    first_all += fetch(jnp.stack(fetch(first_pack[1], ALONG_Y)), ALONG_X)
    place_now = jnp.stack([plane // SIDE, plane % SIDE])
    place_spec = pl.BlockSpec(memory_space=pltpu.SMEM)

    main_rows = ff_all[:, 2 * units : 2 * units + model_width].reshape(2, PLANE, 2 * rows, -1)
    main_rows = main_rows.transpose(1, 0, 2, 3).reshape(PLANE, block, model_width)
    rest_rows = ff_all[:, 2 * units + model_width :].reshape(2, PLANE, 2 * rows, -1)
    rest_rows = rest_rows.transpose(1, 0, 2, 3).reshape(PLANE, block // rest, rest, -1)
    rest_rows = rest_rows.transpose(0, 2, 1, 3).reshape(PLANE, rest, model_width)
    down_full = jnp.concatenate([main_rows, rest_rows], 1).reshape(units, model_width)

    pair = jnp.stack([tokens, cotangent])
    pair = jnp.stack([pair, to_z(pair)])
    other = to_core(pair)
    team_pairs = [pair_of_values(length, model_width, 0)] * 2
    slot_wide, slot_narrow = (4, length, model_width), (4, length, channels)
    pair_wide = (2, length, model_width)
    pairs = [per_pair(length, model_width)] * 2
    narrow = per_slot(length, channels)
    out_gate = per_slot(length, channels, 1)
    edge = per_slot(8, channels)
    out_matrix, in_matrix = whole(channels, model_width), whole(model_width, in_width)
    taps = whole(8, channels)
    unit = 2 * 4 * length * model_width * channels

    normed, projected, mixed, in_full, out_full, gains, kernel = run(
        project_kernel,
        (4,),
        [place_spec] + team_pairs + [whole(*first_all[0].shape)] * len(first_all),
        [
            per_slot(length, model_width),
            per_slot(length, in_width),
            narrow,
            in_matrix,
            out_matrix,
            whole(8, model_width),
            taps,
        ],
        [
            array(slot_wide, low),
            array((4, length, in_width), wide),
            array(slot_narrow, low),
            array((model_width, in_width), low),
            array((channels, model_width), low),
            array((8, model_width), wide),
            array((8, channels), wide),
        ],
        [pltpu.VMEM((model_width, SPARE), wide), pltpu.VMEM((channels, SPARE), wide)],
        3 * unit,
        [place_now, pair, other, *first_all],
    )
    gain_one, gain_two = gains[0], gains[1]

    def by_core(first, second):
        return jnp.where(core == 0, first, second)

    tails = mixed[:, length - 2 :]
    sent = by_core(tails[1::2], tails[0::2])
    received = lax.ppermute(sent, "fsdp", TO_NEXT)
    nothing = jnp.zeros_like(received[0])
    shifted = jnp.where(
        z == 0, jnp.stack([nothing, received[0]]), jnp.stack([received[1], nothing])
    )
    before = jnp.where(plane == 0, shifted, received)
    own_before = by_core(before, tails[1::2])
    other_before = by_core(tails[0::2], before)
    earlier = jnp.stack([own_before[0], other_before[0], own_before[1], other_before[1]])
    earlier = jnp.pad(earlier.astype(wide), ((0, 0), (0, 6), (0, 0)))
    convolved, gated, branch_keep, branch_sent = run(
        branch_kernel,
        (4,),
        [narrow, edge, out_gate, taps, out_matrix],
        [narrow, narrow] + pairs,
        [
            array(slot_narrow, wide),
            array(slot_narrow, low),
            array(pair_wide, wide),
            array(pair_wide, low),
        ],
        [],
        unit,
        [mixed, earlier, projected, kernel, out_full],
    )
    branch_pair = core_sum(branch_keep, branch_sent)
    branch_other = to_z(branch_pair.astype(low))
    branch_other, down_full = lax.optimization_barrier((branch_other, down_full))
    inputs = pair[:, 0].astype(wide)
    middle = inputs + branch_pair + branch_other.astype(wide)[::-1]
    scale_two = norm_scale(middle)
    normed_two = (middle * scale_two * gain_two).astype(low)
    normed_swap = to_core(normed_two)

    outer_pairs = [pair_of_values(length, model_width, 1)] * 2
    unit_slot = per_slot(length, units)
    unit_shape = array((4, length, units), low)
    hidden, grad_gate, grad_upper, grad_keep, grad_sent = run(
        ff_kernel,
        (4,),
        pairs
        + outer_pairs
        + [whole(*ff_all.shape), whole(units, model_width)],
        [unit_slot] * 3 + pairs,
        [unit_shape] * 3 + [array(pair_wide, wide), array(pair_wide, low)],
        [],
        5 * 2 * 4 * length * model_width * units,
        [normed_two, normed_swap, pair, other, ff_all, down_full],
    )
    grad_pair = core_sum(grad_keep, grad_sent)
    grad_sent = grad_pair.astype(low)
    grad_other = to_z(grad_sent)

    grad_sent, hidden, grad_gate, grad_upper = lax.optimization_barrier(
        (grad_sent, hidden, grad_gate, grad_upper)
    )
    (ff_grads,) = run(
        ff_grads_kernel,
        (4,),
        pairs + outer_pairs + [unit_slot] * 3,
        [whole(*ff_all.shape)],
        [array(ff_all.shape, low)],
        [
            pltpu.VMEM((model_width, units), wide),
            pltpu.VMEM((model_width, units), wide),
            pltpu.VMEM((units, model_width), wide),
        ],
        unit,
        [normed_two, normed_swap, pair, other, hidden, grad_gate, grad_upper],
    )
    ff_share = scatter_rows(ff_grads)
    down_term = jnp.dot(
        hidden.reshape(4 * length, units), down_full, preferred_element_type=wide
    )
    grad_other, ff_grads, down_term = lax.optimization_barrier((grad_other, ff_grads, down_term))
    grad_normed_two = grad_pair + grad_other.astype(wide)[::-1]
    grad_gain_two = jnp.sum(grad_normed_two[0] * middle[0] * scale_two[0], axis=0)
    outer = pair[:, 1].astype(wide)
    grad_middle = outer + norm_back(grad_normed_two * gain_two, middle, scale_two)
    grad_branch = grad_middle.astype(low)
    grad_swap = to_core(grad_branch)

    grad_out, grad_conv = run(
        gated_back_kernel,
        (4,),
        pairs + [out_matrix, narrow, out_gate],
        [narrow, narrow],
        [array(slot_narrow, low), array(slot_narrow, wide)],
        [],
        unit,
        [grad_branch, grad_swap, out_full, convolved, projected],
    )
    heads = grad_conv[:, :2]
    sent = by_core(heads[0::2], heads[1::2])
    received = lax.ppermute(sent, "fsdp", TO_PREVIOUS)
    nothing = jnp.zeros_like(received[0])
    shifted = jnp.where(
        z == 0, jnp.stack([received[1], nothing]), jnp.stack([nothing, received[0]])
    )
    after = jnp.where(plane == PLANE - 1, shifted, received)
    own_after = by_core(heads[1::2], after)
    other_after = by_core(after, heads[0::2])
    later = jnp.stack([own_after[0], other_after[0], own_after[1], other_after[1]])
    later = jnp.pad(later, ((0, 0), (0, 6), (0, 0)))
    part_shape, spare_shape = (PLANE, 4 * rows, channels), (PLANE, 4 * rows, SPARE)
    out_part, spare_part = run(
        out_grads_kernel,
        (4,),
        pairs + [narrow, narrow, narrow, edge, whole(1, model_width)],
        [whole(*part_shape), whole(*spare_shape)],
        [array(part_shape, low), array(spare_shape, wide)],
        [
            pltpu.VMEM((channels, model_width), wide),
            pltpu.VMEM((SPARE, channels), wide),
            pltpu.VMEM((SPARE, model_width), wide),
        ],
        unit,
        [grad_branch, grad_swap, gated, grad_conv, mixed, earlier, grad_gain_two[None]],
    )
    *first_grads, normed_keep, normed_sent = run(
        project_back_kernel,
        (4,),
        [
            place_spec,
            narrow,
            edge,
            per_slot(length, in_width),
            narrow,
            per_slot(length, model_width),
            in_matrix,
            taps,
        ]
        + team_pairs
        + [whole(*part_shape), whole(*spare_shape)],
        [whole(*first_all[0].shape)] * len(first_all) + pairs,
        [array(value.shape, low) for value in first_all]
        + [array(pair_wide, wide), array(pair_wide, low)],
        [
            pltpu.VMEM((model_width, in_width), wide),
            pltpu.VMEM((SPARE, model_width), wide),
            pltpu.VMEM((model_width, SPARE), wide),
        ],
        6 * unit,
        [
            place_now,
            grad_conv,
            later,
            projected,
            grad_out,
            normed,
            in_full,
            kernel,
            pair,
            other,
            out_part,
            spare_part,
        ],
    )
    first_half = deliver(first_grads[:SIDE], ALONG_Y).astype(low)
    second_half = deliver(first_grads[SIDE:], ALONG_X).astype(low)
    first_share = jnp.stack(
        [deliver(list(first_half), ALONG_X), deliver(list(second_half), ALONG_Y)]
    )
    first_share = first_share.astype(low).reshape(4, rows, -1)

    down_term, normed_sent = lax.optimization_barrier((down_term, normed_sent))
    down_term = down_term.reshape(4, length, model_width)
    result = middle[0] + own_sum(down_term[0::2], down_term[1::2].astype(low))
    grad_normed_own = own_sum(normed_keep, normed_sent)
    grad_inputs = grad_middle[0] + norm_back(
        grad_normed_own * gain_one, inputs[0], norm_scale(inputs[0])
    )

    def all_pieces(blocks):
        return lax.all_to_all(
            jnp.concatenate([blocks, blocks]),
            ("rep", "fsdp"),
            0,
            0,
            tiled=True,
            axis_index_groups=BOTH_TEAMS,
        )

    def all_reps(blocks):
        swapped = all_pieces(blocks)
        return swapped[:4].astype(wide) + swapped[4:].astype(wide)

    def both_reps(value):
        other = lax.ppermute(value, "rep", [(0, 1), (1, 0)])
        return value.astype(wide) + other.astype(wide)

    down_total = both_reps(ff_share[:, :, 2 * units :])
    down_rest = down_total[:, :, model_width:].reshape(block // rest, rest, -1)
    down_rest = down_rest.transpose(1, 0, 2).reshape(rest, model_width)
    down_total = jnp.concatenate(
        [down_total[:, :, :model_width].reshape(block, model_width), down_rest], 0
    )
    out_total = both_reps(first_share[:, :, in_width:])
    conv_total = out_total[0, :, channels + 2 : channels + 5]
    out_total = out_total[:, :, :channels].transpose(1, 0, 2).reshape(rows, model_width)
    ff_total = all_reps(ff_share[:, :, : 2 * units])
    in_blocks = all_pieces(
        jnp.concatenate(
            [first_share[:, :, :in_width], first_share[:, :, in_width + channels :]], 2
        )
    )
    in_total, gain_total = run(
        in_total_kernel,
        (1,),
        [whole(*in_blocks.shape)],
        [whole(rows, w_in.shape[1]), whole(rows, SPARE)],
        [array((rows, w_in.shape[1]), wide), array((rows, SPARE), wide)],
        [],
        unit,
        [in_blocks],
    )

    return (
        result.astype(low),
        grad_inputs,
        gain_total[:, 0],
        in_total,
        conv_total,
        out_total,
        gain_total[:, 1],
        from_members(ff_total[:, :, :units], 1),
        from_members(ff_total[:, :, units:], 1),
        down_total,
    )


def solution(mesh):
    return jax.shard_map(
        body,
        mesh=mesh,
        in_specs=(
            P(("rep", "fsdp"), None),
            P("fsdp"),
            P("fsdp", None),
            P("fsdp", None),
            P("fsdp", None),
            P("fsdp"),
            P("fsdp", None),
            P("fsdp", None),
            P("fsdp", None),
            P(("rep", "fsdp"), None),
        ),
        out_specs=(
            P(("rep", "fsdp"), None),
            P(("rep", "fsdp"), None),
            P("fsdp"),
            P("fsdp", None),
            P("fsdp", None),
            P("fsdp", None),
            P("fsdp"),
            P("fsdp", None),
            P("fsdp", None),
            P("fsdp", None),
        ),
        check_vma=False,
    )
```

```python
import jax
import jax.numpy as jnp
from jax import lax
from jax.experimental import pallas as pl
from jax.experimental.pallas import tpu as pltpu
from jax.sharding import PartitionSpec as P

epsilon = 1e-05

SIDE = 4
PLANE = SIDE * SIDE
HALF = PLANE * 2
SPARE = 128
CHUNK = 256
VMEM_BYTES = 56 * 1024 * 1024


def place(z, plane, core):
    return (z * PLANE + plane) * 2 + core


def moves(target):
    return [
        (place(z, plane, core), place(*target(z, plane, core)))
        for z in range(2)
        for plane in range(PLANE)
        for core in range(2)
    ]


TO_CORE = moves(lambda z, plane, core: (z, plane, 1 - core))
TO_Z = moves(lambda z, plane, core: (1 - z, plane, core))
TO_NEXT = moves(lambda z, plane, core: (z, (plane + 1) % PLANE, core))
TO_PREVIOUS = moves(lambda z, plane, core: (z, (plane - 1) % PLANE, core))
TEAMS = [
    [place(z, plane, core) for z in range(2) for core in range(2)] for plane in range(PLANE)
]
PLANES = [
    [place(z, plane, core) for plane in range(PLANE)] for z in range(2) for core in range(2)
]
BOTH_TEAMS = [[rep * 2 * HALF + member for rep in range(2) for member in team] for team in TEAMS]


def to_core(value):
    return lax.ppermute(value, "fsdp", TO_CORE)


def to_z(value):
    return lax.ppermute(value, "fsdp", TO_Z)


def norm_scale(values):
    return lax.rsqrt(jnp.mean(values * values, axis=-1, keepdims=True) + epsilon)


def norm_back(grad_normed, values, scale):
    inner = jnp.mean(grad_normed * values, axis=-1, keepdims=True)
    return scale * (grad_normed - values * scale * scale * inner)


def contract_rows(left, right):
    return lax.dot_general(
        left, right, (((0,), (0,)), ((), ())), preferred_element_type=jnp.float32
    )


def contract_cols(left, right):
    return lax.dot_general(
        left, right, (((1,), (1,)), ((), ())), preferred_element_type=jnp.float32
    )


def by_member(shard, parts):
    rows, columns = shard.shape
    split = shard.reshape(rows, parts, 2, PLANE, 2, -1)
    return split.transpose(2, 4, 0, 1, 3, 5).reshape(4, rows, columns // 4)


def from_members(blocks, parts):
    members, rows, columns = blocks.shape
    split = blocks.reshape(2, 2, rows, parts, PLANE, -1)
    return split.transpose(2, 3, 0, 4, 1, 5).reshape(rows, 4 * columns)


def team_swap(blocks):
    return lax.all_to_all(blocks, "fsdp", 0, 0, tiled=True, axis_index_groups=TEAMS)


def plane_swap(blocks):
    return lax.all_to_all(blocks, "fsdp", 0, 0, tiled=True, axis_index_groups=PLANES)


def gather_rows(blocks):
    members, rows, columns = blocks.shape
    return lax.all_gather(
        blocks.reshape(2, 2 * rows, columns),
        "fsdp",
        axis=1,
        tiled=True,
        axis_index_groups=PLANES,
    ).reshape(-1, columns)


def scatter_rows(value):
    total, columns = value.shape
    return lax.psum_scatter(
        value.reshape(2, total // 2, columns),
        "fsdp",
        scatter_dimension=1,
        tiled=True,
        axis_index_groups=PLANES,
    ).reshape(4, -1, columns)


def slots_of(pair, other):
    return jnp.stack([pair[0], other[0], pair[1], other[1]])


def core_sum(keep, sent):
    return keep + to_core(sent).astype(jnp.float32)


def own_sum(keep, sent):
    pair = core_sum(keep, sent)
    return pair[0] + to_z(pair[1].astype(jnp.bfloat16)).astype(jnp.float32)


def whole(*shape):
    return pl.BlockSpec(shape, lambda *_: (0,) * len(shape))


def per_slot(length, width, column=0):
    return pl.BlockSpec((1, length, width), lambda slot: (slot, 0, column))


def per_pair(length, width):
    return pl.BlockSpec((1, length, width), lambda slot: (slot // 2, 0, 0))


def pair_of_values(length, width, which):
    return pl.BlockSpec((1, 1, length, width), lambda slot: (slot // 2, which, 0, 0))


def run(kernel, grid, in_specs, out_specs, out_shape, scratch, flops, values):
    moved = 0 if flops == 0 else sum(value.size * value.dtype.itemsize for value in values)
    moved += 0 if flops == 0 else sum(value.size * value.dtype.itemsize for value in out_shape)
    return pl.pallas_call(
        kernel,
        grid=grid,
        in_specs=in_specs,
        out_specs=out_specs,
        out_shape=out_shape,
        scratch_shapes=scratch,
        compiler_params=pltpu.CompilerParams(vmem_limit_bytes=VMEM_BYTES),
        cost_estimate=pl.CostEstimate(flops=flops, bytes_accessed=moved, transcendentals=0),
    )(*values)


def array(shape, kind):
    return jax.ShapeDtypeStruct(shape, kind)


def pick(slot, even, odd):
    return jnp.where(slot % 2 == 0, even, odd)


def shifted_in(values, first_rows, steps):
    moved = pltpu.roll(values, steps, 0)
    row = lax.broadcasted_iota(jnp.int32, values.shape, 0)
    for index in range(steps):
        moved = jnp.where(row == index, first_rows[2 - steps + index :][:1], moved)
    return moved


def shifted_out(values, next_rows, steps):
    length = values.shape[0]
    moved = pltpu.roll(values, length - steps, 0)
    row = lax.broadcasted_iota(jnp.int32, values.shape, 0)
    for index in range(steps):
        moved = jnp.where(row == length - steps + index, next_rows[index : index + 1], moved)
    return moved


def store_pair(slot, value, keep_ref, sent_ref):
    @pl.when(slot % 2 == 0)
    def _():
        keep_ref[0] = value

    @pl.when(slot % 2 == 1)
    def _():
        sent_ref[0] = value.astype(sent_ref.dtype)


def project_kernel(
    pair_ref, other_ref, first_ref,
    normed_ref, proj_ref, mixed_ref, in_ref, out_ref, gains_ref, taps_ref,
    column, taps_column,
):
    slot = pl.program_id(0)
    width = in_ref.shape[1]
    channels = width // 3
    rows = channels // PLANE

    @pl.when(slot == 0)
    def _():
        for plane in range(PLANE):
            for z in range(2):
                at = pl.ds((z * PLANE + plane) * 2 * rows, 2 * rows)
                source = pl.ds(z * 2 * rows, 2 * rows)
                in_ref[at, :] = first_ref[plane, source, :width]
                column[at, :] = first_ref[plane, source, width + channels :].astype(jnp.float32)
            at = pl.ds(plane * rows, rows)
            for part in range(4):
                out_ref[at, part * channels : (part + 1) * channels] = first_ref[
                    plane, pl.ds(part * rows, rows), width : width + channels
                ]
            taps_column[at, :] = first_ref[plane, :rows, width + channels :].astype(jnp.float32)
        gains_ref[...] = column[...].T[:8]
        taps_ref[...] = taps_column[...].T[:8]

    values = pick(slot, pair_ref[0, 0], other_ref[0, 0]).astype(jnp.float32)
    normed = (values * norm_scale(values) * gains_ref[0:1]).astype(jnp.bfloat16)
    normed_ref[0] = normed
    projected = jnp.dot(normed, in_ref[...], preferred_element_type=jnp.float32)
    proj_ref[0] = projected
    mixed = projected[:, :channels] * projected[:, 2 * channels :]
    mixed_ref[0] = mixed.astype(jnp.bfloat16)


def branch_kernel(
    mixed_ref, earlier_ref, out_gate_ref, taps_ref, out_ref,
    convolved_ref, gated_ref, keep_ref, sent_ref,
):
    slot = pl.program_id(0)
    mixed = mixed_ref[0].astype(jnp.float32)
    earlier = earlier_ref[0]
    convolved = (
        taps_ref[2:3] * mixed
        + taps_ref[3:4] * shifted_in(mixed, earlier, 1)
        + taps_ref[4:5] * shifted_in(mixed, earlier, 2)
    )
    convolved_ref[0] = convolved
    gated = (out_gate_ref[0] * convolved).astype(jnp.bfloat16)
    gated_ref[0] = gated
    branch = jnp.dot(gated, out_ref[...], preferred_element_type=jnp.float32)
    store_pair(slot, branch, keep_ref, sent_ref)


def ff_kernel(
    own_ref, swap_ref, pair_ref, other_ref, weights_ref, down_ref,
    hidden_ref, grad_gate_ref, grad_up_ref, keep_ref, sent_ref,
):
    slot = pl.program_id(0)
    units = down_ref.shape[0]
    normed = pick(slot, own_ref[0], swap_ref[0])
    outer = pick(slot, pair_ref[0, 0], other_ref[0, 0])
    for start in range(0, units, CHUNK):
        lanes = slice(start, min(start + CHUNK, units))
        up_lanes = slice(units + lanes.start, units + lanes.stop)
        gate = jnp.dot(normed, weights_ref[:, lanes], preferred_element_type=jnp.float32)
        up = jnp.dot(normed, weights_ref[:, up_lanes], preferred_element_type=jnp.float32)
        grad = contract_cols(outer, down_ref[lanes, :])
        sigmoid = jax.nn.sigmoid(gate)
        silu = gate * sigmoid
        hidden_ref[0, :, lanes] = (silu * up).astype(jnp.bfloat16)
        grad_gate = grad * up * sigmoid * (1.0 + gate * (1.0 - sigmoid))
        grad_gate_ref[0, :, lanes] = grad_gate.astype(jnp.bfloat16)
        grad_up_ref[0, :, lanes] = (grad * silu).astype(jnp.bfloat16)
    term = contract_cols(grad_gate_ref[0], weights_ref[:, :units])
    term += contract_cols(grad_up_ref[0], weights_ref[:, units : 2 * units])
    store_pair(slot, term, keep_ref, sent_ref)


def ff_grads_kernel(
    own_ref, swap_ref, pair_ref, other_ref, hidden_ref, grad_gate_ref, grad_up_ref, down_ref,
    pack_ref, keep_ref, sent_ref,
    gate_total, up_total, down_total,
):
    slot = pl.program_id(0)
    width, units = gate_total.shape
    each = units // PLANE
    block = width // PLANE
    rest = each - block
    normed = pick(slot, own_ref[0], swap_ref[0])
    outer = pick(slot, pair_ref[0, 0], other_ref[0, 0])

    @pl.when(slot == 0)
    def _():
        gate_total[...] = jnp.zeros_like(gate_total)
        up_total[...] = jnp.zeros_like(up_total)
        down_total[...] = jnp.zeros_like(down_total)

    gate_total[...] += contract_rows(normed, grad_gate_ref[0])
    up_total[...] += contract_rows(normed, grad_up_ref[0])
    down_total[...] += contract_rows(hidden_ref[0], outer)
    term = jnp.dot(hidden_ref[0], down_ref[...], preferred_element_type=jnp.float32)
    store_pair(slot, term, keep_ref, sent_ref)

    @pl.when(slot == 3)
    def _():
        pack_ref[:, :units] = gate_total[...].astype(jnp.bfloat16)
        pack_ref[:, units : 2 * units] = up_total[...].astype(jnp.bfloat16)
        for plane in range(PLANE):
            start = plane * each
            for half in range(2):
                to = half * width // 2 + plane * block // 2
                pack_ref[to : to + block // 2, 2 * units : 2 * units + width] = down_total[
                    start + half * block // 2 : start + (half + 1) * block // 2
                ].astype(jnp.bfloat16)
                parts = block // rest // 2
                lanes = width * rest // block
                last = down_total[start + block : start + each]
                pieces = [
                    last[:, (half * parts + part) * lanes : (half * parts + part + 1) * lanes]
                    for part in range(parts)
                ]
                pack_ref[to : to + block // 2, 2 * units + width :] = jnp.concatenate(
                    pieces, 0
                ).astype(jnp.bfloat16)


def gated_back_kernel(
    own_ref, swap_ref, out_ref, convolved_ref, out_gate_ref, grad_out_ref, grad_conv_ref
):
    slot = pl.program_id(0)
    grad_gated = contract_cols(pick(slot, own_ref[0], swap_ref[0]), out_ref[...])
    grad_out_ref[0] = (grad_gated * convolved_ref[0]).astype(jnp.bfloat16)
    grad_conv_ref[0] = grad_gated * out_gate_ref[0]


def out_grads_kernel(
    own_ref, swap_ref, gated_ref, grad_conv_ref, mixed_ref, earlier_ref, gain_ref,
    part_ref, spare_ref,
    total, taps_rows, gain_rows,
):
    slot = pl.program_id(0)
    rows = spare_ref.shape[1] // 4
    channels = gated_ref.shape[2]

    @pl.when(slot == 0)
    def _():
        total[...] = jnp.zeros_like(total)
        taps_rows[...] = jnp.zeros_like(taps_rows)
        gain_rows[...] = jnp.zeros_like(gain_rows)
        gain_rows[1:2] = gain_ref[...]

    total[...] += contract_rows(gated_ref[0], pick(slot, own_ref[0], swap_ref[0]))
    grad_conv = grad_conv_ref[0]
    mixed = mixed_ref[0].astype(jnp.float32)
    earlier = earlier_ref[0]
    lagged = (mixed, shifted_in(mixed, earlier, 1), shifted_in(mixed, earlier, 2))
    for lag, value in enumerate(lagged):
        taps_rows[2 + lag : 3 + lag] += jnp.sum(grad_conv * value, axis=0, keepdims=True)

    @pl.when(slot == 3)
    def _():
        gain_column = gain_rows[...].T
        taps_column = taps_rows[...].T
        for plane in range(PLANE):
            at = slice(plane * rows, (plane + 1) * rows)
            for part in range(4):
                part_ref[plane, part * rows : (part + 1) * rows, :] = total[
                    at, part * channels : (part + 1) * channels
                ].astype(jnp.bfloat16)
            for z in range(2):
                start = (z * PLANE + plane) * 2 * rows
                spare_ref[plane, z * 2 * rows : (z + 1) * 2 * rows, :] = gain_column[
                    start : start + 2 * rows
                ]
            spare_ref[plane, :rows, :] += taps_column[at]


def project_back_kernel(
    grad_conv_ref, later_ref, proj_ref, grad_out_ref, normed_ref, in_ref, taps_ref,
    pair_ref, other_ref, part_ref, spare_ref,
    pack_ref, keep_ref, sent_ref,
    total, gain_rows,
):
    slot = pl.program_id(0)
    width = in_ref.shape[1]
    channels = width // 3
    rows = channels // PLANE

    @pl.when(slot == 0)
    def _():
        total[...] = jnp.zeros_like(total)
        gain_rows[...] = jnp.zeros_like(gain_rows)

    grad_conv, later = grad_conv_ref[0], later_ref[0]
    grad_mixed = (
        taps_ref[2:3] * grad_conv
        + taps_ref[3:4] * shifted_out(grad_conv, later, 1)
        + taps_ref[4:5] * shifted_out(grad_conv, later, 2)
    )
    grad_projected = jnp.concatenate(
        [
            (grad_mixed * proj_ref[0, :, 2 * channels :]).astype(jnp.bfloat16),
            grad_out_ref[0],
            (grad_mixed * proj_ref[0, :, :channels]).astype(jnp.bfloat16),
        ],
        1,
    )
    total[...] += contract_rows(normed_ref[0], grad_projected)
    grad_normed = contract_cols(grad_projected, in_ref[...])
    store_pair(slot, grad_normed, keep_ref, sent_ref)
    values = pick(slot, pair_ref[0, 0], other_ref[0, 0]).astype(jnp.float32)
    gain_rows[0:1] += jnp.sum(grad_normed * values * norm_scale(values), axis=0, keepdims=True)

    @pl.when(slot == 3)
    def _():
        gain_column = gain_rows[...].T
        for plane in range(PLANE):
            for z in range(2):
                start = (z * PLANE + plane) * 2 * rows
                to = slice(z * 2 * rows, (z + 1) * 2 * rows)
                pack_ref[plane, to, :width] = total[start : start + 2 * rows].astype(jnp.bfloat16)
                pack_ref[plane, to, width + channels :] = (
                    spare_ref[plane, to] + gain_column[start : start + 2 * rows]
                ).astype(jnp.bfloat16)
            pack_ref[plane, :, width : width + channels] = part_ref[plane]


def in_total_kernel(blocks_ref, total_ref, spare_ref):
    members, rows, width = blocks_ref.shape
    channels = total_ref.shape[1] // 12
    first = width - SPARE - 3 * channels
    unit = channels // PLANE
    source = lax.broadcasted_iota(jnp.int32, (channels, 2 * channels), 0)
    target = lax.broadcasted_iota(jnp.int32, (channels, 2 * channels), 1)
    for z in range(2):
        for part in range(3):
            total = jnp.zeros((rows, 2 * channels), jnp.float32)
            for core in range(2):
                placed = source // unit * (2 * unit) + core * unit + source % unit == target
                placed = placed.astype(jnp.float32).astype(jnp.bfloat16)
                for rep in range(2):
                    block = blocks_ref[rep * 4 + z * 2 + core]
                    total += jnp.dot(
                        block[:, first + part * channels : first + (part + 1) * channels],
                        placed,
                        preferred_element_type=jnp.float32,
                    )
            start = (part * 2 + z) * 2 * channels
            total_ref[:, start : start + 2 * channels] = total
    spare = jnp.zeros((rows, SPARE), jnp.float32)
    for member in range(members):
        spare += blocks_ref[member, :, width - SPARE :].astype(jnp.float32)
    spare_ref[...] = spare


def body(
    tokens, gain_first, w_in, conv_weight, w_out, gain_second, w_gate, w_up, w_down, cotangent
):
    low, wide = jnp.bfloat16, jnp.float32
    length, model_width = tokens.shape
    position = lax.axis_index("fsdp")
    core, plane, z = position % 2, position // 2 % PLANE, position // HALF
    rows = w_in.shape[0]
    channels = model_width // 4

    block = 4 * rows
    rest = w_down.shape[0] - block
    units = w_down.shape[0] * PLANE
    gains = jnp.pad(jnp.stack([gain_first, gain_second], 1), ((0, 0), (0, SPARE - 2)))
    gains = jnp.broadcast_to(gains, (4, rows, SPARE))
    swapped = team_swap(
        jnp.concatenate(
            [by_member(w_gate, 1), by_member(w_up, 1), by_member(w_in, 3), gains], 2
        )
    )
    down_main = w_down[:block].reshape(4, rows, model_width)
    down_rest = w_down[block:].reshape(rest, block // rest, -1).transpose(1, 0, 2)
    ff_all = gather_rows(
        jnp.concatenate(
            [swapped[:, :, : 2 * units], down_main, down_rest.reshape(4, rows, -1)], 2
        )
    )

    in_width = 3 * channels
    conv_lanes = jnp.pad(conv_weight, ((0, 0), (2, SPARE - 5)))
    first_pack = jnp.concatenate(
        [
            swapped[:, :, 2 * units : 2 * units + in_width],
            w_out.reshape(rows, 4, channels).transpose(1, 0, 2),
            swapped[:, :, 2 * units + in_width :] + conv_lanes,
        ],
        2,
    )
    first_all = plane_swap(jnp.broadcast_to(first_pack, (PLANE,) + first_pack.shape))
    first_all = first_all.reshape(PLANE, 4 * rows, -1)

    main_rows = ff_all[:, 2 * units : 2 * units + model_width].reshape(2, PLANE, 2 * rows, -1)
    main_rows = main_rows.transpose(1, 0, 2, 3).reshape(PLANE, block, model_width)
    rest_rows = ff_all[:, 2 * units + model_width :].reshape(2, PLANE, 2 * rows, -1)
    rest_rows = rest_rows.transpose(1, 0, 2, 3).reshape(PLANE, block // rest, rest, -1)
    rest_rows = rest_rows.transpose(0, 2, 1, 3).reshape(PLANE, rest, model_width)
    down_full = jnp.concatenate([main_rows, rest_rows], 1).reshape(units, model_width)

    pair = jnp.stack([tokens, cotangent])
    pair = jnp.stack([pair, to_z(pair)])
    other = to_core(pair)
    team_pairs = [pair_of_values(length, model_width, 0)] * 2
    slot_wide, slot_narrow = (4, length, model_width), (4, length, channels)
    pair_wide = (2, length, model_width)
    pairs = [per_pair(length, model_width)] * 2
    narrow = per_slot(length, channels)
    out_gate = per_slot(length, channels, 1)
    edge = per_slot(8, channels)
    out_matrix, in_matrix = whole(channels, model_width), whole(model_width, in_width)
    taps = whole(8, channels)
    unit = 2 * 4 * length * model_width * channels

    normed, projected, mixed, in_full, out_full, gains, kernel = run(
        project_kernel,
        (4,),
        team_pairs + [whole(*first_all.shape)],
        [
            per_slot(length, model_width),
            per_slot(length, in_width),
            narrow,
            in_matrix,
            out_matrix,
            whole(8, model_width),
            taps,
        ],
        [
            array(slot_wide, low),
            array((4, length, in_width), wide),
            array(slot_narrow, low),
            array((model_width, in_width), low),
            array((channels, model_width), low),
            array((8, model_width), wide),
            array((8, channels), wide),
        ],
        [pltpu.VMEM((model_width, SPARE), wide), pltpu.VMEM((channels, SPARE), wide)],
        3 * unit,
        [pair, other, first_all],
    )
    gain_one, gain_two = gains[0], gains[1]

    def by_core(first, second):
        return jnp.where(core == 0, first, second)

    tails = mixed[:, length - 2 :]
    sent = by_core(tails[1::2], tails[0::2])
    received = lax.ppermute(sent, "fsdp", TO_NEXT)
    nothing = jnp.zeros_like(received[0])
    shifted = jnp.where(
        z == 0, jnp.stack([nothing, received[0]]), jnp.stack([received[1], nothing])
    )
    before = jnp.where(plane == 0, shifted, received)
    own_before = by_core(before, tails[1::2])
    other_before = by_core(tails[0::2], before)
    earlier = jnp.stack([own_before[0], other_before[0], own_before[1], other_before[1]])
    earlier = jnp.pad(earlier.astype(wide), ((0, 0), (0, 6), (0, 0)))
    convolved, gated, branch_keep, branch_sent = run(
        branch_kernel,
        (4,),
        [narrow, edge, out_gate, taps, out_matrix],
        [narrow, narrow] + pairs,
        [
            array(slot_narrow, wide),
            array(slot_narrow, low),
            array(pair_wide, wide),
            array(pair_wide, low),
        ],
        [],
        unit,
        [mixed, earlier, projected, kernel, out_full],
    )
    branch_pair = core_sum(branch_keep, branch_sent)
    branch_other = to_z(branch_pair.astype(low))
    branch_other, down_full = lax.optimization_barrier((branch_other, down_full))
    inputs = pair[:, 0].astype(wide)
    middle = inputs + branch_pair + branch_other.astype(wide)[::-1]
    scale_two = norm_scale(middle)
    normed_two = (middle * scale_two * gain_two).astype(low)
    normed_swap = to_core(normed_two)

    outer_pairs = [pair_of_values(length, model_width, 1)] * 2
    unit_slot = per_slot(length, units)
    unit_shape = array((4, length, units), low)
    hidden, grad_gate, grad_upper, grad_keep, grad_sent = run(
        ff_kernel,
        (4,),
        pairs
        + outer_pairs
        + [whole(*ff_all.shape), whole(units, model_width)],
        [unit_slot] * 3 + pairs,
        [unit_shape] * 3 + [array(pair_wide, wide), array(pair_wide, low)],
        [],
        5 * 2 * 4 * length * model_width * units,
        [normed_two, normed_swap, pair, other, ff_all, down_full],
    )
    grad_pair = core_sum(grad_keep, grad_sent)
    grad_sent = grad_pair.astype(low)
    grad_other = to_z(grad_sent)

    grad_sent, hidden, grad_gate, grad_upper = lax.optimization_barrier(
        (grad_sent, hidden, grad_gate, grad_upper)
    )
    ff_grads, down_keep, down_sent = run(
        ff_grads_kernel,
        (4,),
        pairs + outer_pairs + [unit_slot] * 3 + [whole(units, model_width)],
        [whole(*ff_all.shape)] + pairs,
        [array(ff_all.shape, low), array(pair_wide, wide), array(pair_wide, low)],
        [
            pltpu.VMEM((model_width, units), wide),
            pltpu.VMEM((model_width, units), wide),
            pltpu.VMEM((units, model_width), wide),
        ],
        0,
        [normed_two, normed_swap, pair, other, hidden, grad_gate, grad_upper, down_full],
    )
    ff_share = scatter_rows(ff_grads)
    grad_other, down_keep = lax.optimization_barrier((grad_other, down_keep))
    grad_normed_two = grad_pair + grad_other.astype(wide)[::-1]
    grad_gain_two = jnp.sum(grad_normed_two[0] * middle[0] * scale_two[0], axis=0)
    outer = pair[:, 1].astype(wide)
    grad_middle = outer + norm_back(grad_normed_two * gain_two, middle, scale_two)
    grad_branch = grad_middle.astype(low)
    grad_swap = to_core(grad_branch)

    grad_out, grad_conv = run(
        gated_back_kernel,
        (4,),
        pairs + [out_matrix, narrow, out_gate],
        [narrow, narrow],
        [array(slot_narrow, low), array(slot_narrow, wide)],
        [],
        unit,
        [grad_branch, grad_swap, out_full, convolved, projected],
    )
    heads = grad_conv[:, :2]
    sent = by_core(heads[0::2], heads[1::2])
    received = lax.ppermute(sent, "fsdp", TO_PREVIOUS)
    nothing = jnp.zeros_like(received[0])
    shifted = jnp.where(
        z == 0, jnp.stack([received[1], nothing]), jnp.stack([nothing, received[0]])
    )
    after = jnp.where(plane == PLANE - 1, shifted, received)
    own_after = by_core(heads[1::2], after)
    other_after = by_core(after, heads[0::2])
    later = jnp.stack([own_after[0], other_after[0], own_after[1], other_after[1]])
    later = jnp.pad(later, ((0, 0), (0, 6), (0, 0)))
    part_shape, spare_shape = (PLANE, 4 * rows, channels), (PLANE, 4 * rows, SPARE)
    out_part, spare_part = run(
        out_grads_kernel,
        (4,),
        pairs + [narrow, narrow, narrow, edge, whole(1, model_width)],
        [whole(*part_shape), whole(*spare_shape)],
        [array(part_shape, low), array(spare_shape, wide)],
        [
            pltpu.VMEM((channels, model_width), wide),
            pltpu.VMEM((SPARE, channels), wide),
            pltpu.VMEM((SPARE, model_width), wide),
        ],
        unit,
        [grad_branch, grad_swap, gated, grad_conv, mixed, earlier, grad_gain_two[None]],
    )
    first_grads, normed_keep, normed_sent = run(
        project_back_kernel,
        (4,),
        [
            narrow,
            edge,
            per_slot(length, in_width),
            narrow,
            per_slot(length, model_width),
            in_matrix,
            taps,
        ]
        + team_pairs
        + [whole(*part_shape), whole(*spare_shape)],
        [whole(*first_all.shape)] + pairs,
        [array(first_all.shape, low), array(pair_wide, wide), array(pair_wide, low)],
        [pltpu.VMEM((model_width, in_width), wide), pltpu.VMEM((SPARE, model_width), wide)],
        6 * unit,
        [
            grad_conv,
            later,
            projected,
            grad_out,
            normed,
            in_full,
            kernel,
            pair,
            other,
            out_part,
            spare_part,
        ],
    )
    first_grads = first_grads.reshape(PLANE, 4, rows, -1)
    first_arrived = plane_swap(first_grads)

    down_sent, normed_sent = lax.optimization_barrier((down_sent, normed_sent))
    result = middle[0] + own_sum(down_keep, down_sent)
    grad_normed_own = own_sum(normed_keep, normed_sent)
    grad_inputs = grad_middle[0] + norm_back(
        grad_normed_own * gain_one, inputs[0], norm_scale(inputs[0])
    )
    result, grad_inputs, first_arrived = lax.optimization_barrier(
        (result.astype(low), grad_inputs, first_arrived)
    )
    first_share = jnp.sum(first_arrived.astype(wide), axis=0).astype(low)

    def both_reps(value):
        other = lax.ppermute(value, "rep", [(0, 1), (1, 0)])
        return value.astype(wide) + other.astype(wide)

    down_total = both_reps(ff_share[:, :, 2 * units :])
    down_rest = down_total[:, :, model_width:].reshape(block // rest, rest, -1)
    down_rest = down_rest.transpose(1, 0, 2).reshape(rest, model_width)
    down_total = jnp.concatenate(
        [down_total[:, :, :model_width].reshape(block, model_width), down_rest], 0
    )
    out_total = both_reps(first_share[:, :, in_width:])
    conv_total = out_total[0, :, channels + 2 : channels + 5]
    out_total = out_total[:, :, :channels].transpose(1, 0, 2).reshape(rows, model_width)
    blocks = jnp.concatenate(
        [
            ff_share[:, :, : 2 * units],
            first_share[:, :, :in_width],
            first_share[:, :, in_width + channels :],
        ],
        2,
    )
    blocks = lax.all_to_all(
        jnp.concatenate([blocks, blocks]),
        ("rep", "fsdp"),
        0,
        0,
        tiled=True,
        axis_index_groups=BOTH_TEAMS,
    )
    in_total, gain_total = run(
        in_total_kernel,
        (1,),
        [whole(*blocks.shape)],
        [whole(rows, w_in.shape[1]), whole(rows, SPARE)],
        [array((rows, w_in.shape[1]), wide), array((rows, SPARE), wide)],
        [],
        unit,
        [blocks],
    )
    ff_total = blocks[:, :, : 2 * units].astype(wide)
    ff_total = ff_total[:4] + ff_total[4:]

    return (
        result,
        grad_inputs,
        gain_total[:, 0],
        in_total,
        conv_total,
        out_total,
        gain_total[:, 1],
        from_members(ff_total[:, :, :units], 1),
        from_members(ff_total[:, :, units:], 1),
        down_total,
    )


def solution(mesh):
    return jax.shard_map(
        body,
        mesh=mesh,
        in_specs=(
            P(("rep", "fsdp"), None),
            P("fsdp"),
            P("fsdp", None),
            P("fsdp", None),
            P("fsdp", None),
            P("fsdp"),
            P("fsdp", None),
            P("fsdp", None),
            P("fsdp", None),
            P(("rep", "fsdp"), None),
        ),
        out_specs=(
            P(("rep", "fsdp"), None),
            P(("rep", "fsdp"), None),
            P("fsdp"),
            P("fsdp", None),
            P("fsdp", None),
            P("fsdp", None),
            P("fsdp"),
            P("fsdp", None),
            P("fsdp", None),
            P("fsdp", None),
        ),
        check_vma=False,
    )
```

```python
import jax
import jax.numpy as jnp
from jax import lax
from jax.experimental import pallas as pl
from jax.experimental.pallas import tpu as pltpu
from jax.sharding import PartitionSpec as P

epsilon = 1e-05

SIDE = 4
PLANE = SIDE * SIDE
HALF = PLANE * 2
SPARE = 128
EDGE = 16
CHUNK = 256
MIB = 1024 * 1024


def place(z, plane, core):
    return (z * PLANE + plane) * 2 + core


def moves(target):
    return [
        (place(z, plane, core), place(*target(z, plane, core)))
        for z in range(2)
        for plane in range(PLANE)
        for core in range(2)
    ]


TO_CORE = moves(lambda z, plane, core: (z, plane, 1 - core))
TO_Z = moves(lambda z, plane, core: (1 - z, plane, core))
TO_FOLLOWING = [(index, index + 1) for index in range(2 * HALF - 1)]
TO_PREVIOUS = moves(lambda z, plane, core: (z, (plane - 1) % PLANE, core))
TEAMS = [
    [place(z, plane, core) for z in range(2) for core in range(2)] for plane in range(PLANE)
]
PLANES = [
    [place(z, plane, core) for plane in range(PLANE)] for z in range(2) for core in range(2)
]
BOTH_TEAMS = [[rep * 2 * HALF + member for rep in range(2) for member in team] for team in TEAMS]


def to_core(value):
    return lax.ppermute(value, "fsdp", TO_CORE)


def to_z(value):
    return lax.ppermute(value, "fsdp", TO_Z)


def norm_scale(values):
    return lax.rsqrt(jnp.mean(values * values, axis=-1, keepdims=True) + epsilon)


def norm_back(grad_normed, values, scale):
    inner = jnp.mean(grad_normed * values, axis=-1, keepdims=True)
    return scale * (grad_normed - values * scale * scale * inner)


def contract_rows(left, right):
    return lax.dot_general(
        left, right, (((0,), (0,)), ((), ())), preferred_element_type=jnp.float32
    )


def contract_cols(left, right):
    return lax.dot_general(
        left, right, (((1,), (1,)), ((), ())), preferred_element_type=jnp.float32
    )


def by_member(shard, parts):
    rows, columns = shard.shape
    split = shard.reshape(rows, parts, 2, PLANE, 2, -1)
    return split.transpose(2, 4, 0, 1, 3, 5).reshape(4, rows, columns // 4)


def from_members(blocks, parts):
    members, rows, columns = blocks.shape
    split = blocks.reshape(2, 2, rows, parts, PLANE, -1)
    return split.transpose(2, 3, 0, 4, 1, 5).reshape(rows, 4 * columns)


def team_swap(blocks):
    return lax.all_to_all(blocks, "fsdp", 0, 0, tiled=True, axis_index_groups=TEAMS)


def plane_swap(blocks):
    return lax.all_to_all(blocks, "fsdp", 0, 0, tiled=True, axis_index_groups=PLANES)


def gather_rows(blocks):
    members, rows, columns = blocks.shape
    return lax.all_gather(
        blocks.reshape(2, 2 * rows, columns),
        "fsdp",
        axis=1,
        tiled=True,
        axis_index_groups=PLANES,
    ).reshape(-1, columns)


def scatter_rows(value):
    total, columns = value.shape
    return lax.psum_scatter(
        value.reshape(2, total // 2, columns),
        "fsdp",
        scatter_dimension=1,
        tiled=True,
        axis_index_groups=PLANES,
    ).reshape(4, -1, columns)


def slots_of(pair, other):
    return jnp.stack([pair[0], other[0], pair[1], other[1]])


def core_sum(keep, sent):
    return keep + to_core(sent).astype(jnp.float32)


def own_sum(keep, sent):
    pair = core_sum(keep, sent)
    return pair[0] + to_z(pair[1].astype(jnp.bfloat16)).astype(jnp.float32)


def whole(*shape):
    return pl.BlockSpec(shape, lambda *_: (0,) * len(shape))


def per_slot(length, width, column=0):
    return pl.BlockSpec((1, length, width), lambda slot: (slot, 0, column))


def per_pair(length, width):
    return pl.BlockSpec((1, length, width), lambda slot: (slot // 2, 0, 0))


def pair_of_values(length, width, which):
    return pl.BlockSpec((1, 1, length, width), lambda slot: (slot // 2, which, 0, 0))


def run(kernel, grid, in_specs, out_specs, out_shape, scratch, room, busy, values):
    return pl.pallas_call(
        kernel,
        grid=grid,
        in_specs=in_specs,
        out_specs=out_specs,
        out_shape=out_shape,
        scratch_shapes=scratch,
        compiler_params=pltpu.CompilerParams(vmem_limit_bytes=room * MIB),
        cost_estimate=pl.CostEstimate(
            flops=int(busy * 1.15e9), bytes_accessed=0, transcendentals=0
        ),
    )(*values)


def array(shape, kind):
    return jax.ShapeDtypeStruct(shape, kind)


def pick(slot, even, odd):
    return jnp.where(slot % 2 == 0, even, odd)


def shifted_in(values, rows_before, steps):
    moved = pltpu.roll(values, steps, 0)
    row = lax.broadcasted_iota(jnp.int32, values.shape, 0)
    for index in range(steps):
        at = EDGE - steps + index
        moved = jnp.where(row == index, rows_before[at : at + 1], moved)
    return moved


def shifted_out(values, next_rows, steps):
    length = values.shape[0]
    moved = pltpu.roll(values, length - steps, 0)
    row = lax.broadcasted_iota(jnp.int32, values.shape, 0)
    for index in range(steps):
        moved = jnp.where(row == length - steps + index, next_rows[index : index + 1], moved)
    return moved


def store_pair(slot, value, keep_ref, sent_ref):
    @pl.when(slot % 2 == 0)
    def _():
        keep_ref[0] = value

    @pl.when(slot % 2 == 1)
    def _():
        sent_ref[0] = value.astype(sent_ref.dtype)


def project_kernel(
    pair_ref, other_ref, pair_edge_ref, other_edge_ref, first_ref,
    normed_ref, proj_ref, mixed_ref, earlier_ref, in_ref, out_ref, gains_ref, taps_ref,
    column, taps_column,
):
    slot = pl.program_id(0)
    width = in_ref.shape[1]
    channels = width // 3
    rows = channels // PLANE

    @pl.when(slot == 0)
    def _():
        for plane in range(PLANE):
            for z in range(2):
                at = pl.ds((z * PLANE + plane) * 2 * rows, 2 * rows)
                source = pl.ds(z * 2 * rows, 2 * rows)
                in_ref[at, :] = first_ref[plane, source, :width]
                column[at, :] = first_ref[plane, source, width + channels :].astype(jnp.float32)
            at = pl.ds(plane * rows, rows)
            for part in range(4):
                out_ref[at, part * channels : (part + 1) * channels] = first_ref[
                    plane, pl.ds(part * rows, rows), width : width + channels
                ]
            taps_column[at, :] = first_ref[plane, :rows, width + channels :].astype(jnp.float32)
        gains_ref[...] = column[...].T[:8]
        taps_ref[...] = taps_column[...].T[:8]

    def project(values):
        values = values.astype(jnp.float32)
        normed = (values * norm_scale(values) * gains_ref[0:1]).astype(jnp.bfloat16)
        projected = jnp.dot(normed, in_ref[...], preferred_element_type=jnp.float32)
        mixed = (projected[:, :channels] * projected[:, 2 * channels :]).astype(jnp.bfloat16)
        return normed, projected, mixed

    normed_ref[0], proj_ref[0], mixed_ref[0] = project(pick(slot, pair_ref[0, 0], other_ref[0, 0]))
    edge = project(pick(slot, pair_edge_ref[0, 0], other_edge_ref[0, 0]))[2]
    earlier_ref[0] = edge.astype(jnp.float32)


def branch_kernel(
    mixed_ref, earlier_ref, out_gate_ref, taps_ref, out_ref,
    convolved_ref, gated_ref, keep_ref, sent_ref,
):
    slot = pl.program_id(0)
    mixed = mixed_ref[0].astype(jnp.float32)
    earlier = earlier_ref[0]
    convolved = (
        taps_ref[2:3] * mixed
        + taps_ref[3:4] * shifted_in(mixed, earlier, 1)
        + taps_ref[4:5] * shifted_in(mixed, earlier, 2)
    )
    convolved_ref[0] = convolved
    gated = (out_gate_ref[0] * convolved).astype(jnp.bfloat16)
    gated_ref[0] = gated
    branch = jnp.dot(gated, out_ref[...], preferred_element_type=jnp.float32)
    store_pair(slot, branch, keep_ref, sent_ref)


def ff_kernel(
    own_ref, swap_ref, pair_ref, other_ref, weights_ref, down_ref,
    hidden_ref, grad_gate_ref, grad_up_ref, keep_ref, sent_ref,
):
    slot = pl.program_id(0)
    units = down_ref.shape[0]
    normed = pick(slot, own_ref[0], swap_ref[0])
    outer = pick(slot, pair_ref[0, 0], other_ref[0, 0])
    for start in range(0, units, CHUNK):
        lanes = slice(start, min(start + CHUNK, units))
        up_lanes = slice(units + lanes.start, units + lanes.stop)
        gate = jnp.dot(normed, weights_ref[:, lanes], preferred_element_type=jnp.float32)
        up = jnp.dot(normed, weights_ref[:, up_lanes], preferred_element_type=jnp.float32)
        grad = contract_cols(outer, down_ref[lanes, :])
        sigmoid = jax.nn.sigmoid(gate)
        silu = gate * sigmoid
        hidden_ref[0, :, lanes] = (silu * up).astype(jnp.bfloat16)
        grad_gate = grad * up * sigmoid * (1.0 + gate * (1.0 - sigmoid))
        grad_gate_ref[0, :, lanes] = grad_gate.astype(jnp.bfloat16)
        grad_up_ref[0, :, lanes] = (grad * silu).astype(jnp.bfloat16)
    term = contract_cols(grad_gate_ref[0], weights_ref[:, :units])
    term += contract_cols(grad_up_ref[0], weights_ref[:, units : 2 * units])
    store_pair(slot, term, keep_ref, sent_ref)


def ff_grads_kernel(
    own_ref, swap_ref, pair_ref, other_ref, hidden_ref, grad_gate_ref, grad_up_ref,
    pack_ref,
    gate_total, up_total, down_total,
):
    slot = pl.program_id(0)
    width, units = gate_total.shape
    each = units // PLANE
    block = width // PLANE
    rest = each - block
    normed = pick(slot, own_ref[0], swap_ref[0])
    outer = pick(slot, pair_ref[0, 0], other_ref[0, 0])

    @pl.when(slot == 0)
    def _():
        gate_total[...] = jnp.zeros_like(gate_total)
        up_total[...] = jnp.zeros_like(up_total)
        down_total[...] = jnp.zeros_like(down_total)

    gate_total[...] += contract_rows(normed, grad_gate_ref[0])
    up_total[...] += contract_rows(normed, grad_up_ref[0])
    down_total[...] += contract_rows(hidden_ref[0], outer)

    @pl.when(slot == 3)
    def _():
        pack_ref[:, :units] = gate_total[...].astype(jnp.bfloat16)
        pack_ref[:, units : 2 * units] = up_total[...].astype(jnp.bfloat16)
        for plane in range(PLANE):
            start = plane * each
            for half in range(2):
                to = half * width // 2 + plane * block // 2
                pack_ref[to : to + block // 2, 2 * units : 2 * units + width] = down_total[
                    start + half * block // 2 : start + (half + 1) * block // 2
                ].astype(jnp.bfloat16)
                parts = block // rest // 2
                lanes = width * rest // block
                last = down_total[start + block : start + each]
                pieces = [
                    last[:, (half * parts + part) * lanes : (half * parts + part + 1) * lanes]
                    for part in range(parts)
                ]
                pack_ref[to : to + block // 2, 2 * units + width :] = jnp.concatenate(
                    pieces, 0
                ).astype(jnp.bfloat16)


def gated_back_kernel(
    own_ref, swap_ref, out_ref, convolved_ref, out_gate_ref, grad_out_ref, grad_conv_ref
):
    slot = pl.program_id(0)
    grad_gated = contract_cols(pick(slot, own_ref[0], swap_ref[0]), out_ref[...])
    grad_out_ref[0] = (grad_gated * convolved_ref[0]).astype(jnp.bfloat16)
    grad_conv_ref[0] = grad_gated * out_gate_ref[0]


def out_grads_kernel(
    own_ref, swap_ref, gated_ref, grad_conv_ref, mixed_ref, earlier_ref, gain_ref,
    part_ref, spare_ref,
    total, taps_rows, gain_rows,
):
    slot = pl.program_id(0)
    rows = spare_ref.shape[1] // 4
    channels = gated_ref.shape[2]

    @pl.when(slot == 0)
    def _():
        total[...] = jnp.zeros_like(total)
        taps_rows[...] = jnp.zeros_like(taps_rows)
        gain_rows[...] = jnp.zeros_like(gain_rows)
        gain_rows[1:2] = gain_ref[...]

    total[...] += contract_rows(gated_ref[0], pick(slot, own_ref[0], swap_ref[0]))
    grad_conv = grad_conv_ref[0]
    mixed = mixed_ref[0].astype(jnp.float32)
    earlier = earlier_ref[0]
    lagged = (mixed, shifted_in(mixed, earlier, 1), shifted_in(mixed, earlier, 2))
    for lag, value in enumerate(lagged):
        taps_rows[2 + lag : 3 + lag] += jnp.sum(grad_conv * value, axis=0, keepdims=True)

    @pl.when(slot == 3)
    def _():
        gain_column = gain_rows[...].T
        taps_column = taps_rows[...].T
        for plane in range(PLANE):
            at = slice(plane * rows, (plane + 1) * rows)
            for part in range(4):
                part_ref[plane, part * rows : (part + 1) * rows, :] = total[
                    at, part * channels : (part + 1) * channels
                ].astype(jnp.bfloat16)
            for z in range(2):
                start = (z * PLANE + plane) * 2 * rows
                spare_ref[plane, z * 2 * rows : (z + 1) * 2 * rows, :] = gain_column[
                    start : start + 2 * rows
                ]
            spare_ref[plane, :rows, :] += taps_column[at]


def project_back_kernel(
    grad_conv_ref, later_ref, proj_ref, grad_out_ref, normed_ref, in_ref, taps_ref,
    pair_ref, other_ref, part_ref, spare_ref,
    pack_ref, keep_ref, sent_ref,
    total, gain_rows,
):
    slot = pl.program_id(0)
    width = in_ref.shape[1]
    channels = width // 3
    rows = channels // PLANE

    @pl.when(slot == 0)
    def _():
        total[...] = jnp.zeros_like(total)
        gain_rows[...] = jnp.zeros_like(gain_rows)

    grad_conv, later = grad_conv_ref[0], later_ref[0]
    grad_mixed = (
        taps_ref[2:3] * grad_conv
        + taps_ref[3:4] * shifted_out(grad_conv, later, 1)
        + taps_ref[4:5] * shifted_out(grad_conv, later, 2)
    )
    grad_projected = jnp.concatenate(
        [
            (grad_mixed * proj_ref[0, :, 2 * channels :]).astype(jnp.bfloat16),
            grad_out_ref[0],
            (grad_mixed * proj_ref[0, :, :channels]).astype(jnp.bfloat16),
        ],
        1,
    )
    total[...] += contract_rows(normed_ref[0], grad_projected)
    grad_normed = contract_cols(grad_projected, in_ref[...])
    store_pair(slot, grad_normed, keep_ref, sent_ref)
    values = pick(slot, pair_ref[0, 0], other_ref[0, 0]).astype(jnp.float32)
    gain_rows[0:1] += jnp.sum(grad_normed * values * norm_scale(values), axis=0, keepdims=True)

    @pl.when(slot == 3)
    def _():
        gain_column = gain_rows[...].T
        for plane in range(PLANE):
            for z in range(2):
                start = (z * PLANE + plane) * 2 * rows
                to = slice(z * 2 * rows, (z + 1) * 2 * rows)
                pack_ref[plane, to, :width] = total[start : start + 2 * rows].astype(jnp.bfloat16)
                pack_ref[plane, to, width + channels :] = (
                    spare_ref[plane, to] + gain_column[start : start + 2 * rows]
                ).astype(jnp.bfloat16)
            pack_ref[plane, :, width : width + channels] = part_ref[plane]


def in_total_kernel(blocks_ref, total_ref, spare_ref):
    members, rows, width = blocks_ref.shape
    channels = total_ref.shape[1] // 12
    first = width - SPARE - 3 * channels
    unit = channels // PLANE
    source = lax.broadcasted_iota(jnp.int32, (channels, 2 * channels), 0)
    target = lax.broadcasted_iota(jnp.int32, (channels, 2 * channels), 1)
    for z in range(2):
        for part in range(3):
            total = jnp.zeros((rows, 2 * channels), jnp.float32)
            for core in range(2):
                placed = source // unit * (2 * unit) + core * unit + source % unit == target
                placed = placed.astype(jnp.float32).astype(jnp.bfloat16)
                for rep in range(2):
                    block = blocks_ref[rep * 4 + z * 2 + core]
                    total += jnp.dot(
                        block[:, first + part * channels : first + (part + 1) * channels],
                        placed,
                        preferred_element_type=jnp.float32,
                    )
            start = (part * 2 + z) * 2 * channels
            total_ref[:, start : start + 2 * channels] = total
    spare = jnp.zeros((rows, SPARE), jnp.float32)
    for member in range(members):
        spare += blocks_ref[member, :, width - SPARE :].astype(jnp.float32)
    spare_ref[...] = spare


def body(
    tokens, gain_first, w_in, conv_weight, w_out, gain_second, w_gate, w_up, w_down, cotangent
):
    low, wide = jnp.bfloat16, jnp.float32
    length, model_width = tokens.shape
    position = lax.axis_index("fsdp")
    core, plane, z = position % 2, position // 2 % PLANE, position // HALF
    rows = w_in.shape[0]
    channels = model_width // 4

    block = 4 * rows
    rest = w_down.shape[0] - block
    units = w_down.shape[0] * PLANE
    gains = jnp.pad(jnp.stack([gain_first, gain_second], 1), ((0, 0), (0, SPARE - 2)))
    gains = jnp.broadcast_to(gains, (4, rows, SPARE))
    swapped = team_swap(
        jnp.concatenate(
            [by_member(w_gate, 1), by_member(w_up, 1), by_member(w_in, 3), gains], 2
        )
    )
    down_main = w_down[:block].reshape(4, rows, model_width)
    down_rest = w_down[block:].reshape(rest, block // rest, -1).transpose(1, 0, 2)
    ff_all = gather_rows(
        jnp.concatenate(
            [swapped[:, :, : 2 * units], down_main, down_rest.reshape(4, rows, -1)], 2
        )
    )

    in_width = 3 * channels
    conv_lanes = jnp.pad(conv_weight, ((0, 0), (2, SPARE - 5)))
    first_pack = jnp.concatenate(
        [
            swapped[:, :, 2 * units : 2 * units + in_width],
            w_out.reshape(rows, 4, channels).transpose(1, 0, 2),
            swapped[:, :, 2 * units + in_width :] + conv_lanes,
        ],
        2,
    )
    first_all = plane_swap(jnp.broadcast_to(first_pack, (PLANE,) + first_pack.shape))
    first_all = first_all.reshape(PLANE, 4 * rows, -1)

    main_rows = ff_all[:, 2 * units : 2 * units + model_width].reshape(2, PLANE, 2 * rows, -1)
    main_rows = main_rows.transpose(1, 0, 2, 3).reshape(PLANE, block, model_width)
    rest_rows = ff_all[:, 2 * units + model_width :].reshape(2, PLANE, 2 * rows, -1)
    rest_rows = rest_rows.transpose(1, 0, 2, 3).reshape(PLANE, block // rest, rest, -1)
    rest_rows = rest_rows.transpose(0, 2, 1, 3).reshape(PLANE, rest, model_width)
    down_full = jnp.concatenate([main_rows, rest_rows], 1).reshape(units, model_width)

    before = lax.ppermute(tokens[length - EDGE :], "fsdp", TO_FOLLOWING)
    pair = jnp.stack(
        [
            jnp.concatenate([tokens, before], 0),
            jnp.concatenate([cotangent, jnp.zeros_like(before)], 0),
        ]
    )
    pair = jnp.stack([pair, to_z(pair)])
    other = to_core(pair)
    team_pairs = [pair_of_values(length, model_width, 0)] * 2
    slot_wide, slot_narrow = (4, length, model_width), (4, length, channels)
    pair_wide = (2, length, model_width)
    pairs = [per_pair(length, model_width)] * 2
    narrow = per_slot(length, channels)
    out_gate = per_slot(length, channels, 1)
    edge, edge_after = per_slot(EDGE, channels), per_slot(8, channels)
    team_edges = [
        pl.BlockSpec((1, 1, EDGE, model_width), lambda slot: (slot // 2, 0, length // EDGE, 0))
    ] * 2
    out_matrix, in_matrix = whole(channels, model_width), whole(model_width, in_width)
    taps = whole(8, channels)

    normed, projected, mixed, earlier, in_full, out_full, gains, kernel = run(
        project_kernel,
        (4,),
        team_pairs + team_edges + [whole(*first_all.shape)],
        [
            per_slot(length, model_width),
            per_slot(length, in_width),
            narrow,
            edge,
            in_matrix,
            out_matrix,
            whole(8, model_width),
            taps,
        ],
        [
            array(slot_wide, low),
            array((4, length, in_width), wide),
            array(slot_narrow, low),
            array((4, EDGE, channels), wide),
            array((model_width, in_width), low),
            array((channels, model_width), low),
            array((8, model_width), wide),
            array((8, channels), wide),
        ],
        [pltpu.VMEM((model_width, SPARE), wide), pltpu.VMEM((channels, SPARE), wide)],
        24,
        7.5,
        [pair, other, pair, other, first_all],
    )
    gain_one, gain_two = gains[0], gains[1]

    def by_core(first, second):
        return jnp.where(core == 0, first, second)

    convolved, gated, branch_keep, branch_sent = run(
        branch_kernel,
        (4,),
        [narrow, edge, out_gate, taps, out_matrix],
        [narrow, narrow] + pairs,
        [
            array(slot_narrow, wide),
            array(slot_narrow, low),
            array(pair_wide, wide),
            array(pair_wide, low),
        ],
        [],
        16,
        5.5,
        [mixed, earlier, projected, kernel, out_full],
    )
    branch_pair = core_sum(branch_keep, branch_sent)
    branch_other = to_z(branch_pair.astype(low))
    branch_other, down_full = lax.optimization_barrier((branch_other, down_full))
    inputs = pair[:, 0, :length].astype(wide)
    middle = inputs + branch_pair + branch_other.astype(wide)[::-1]
    scale_two = norm_scale(middle)
    normed_two = (middle * scale_two * gain_two).astype(low)
    normed_swap = to_core(normed_two)

    outer_pairs = [pair_of_values(length, model_width, 1)] * 2
    unit_slot = per_slot(length, units)
    unit_shape = array((4, length, units), low)
    hidden, grad_gate, grad_upper, grad_keep, grad_sent = run(
        ff_kernel,
        (4,),
        pairs
        + outer_pairs
        + [whole(*ff_all.shape), whole(units, model_width)],
        [unit_slot] * 3 + pairs,
        [unit_shape] * 3 + [array(pair_wide, wide), array(pair_wide, low)],
        [],
        40,
        21,
        [normed_two, normed_swap, pair, other, ff_all, down_full],
    )
    grad_pair = core_sum(grad_keep, grad_sent)
    grad_sent = grad_pair.astype(low)
    grad_other = to_z(grad_sent)

    grad_sent, hidden, grad_gate, grad_upper = lax.optimization_barrier(
        (grad_sent, hidden, grad_gate, grad_upper)
    )
    (ff_grads,) = run(
        ff_grads_kernel,
        (4,),
        pairs + outer_pairs + [unit_slot] * 3,
        [whole(*ff_all.shape)],
        [array(ff_all.shape, low)],
        [
            pltpu.VMEM((model_width, units), wide),
            pltpu.VMEM((model_width, units), wide),
            pltpu.VMEM((units, model_width), wide),
        ],
        44,
        16,
        [normed_two, normed_swap, pair, other, hidden, grad_gate, grad_upper],
    )
    ff_share = scatter_rows(ff_grads)
    down_term = jnp.dot(
        hidden.reshape(4 * length, units), down_full, preferred_element_type=wide
    ).reshape(4, length, model_width)
    grad_other, ff_grads, down_term = lax.optimization_barrier((grad_other, ff_grads, down_term))
    grad_normed_two = grad_pair + grad_other.astype(wide)[::-1]
    grad_gain_two = jnp.sum(grad_normed_two[0] * middle[0] * scale_two[0], axis=0)
    outer = pair[:, 1, :length].astype(wide)
    grad_middle = outer + norm_back(grad_normed_two * gain_two, middle, scale_two)
    grad_branch = grad_middle.astype(low)
    grad_swap = to_core(grad_branch)

    grad_out, grad_conv = run(
        gated_back_kernel,
        (4,),
        pairs + [out_matrix, narrow, out_gate],
        [narrow, narrow],
        [array(slot_narrow, low), array(slot_narrow, wide)],
        [],
        16,
        5,
        [grad_branch, grad_swap, out_full, convolved, projected],
    )
    heads = grad_conv[:, :2]
    sent = by_core(heads[0::2], heads[1::2])
    received = lax.ppermute(sent, "fsdp", TO_PREVIOUS)
    nothing = jnp.zeros_like(received[0])
    shifted = jnp.where(
        z == 0, jnp.stack([received[1], nothing]), jnp.stack([nothing, received[0]])
    )
    after = jnp.where(plane == PLANE - 1, shifted, received)
    own_after = by_core(heads[1::2], after)
    other_after = by_core(after, heads[0::2])
    later = jnp.stack([own_after[0], other_after[0], own_after[1], other_after[1]])
    later = jnp.pad(later, ((0, 0), (0, 6), (0, 0)))
    part_shape, spare_shape = (PLANE, 4 * rows, channels), (PLANE, 4 * rows, SPARE)
    out_part, spare_part = run(
        out_grads_kernel,
        (4,),
        pairs + [narrow, narrow, narrow, edge, whole(1, model_width)],
        [whole(*part_shape), whole(*spare_shape)],
        [array(part_shape, low), array(spare_shape, wide)],
        [
            pltpu.VMEM((channels, model_width), wide),
            pltpu.VMEM((SPARE, channels), wide),
            pltpu.VMEM((SPARE, model_width), wide),
        ],
        20,
        5.3,
        [grad_branch, grad_swap, gated, grad_conv, mixed, earlier, grad_gain_two[None]],
    )
    first_grads, normed_keep, normed_sent = run(
        project_back_kernel,
        (4,),
        [
            narrow,
            edge_after,
            per_slot(length, in_width),
            narrow,
            per_slot(length, model_width),
            in_matrix,
            taps,
        ]
        + team_pairs
        + [whole(*part_shape), whole(*spare_shape)],
        [whole(*first_all.shape)] + pairs,
        [array(first_all.shape, low), array(pair_wide, wide), array(pair_wide, low)],
        [pltpu.VMEM((model_width, in_width), wide), pltpu.VMEM((SPARE, model_width), wide)],
        32,
        12,
        [
            grad_conv,
            later,
            projected,
            grad_out,
            normed,
            in_full,
            kernel,
            pair,
            other,
            out_part,
            spare_part,
        ],
    )
    first_grads = first_grads.reshape(PLANE, 4, rows, -1)
    first_arrived = plane_swap(first_grads)

    down_term, normed_sent = lax.optimization_barrier((down_term, normed_sent))
    result = middle[0] + own_sum(down_term[0::2], down_term[1::2].astype(low))
    grad_normed_own = own_sum(normed_keep, normed_sent)
    grad_inputs = grad_middle[0] + norm_back(
        grad_normed_own * gain_one, inputs[0], norm_scale(inputs[0])
    )
    result, grad_inputs, first_arrived = lax.optimization_barrier(
        (result.astype(low), grad_inputs, first_arrived)
    )
    first_share = jnp.sum(first_arrived.astype(wide), axis=0).astype(low)

    def both_reps(value):
        other = lax.ppermute(value, "rep", [(0, 1), (1, 0)])
        return value.astype(wide) + other.astype(wide)

    blocks = jnp.concatenate(
        [
            ff_share[:, :, : 2 * units],
            first_share[:, :, :in_width],
            first_share[:, :, in_width + channels :],
        ],
        2,
    )
    blocks = lax.all_to_all(
        jnp.concatenate([blocks, blocks]),
        ("rep", "fsdp"),
        0,
        0,
        tiled=True,
        axis_index_groups=BOTH_TEAMS,
    )
    owned = jnp.concatenate([ff_share[:, :, 2 * units :], first_share[:, :, in_width:]], 2)
    owned, blocks = lax.optimization_barrier((owned, blocks))
    owned = both_reps(owned)
    down_total, out_total = owned[:, :, : model_width + SPARE], owned[:, :, model_width + SPARE :]
    down_rest = down_total[:, :, model_width:].reshape(block // rest, rest, -1)
    down_rest = down_rest.transpose(1, 0, 2).reshape(rest, model_width)
    down_total = jnp.concatenate(
        [down_total[:, :, :model_width].reshape(block, model_width), down_rest], 0
    )
    conv_total = out_total[0, :, channels + 2 : channels + 5]
    out_total = out_total[:, :, :channels].transpose(1, 0, 2).reshape(rows, model_width)
    in_total, gain_total = run(
        in_total_kernel,
        (1,),
        [whole(*blocks.shape)],
        [whole(rows, w_in.shape[1]), whole(rows, SPARE)],
        [array((rows, w_in.shape[1]), wide), array((rows, SPARE), wide)],
        [],
        16,
        3,
        [blocks],
    )
    ff_total = blocks[:, :, : 2 * units].astype(wide)
    ff_total = ff_total[:4] + ff_total[4:]

    return (
        result,
        grad_inputs,
        gain_total[:, 0],
        in_total,
        conv_total,
        out_total,
        gain_total[:, 1],
        from_members(ff_total[:, :, :units], 1),
        from_members(ff_total[:, :, units:], 1),
        down_total,
    )


def solution(mesh):
    return jax.shard_map(
        body,
        mesh=mesh,
        in_specs=(
            P(("rep", "fsdp"), None),
            P("fsdp"),
            P("fsdp", None),
            P("fsdp", None),
            P("fsdp", None),
            P("fsdp"),
            P("fsdp", None),
            P("fsdp", None),
            P("fsdp", None),
            P(("rep", "fsdp"), None),
        ),
        out_specs=(
            P(("rep", "fsdp"), None),
            P(("rep", "fsdp"), None),
            P("fsdp"),
            P("fsdp", None),
            P("fsdp", None),
            P("fsdp", None),
            P("fsdp"),
            P("fsdp", None),
            P("fsdp", None),
            P("fsdp", None),
        ),
        check_vma=False,
    )
```

```python
import jax
import jax.numpy as jnp
from jax import lax
from jax.experimental import pallas as pl
from jax.experimental.pallas import tpu as pltpu
from jax.sharding import PartitionSpec as P

epsilon = 1e-05

SIDE = 4
PLANE = SIDE * SIDE
HALF = PLANE * 2
SPARE = 128
EDGE = 16
CHUNK = 256
MIB = 1024 * 1024


def place(z, plane, core):
    return (z * PLANE + plane) * 2 + core


def moves(target):
    return [
        (place(z, plane, core), place(*target(z, plane, core)))
        for z in range(2)
        for plane in range(PLANE)
        for core in range(2)
    ]


TO_CORE = moves(lambda z, plane, core: (z, plane, 1 - core))
TO_Z = moves(lambda z, plane, core: (1 - z, plane, core))
TO_BOTH = moves(lambda z, plane, core: (1 - z, plane, 1 - core))
TO_FOLLOWING = [(index, index + 1) for index in range(2 * HALF - 1)]
TO_PREVIOUS = moves(lambda z, plane, core: (z, (plane - 1) % PLANE, core))
TEAMS = [
    [place(z, plane, core) for z in range(2) for core in range(2)] for plane in range(PLANE)
]
PLANES = [
    [place(z, plane, core) for plane in range(PLANE)] for z in range(2) for core in range(2)
]
BOTH_TEAMS = [[rep * 2 * HALF + member for rep in range(2) for member in team] for team in TEAMS]


def to_core(value):
    return lax.ppermute(value, "fsdp", TO_CORE)


def to_z(value):
    return lax.ppermute(value, "fsdp", TO_Z)


def to_both(value):
    return lax.ppermute(value, "fsdp", TO_BOTH)


def norm_scale(values):
    return lax.rsqrt(jnp.mean(values * values, axis=-1, keepdims=True) + epsilon)


def norm_back(grad_normed, values, scale):
    inner = jnp.mean(grad_normed * values, axis=-1, keepdims=True)
    return scale * (grad_normed - values * scale * scale * inner)


def contract_rows(left, right):
    return lax.dot_general(
        left, right, (((0,), (0,)), ((), ())), preferred_element_type=jnp.float32
    )


def contract_cols(left, right):
    return lax.dot_general(
        left, right, (((1,), (1,)), ((), ())), preferred_element_type=jnp.float32
    )


def by_member(shard, parts):
    rows, columns = shard.shape
    split = shard.reshape(rows, parts, 2, PLANE, 2, -1)
    return split.transpose(2, 4, 0, 1, 3, 5).reshape(4, rows, columns // 4)


def from_members(blocks, parts):
    members, rows, columns = blocks.shape
    split = blocks.reshape(2, 2, rows, parts, PLANE, -1)
    return split.transpose(2, 3, 0, 4, 1, 5).reshape(rows, 4 * columns)


def team_swap(blocks):
    return lax.all_to_all(blocks, "fsdp", 0, 0, tiled=True, axis_index_groups=TEAMS)


def plane_swap(blocks):
    return lax.all_to_all(blocks, "fsdp", 0, 0, tiled=True, axis_index_groups=PLANES)


def gather_rows(blocks):
    members, rows, columns = blocks.shape
    return lax.all_gather(
        blocks.reshape(2, 2 * rows, columns),
        "fsdp",
        axis=1,
        tiled=True,
        axis_index_groups=PLANES,
    ).reshape(-1, columns)


def scatter_rows(value):
    total, columns = value.shape
    return lax.psum_scatter(
        value.reshape(2, total // 2, columns),
        "fsdp",
        scatter_dimension=1,
        tiled=True,
        axis_index_groups=PLANES,
    ).reshape(4, -1, columns)


def core_sum(keep, sent):
    return keep + to_core(sent).astype(jnp.float32)


def own_sum(keep, sent):
    pair = core_sum(keep, sent)
    return pair[0] + to_z(pair[1].astype(jnp.bfloat16)).astype(jnp.float32)


def whole(*shape):
    return pl.BlockSpec(shape, lambda *_: (0,) * len(shape))


def per_slot(length, width, column=0):
    return pl.BlockSpec((1, length, width), lambda slot: (slot, 0, column))


def per_pair(length, width):
    return pl.BlockSpec((1, length, width), lambda slot: (slot // 2, 0, 0))


def run(kernel, grid, in_specs, out_specs, out_shape, scratch, room, busy, values):
    return pl.pallas_call(
        kernel,
        grid=grid,
        in_specs=in_specs,
        out_specs=out_specs,
        out_shape=out_shape,
        scratch_shapes=scratch,
        compiler_params=pltpu.CompilerParams(vmem_limit_bytes=room * MIB),
        cost_estimate=pl.CostEstimate(
            flops=int(busy * 1.15e9), bytes_accessed=0, transcendentals=0
        ),
    )(*values)


def array(shape, kind):
    return jax.ShapeDtypeStruct(shape, kind)


def pick(slot, even, odd):
    return jnp.where(slot % 2 == 0, even, odd)


def pick_slot(slot, *values):
    picked = values[0]
    for index in range(1, 4):
        picked = jnp.where(slot == index, values[index], picked)
    return picked


def shifted_in(values, rows_before, steps):
    moved = pltpu.roll(values, steps, 0)
    row = lax.broadcasted_iota(jnp.int32, values.shape, 0)
    for index in range(steps):
        at = EDGE - steps + index
        moved = jnp.where(row == index, rows_before[at : at + 1], moved)
    return moved


def shifted_out(values, next_rows, steps):
    length = values.shape[0]
    moved = pltpu.roll(values, length - steps, 0)
    row = lax.broadcasted_iota(jnp.int32, values.shape, 0)
    for index in range(steps):
        moved = jnp.where(row == length - steps + index, next_rows[index : index + 1], moved)
    return moved


def store_pair(slot, value, keep_ref, sent_ref):
    @pl.when(slot % 2 == 0)
    def _():
        keep_ref[0] = value

    @pl.when(slot % 2 == 1)
    def _():
        sent_ref[0] = value.astype(sent_ref.dtype)


def project_kernel(
    slot0_ref, slot1_ref, slot2_ref, slot3_ref, first_ref,
    normed_ref, proj_ref, mixed_ref, earlier_ref, in_ref, out_ref, gains_ref, taps_ref,
    column, taps_column,
):
    slot = pl.program_id(0)
    width = in_ref.shape[1]
    channels = width // 3
    rows = channels // PLANE

    @pl.when(slot == 0)
    def _():
        for plane in range(PLANE):
            for z in range(2):
                at = pl.ds((z * PLANE + plane) * 2 * rows, 2 * rows)
                source = pl.ds(z * 2 * rows, 2 * rows)
                in_ref[at, :] = first_ref[plane, source, :width]
                column[at, :] = first_ref[plane, source, width + channels :].astype(jnp.float32)
            at = pl.ds(plane * rows, rows)
            for part in range(4):
                out_ref[at, part * channels : (part + 1) * channels] = first_ref[
                    plane, pl.ds(part * rows, rows), width : width + channels
                ]
            taps_column[at, :] = first_ref[plane, :rows, width + channels :].astype(jnp.float32)
        gains_ref[...] = column[...].T[:8]
        taps_ref[...] = taps_column[...].T[:8]

    def project(values):
        values = values.astype(jnp.float32)
        normed = (values * norm_scale(values) * gains_ref[0:1]).astype(jnp.bfloat16)
        projected = jnp.dot(normed, in_ref[...], preferred_element_type=jnp.float32)
        mixed = (projected[:, :channels] * projected[:, 2 * channels :]).astype(jnp.bfloat16)
        return normed, projected, mixed

    values = pick_slot(slot, slot0_ref[...], slot1_ref[...], slot2_ref[...], slot3_ref[...])
    length = normed_ref.shape[1]
    normed_ref[0], proj_ref[0], mixed_ref[0] = project(values[:length])
    edge = project(values[length:])[2]
    earlier_ref[0] = edge.astype(jnp.float32)


def branch_kernel(
    mixed_ref, earlier_ref, out_gate_ref, taps_ref, out_ref,
    convolved_ref, gated_ref, keep_ref, sent_ref,
):
    slot = pl.program_id(0)
    mixed = mixed_ref[0].astype(jnp.float32)
    earlier = earlier_ref[0]
    convolved = (
        taps_ref[2:3] * mixed
        + taps_ref[3:4] * shifted_in(mixed, earlier, 1)
        + taps_ref[4:5] * shifted_in(mixed, earlier, 2)
    )
    convolved_ref[0] = convolved
    gated = (out_gate_ref[0] * convolved).astype(jnp.bfloat16)
    gated_ref[0] = gated
    branch = jnp.dot(gated, out_ref[...], preferred_element_type=jnp.float32)
    store_pair(slot, branch, keep_ref, sent_ref)


def middle_kernel(
    own_ref, far_ref, branch_ref, crossed_ref, gains_ref, middle_ref, normed_ref
):
    inputs = jnp.where(pl.program_id(0) == 0, own_ref[...], far_ref[...])
    middle = inputs[: branch_ref.shape[1]].astype(jnp.float32) + branch_ref[0]
    middle += crossed_ref[0].astype(jnp.float32)
    middle_ref[0] = middle
    normed_ref[0] = (middle * norm_scale(middle) * gains_ref[1:2]).astype(jnp.bfloat16)


def grad_middle_kernel(
    grad_ref, crossed_ref, middle_ref, outer_ref, gains_ref,
    grad_middle_ref, branch_ref, gain_ref,
):
    grad_normed = grad_ref[0] + crossed_ref[0].astype(jnp.float32)
    middle = middle_ref[0]
    scale = norm_scale(middle)

    @pl.when(pl.program_id(0) == 0)
    def _():
        gain_ref[...] = jnp.sum(grad_normed * middle * scale, axis=0, keepdims=True)

    grad_middle = norm_back(grad_normed * gains_ref[1:2], middle, scale)
    grad_middle += outer_ref[0].astype(jnp.float32)
    grad_middle_ref[0] = grad_middle
    branch_ref[0] = grad_middle.astype(jnp.bfloat16)


def ff_kernel(
    own_ref, swap_ref, pair_ref, other_ref, weights_ref, down_ref,
    hidden_ref, grad_gate_ref, grad_up_ref, keep_ref, sent_ref,
):
    slot = pl.program_id(0)
    units = down_ref.shape[0]
    normed = pick(slot, own_ref[0], swap_ref[0])
    outer = pick(slot, pair_ref[0], other_ref[0])
    for start in range(0, units, CHUNK):
        lanes = slice(start, min(start + CHUNK, units))
        up_lanes = slice(units + lanes.start, units + lanes.stop)
        gate = jnp.dot(normed, weights_ref[:, lanes], preferred_element_type=jnp.float32)
        up = jnp.dot(normed, weights_ref[:, up_lanes], preferred_element_type=jnp.float32)
        grad = contract_cols(outer, down_ref[lanes, :])
        sigmoid = jax.nn.sigmoid(gate)
        silu = gate * sigmoid
        hidden_ref[0, :, lanes] = (silu * up).astype(jnp.bfloat16)
        grad_gate = grad * up * sigmoid * (1.0 + gate * (1.0 - sigmoid))
        grad_gate_ref[0, :, lanes] = grad_gate.astype(jnp.bfloat16)
        grad_up_ref[0, :, lanes] = (grad * silu).astype(jnp.bfloat16)
    term = contract_cols(grad_gate_ref[0], weights_ref[:, :units])
    term += contract_cols(grad_up_ref[0], weights_ref[:, units : 2 * units])
    store_pair(slot, term, keep_ref, sent_ref)


def ff_grads_kernel(
    own_ref, swap_ref, pair_ref, other_ref, hidden_ref, grad_gate_ref, grad_up_ref,
    pack_ref,
    gate_total, up_total, down_total,
):
    slot = pl.program_id(0)
    width, units = gate_total.shape
    each = units // PLANE
    block = width // PLANE
    rest = each - block
    normed = pick(slot, own_ref[0], swap_ref[0])
    outer = pick(slot, pair_ref[0], other_ref[0])

    @pl.when(slot == 0)
    def _():
        gate_total[...] = jnp.zeros_like(gate_total)
        up_total[...] = jnp.zeros_like(up_total)
        down_total[...] = jnp.zeros_like(down_total)

    gate_total[...] += contract_rows(normed, grad_gate_ref[0])
    up_total[...] += contract_rows(normed, grad_up_ref[0])
    down_total[...] += contract_rows(hidden_ref[0], outer)

    @pl.when(slot == 3)
    def _():
        pack_ref[:, :units] = gate_total[...].astype(jnp.bfloat16)
        pack_ref[:, units : 2 * units] = up_total[...].astype(jnp.bfloat16)
        for plane in range(PLANE):
            start = plane * each
            for half in range(2):
                to = half * width // 2 + plane * block // 2
                pack_ref[to : to + block // 2, 2 * units : 2 * units + width] = down_total[
                    start + half * block // 2 : start + (half + 1) * block // 2
                ].astype(jnp.bfloat16)
                parts = block // rest // 2
                lanes = width * rest // block
                last = down_total[start + block : start + each]
                pieces = [
                    last[:, (half * parts + part) * lanes : (half * parts + part + 1) * lanes]
                    for part in range(parts)
                ]
                pack_ref[to : to + block // 2, 2 * units + width :] = jnp.concatenate(
                    pieces, 0
                ).astype(jnp.bfloat16)


def gated_back_kernel(
    own_ref, swap_ref, out_ref, convolved_ref, out_gate_ref, grad_out_ref, grad_conv_ref
):
    slot = pl.program_id(0)
    grad_gated = contract_cols(pick(slot, own_ref[0], swap_ref[0]), out_ref[...])
    grad_out_ref[0] = (grad_gated * convolved_ref[0]).astype(jnp.bfloat16)
    grad_conv_ref[0] = grad_gated * out_gate_ref[0]


def out_grads_kernel(
    own_ref, swap_ref, gated_ref, grad_conv_ref, mixed_ref, earlier_ref, gain_ref,
    part_ref, spare_ref,
    total, taps_rows, gain_rows,
):
    slot = pl.program_id(0)
    rows = spare_ref.shape[1] // 4
    channels = gated_ref.shape[2]

    @pl.when(slot == 0)
    def _():
        total[...] = jnp.zeros_like(total)
        taps_rows[...] = jnp.zeros_like(taps_rows)
        gain_rows[...] = jnp.zeros_like(gain_rows)
        gain_rows[1:2] = gain_ref[...]

    total[...] += contract_rows(gated_ref[0], pick(slot, own_ref[0], swap_ref[0]))
    grad_conv = grad_conv_ref[0]
    mixed = mixed_ref[0].astype(jnp.float32)
    earlier = earlier_ref[0]
    lagged = (mixed, shifted_in(mixed, earlier, 1), shifted_in(mixed, earlier, 2))
    for lag, value in enumerate(lagged):
        taps_rows[2 + lag : 3 + lag] += jnp.sum(grad_conv * value, axis=0, keepdims=True)

    @pl.when(slot == 3)
    def _():
        gain_column = gain_rows[...].T
        taps_column = taps_rows[...].T
        for plane in range(PLANE):
            at = slice(plane * rows, (plane + 1) * rows)
            for part in range(4):
                part_ref[plane, part * rows : (part + 1) * rows, :] = total[
                    at, part * channels : (part + 1) * channels
                ].astype(jnp.bfloat16)
            for z in range(2):
                start = (z * PLANE + plane) * 2 * rows
                spare_ref[plane, z * 2 * rows : (z + 1) * 2 * rows, :] = gain_column[
                    start : start + 2 * rows
                ]
            spare_ref[plane, :rows, :] += taps_column[at]


def project_back_kernel(
    grad_conv_ref, later_ref, proj_ref, grad_out_ref, normed_ref, in_ref, taps_ref,
    slot0_ref, slot1_ref, slot2_ref, slot3_ref, part_ref, spare_ref,
    pack_ref, keep_ref, sent_ref,
    total, gain_rows,
):
    slot = pl.program_id(0)
    width = in_ref.shape[1]
    channels = width // 3
    rows = channels // PLANE

    @pl.when(slot == 0)
    def _():
        total[...] = jnp.zeros_like(total)
        gain_rows[...] = jnp.zeros_like(gain_rows)

    grad_conv, later = grad_conv_ref[0], later_ref[0]
    grad_mixed = (
        taps_ref[2:3] * grad_conv
        + taps_ref[3:4] * shifted_out(grad_conv, later, 1)
        + taps_ref[4:5] * shifted_out(grad_conv, later, 2)
    )
    grad_projected = jnp.concatenate(
        [
            (grad_mixed * proj_ref[0, :, 2 * channels :]).astype(jnp.bfloat16),
            grad_out_ref[0],
            (grad_mixed * proj_ref[0, :, :channels]).astype(jnp.bfloat16),
        ],
        1,
    )
    total[...] += contract_rows(normed_ref[0], grad_projected)
    grad_normed = contract_cols(grad_projected, in_ref[...])
    store_pair(slot, grad_normed, keep_ref, sent_ref)
    values = pick_slot(slot, slot0_ref[...], slot1_ref[...], slot2_ref[...], slot3_ref[...])
    values = values[: grad_normed.shape[0]].astype(jnp.float32)
    gain_rows[0:1] += jnp.sum(grad_normed * values * norm_scale(values), axis=0, keepdims=True)

    @pl.when(slot == 3)
    def _():
        gain_column = gain_rows[...].T
        for plane in range(PLANE):
            for z in range(2):
                start = (z * PLANE + plane) * 2 * rows
                to = slice(z * 2 * rows, (z + 1) * 2 * rows)
                pack_ref[plane, to, :width] = total[start : start + 2 * rows].astype(jnp.bfloat16)
                pack_ref[plane, to, width + channels :] = (
                    spare_ref[plane, to] + gain_column[start : start + 2 * rows]
                ).astype(jnp.bfloat16)
            pack_ref[plane, :, width : width + channels] = part_ref[plane]


def in_total_kernel(blocks_ref, total_ref, spare_ref):
    members, rows, width = blocks_ref.shape
    channels = total_ref.shape[1] // 12
    first = width - SPARE - 3 * channels
    unit = channels // PLANE
    source = lax.broadcasted_iota(jnp.int32, (channels, 2 * channels), 0)
    target = lax.broadcasted_iota(jnp.int32, (channels, 2 * channels), 1)
    for z in range(2):
        for part in range(3):
            total = jnp.zeros((rows, 2 * channels), jnp.float32)
            for core in range(2):
                placed = source // unit * (2 * unit) + core * unit + source % unit == target
                placed = placed.astype(jnp.float32).astype(jnp.bfloat16)
                for rep in range(2):
                    block = blocks_ref[rep * 4 + z * 2 + core]
                    total += jnp.dot(
                        block[:, first + part * channels : first + (part + 1) * channels],
                        placed,
                        preferred_element_type=jnp.float32,
                    )
            start = (part * 2 + z) * 2 * channels
            total_ref[:, start : start + 2 * channels] = total
    spare = jnp.zeros((rows, SPARE), jnp.float32)
    for member in range(members):
        spare += blocks_ref[member, :, width - SPARE :].astype(jnp.float32)
    spare_ref[...] = spare


def body(
    tokens, gain_first, w_in, conv_weight, w_out, gain_second, w_gate, w_up, w_down, cotangent
):
    low, wide = jnp.bfloat16, jnp.float32
    length, model_width = tokens.shape
    position = lax.axis_index("fsdp")
    core, plane, z = position % 2, position // 2 % PLANE, position // HALF
    rows = w_in.shape[0]
    channels = model_width // 4

    before = lax.ppermute(tokens[length - EDGE :], "fsdp", TO_FOLLOWING)
    extended = jnp.concatenate([tokens, before], 0)
    slots = [extended, to_core(extended), to_z(extended), to_both(extended)]
    outer_z = to_z(cotangent)

    block = 4 * rows
    rest = w_down.shape[0] - block
    units = w_down.shape[0] * PLANE
    gains = jnp.pad(jnp.stack([gain_first, gain_second], 1), ((0, 0), (0, SPARE - 2)))
    gains = jnp.broadcast_to(gains, (4, rows, SPARE))
    swapped = team_swap(
        jnp.concatenate(
            [by_member(w_gate, 1), by_member(w_up, 1), by_member(w_in, 3), gains], 2
        )
    )
    down_main = w_down[:block].reshape(4, rows, model_width)
    down_rest = w_down[block:].reshape(rest, block // rest, -1).transpose(1, 0, 2)
    ff_all = gather_rows(
        jnp.concatenate(
            [swapped[:, :, : 2 * units], down_main, down_rest.reshape(4, rows, -1)], 2
        )
    )

    in_width = 3 * channels
    conv_lanes = jnp.pad(conv_weight, ((0, 0), (2, SPARE - 5)))
    first_pack = jnp.concatenate(
        [
            swapped[:, :, 2 * units : 2 * units + in_width],
            w_out.reshape(rows, 4, channels).transpose(1, 0, 2),
            swapped[:, :, 2 * units + in_width :] + conv_lanes,
        ],
        2,
    )
    first_all = plane_swap(jnp.broadcast_to(first_pack, (PLANE,) + first_pack.shape))
    first_all, slots, outer_z = lax.optimization_barrier((first_all, slots, outer_z))
    first_all = first_all.reshape(PLANE, 4 * rows, -1)

    main_rows = ff_all[:, 2 * units : 2 * units + model_width].reshape(2, PLANE, 2 * rows, -1)
    main_rows = main_rows.transpose(1, 0, 2, 3).reshape(PLANE, block, model_width)
    rest_rows = ff_all[:, 2 * units + model_width :].reshape(2, PLANE, 2 * rows, -1)
    rest_rows = rest_rows.transpose(1, 0, 2, 3).reshape(PLANE, block // rest, rest, -1)
    rest_rows = rest_rows.transpose(0, 2, 1, 3).reshape(PLANE, rest, model_width)
    down_full = jnp.concatenate([main_rows, rest_rows], 1).reshape(units, model_width)

    team_slots = [whole(length + EDGE, model_width)] * 4
    slot_wide, slot_narrow = (4, length, model_width), (4, length, channels)
    pair_wide = (2, length, model_width)
    pairs = [per_pair(length, model_width)] * 2
    narrow = per_slot(length, channels)
    out_gate = per_slot(length, channels, 1)
    edge, edge_after = per_slot(EDGE, channels), per_slot(8, channels)
    out_matrix, in_matrix = whole(channels, model_width), whole(model_width, in_width)
    taps = whole(8, channels)

    normed, projected, mixed, earlier, in_full, out_full, gains, kernel = run(
        project_kernel,
        (4,),
        team_slots + [whole(*first_all.shape)],
        [
            per_slot(length, model_width),
            per_slot(length, in_width),
            narrow,
            edge,
            in_matrix,
            out_matrix,
            whole(8, model_width),
            taps,
        ],
        [
            array(slot_wide, low),
            array((4, length, in_width), wide),
            array(slot_narrow, low),
            array((4, EDGE, channels), wide),
            array((model_width, in_width), low),
            array((channels, model_width), low),
            array((8, model_width), wide),
            array((8, channels), wide),
        ],
        [pltpu.VMEM((model_width, SPARE), wide), pltpu.VMEM((channels, SPARE), wide)],
        24,
        4,
        [*slots, first_all],
    )

    def by_core(first, second):
        return jnp.where(core == 0, first, second)

    convolved, gated, branch_keep, branch_sent = run(
        branch_kernel,
        (4,),
        [narrow, edge, out_gate, taps, out_matrix],
        [narrow, narrow] + pairs,
        [
            array(slot_narrow, wide),
            array(slot_narrow, low),
            array(pair_wide, wide),
            array(pair_wide, low),
        ],
        [],
        16,
        2,
        [mixed, earlier, projected, kernel, out_full],
    )
    branch_pair = core_sum(branch_keep, branch_sent)
    outer_pair = jnp.stack([cotangent, outer_z])
    outer_other = to_core(outer_pair)
    branch_other = to_z(branch_pair.astype(low))
    branch_other, down_full, outer_other = lax.optimization_barrier(
        (branch_other, down_full, outer_other)
    )
    one = pl.BlockSpec((1, length, model_width), lambda index: (index, 0, 0))
    crossed = pl.BlockSpec((1, length, model_width), lambda index: (1 - index, 0, 0))
    gain_rows = whole(8, model_width)
    middle, normed_two = run(
        middle_kernel,
        (2,),
        team_slots[:2] + [one, crossed, gain_rows],
        [one, one],
        [array(pair_wide, wide), array(pair_wide, low)],
        [],
        20,
        3,
        [slots[0], slots[2], branch_pair, branch_other, gains],
    )
    normed_swap = to_core(normed_two)

    unit_slot = per_slot(length, units)
    unit_shape = array((4, length, units), low)
    hidden, grad_gate, grad_upper, grad_keep, grad_sent = run(
        ff_kernel,
        (4,),
        pairs
        + pairs
        + [whole(*ff_all.shape), whole(units, model_width)],
        [unit_slot] * 3 + pairs,
        [unit_shape] * 3 + [array(pair_wide, wide), array(pair_wide, low)],
        [],
        40,
        21,
        [normed_two, normed_swap, outer_pair, outer_other, ff_all, down_full],
    )
    grad_pair = core_sum(grad_keep, grad_sent)
    grad_sent = grad_pair.astype(low)
    grad_other = to_z(grad_sent)

    grad_sent, hidden, grad_gate, grad_upper = lax.optimization_barrier(
        (grad_sent, hidden, grad_gate, grad_upper)
    )
    (ff_grads,) = run(
        ff_grads_kernel,
        (4,),
        pairs + pairs + [unit_slot] * 3,
        [whole(*ff_all.shape)],
        [array(ff_all.shape, low)],
        [
            pltpu.VMEM((model_width, units), wide),
            pltpu.VMEM((model_width, units), wide),
            pltpu.VMEM((units, model_width), wide),
        ],
        44,
        16,
        [normed_two, normed_swap, outer_pair, outer_other, hidden, grad_gate, grad_upper],
    )
    ff_share = scatter_rows(ff_grads)
    down_term = jnp.dot(
        hidden.reshape(4 * length, units), down_full, preferred_element_type=wide
    ).reshape(4, length, model_width)
    grad_other, ff_grads, down_term = lax.optimization_barrier((grad_other, ff_grads, down_term))
    grad_middle, grad_branch, grad_gain_two = run(
        grad_middle_kernel,
        (2,),
        [one, crossed, one, one, gain_rows],
        [one, one, whole(1, model_width)],
        [array(pair_wide, wide), array(pair_wide, low), array((1, model_width), wide)],
        [],
        24,
        4,
        [grad_pair, grad_other, middle, outer_pair, gains],
    )
    grad_swap = to_core(grad_branch)

    grad_out, grad_conv = run(
        gated_back_kernel,
        (4,),
        pairs + [out_matrix, narrow, out_gate],
        [narrow, narrow],
        [array(slot_narrow, low), array(slot_narrow, wide)],
        [],
        16,
        2,
        [grad_branch, grad_swap, out_full, convolved, projected],
    )
    heads = grad_conv[:, :2]
    sent = by_core(heads[0::2], heads[1::2])
    received = lax.ppermute(sent, "fsdp", TO_PREVIOUS)
    nothing = jnp.zeros_like(received[0])
    shifted = jnp.where(
        z == 0, jnp.stack([received[1], nothing]), jnp.stack([nothing, received[0]])
    )
    after = jnp.where(plane == PLANE - 1, shifted, received)
    own_after = by_core(heads[1::2], after)
    other_after = by_core(after, heads[0::2])
    later = jnp.stack([own_after[0], other_after[0], own_after[1], other_after[1]])
    later = jnp.pad(later, ((0, 0), (0, 6), (0, 0)))
    part_shape, spare_shape = (PLANE, 4 * rows, channels), (PLANE, 4 * rows, SPARE)
    out_part, spare_part = run(
        out_grads_kernel,
        (4,),
        pairs + [narrow, narrow, narrow, edge, whole(1, model_width)],
        [whole(*part_shape), whole(*spare_shape)],
        [array(part_shape, low), array(spare_shape, wide)],
        [
            pltpu.VMEM((channels, model_width), wide),
            pltpu.VMEM((SPARE, channels), wide),
            pltpu.VMEM((SPARE, model_width), wide),
        ],
        20,
        2.5,
        [grad_branch, grad_swap, gated, grad_conv, mixed, earlier, grad_gain_two],
    )
    first_grads, normed_keep, normed_sent = run(
        project_back_kernel,
        (4,),
        [
            narrow,
            edge_after,
            per_slot(length, in_width),
            narrow,
            per_slot(length, model_width),
            in_matrix,
            taps,
        ]
        + team_slots
        + [whole(*part_shape), whole(*spare_shape)],
        [whole(*first_all.shape)] + pairs,
        [array(first_all.shape, low), array(pair_wide, wide), array(pair_wide, low)],
        [pltpu.VMEM((model_width, in_width), wide), pltpu.VMEM((SPARE, model_width), wide)],
        32,
        8,
        [
            grad_conv,
            later,
            projected,
            grad_out,
            normed,
            in_full,
            kernel,
            *slots,
            out_part,
            spare_part,
        ],
    )
    first_grads = first_grads.reshape(PLANE, 4, rows, -1)
    first_arrived = plane_swap(first_grads)

    down_term, normed_sent = lax.optimization_barrier((down_term, normed_sent))
    result = middle[0] + own_sum(down_term[0::2], down_term[1::2].astype(low))
    grad_normed_own = own_sum(normed_keep, normed_sent)
    inputs = tokens.astype(wide)
    grad_inputs = grad_middle[0] + norm_back(
        grad_normed_own * gains[0], inputs, norm_scale(inputs)
    )
    result, grad_inputs, first_arrived = lax.optimization_barrier(
        (result.astype(low), grad_inputs, first_arrived)
    )
    first_share = jnp.sum(first_arrived.astype(wide), axis=0).astype(low)

    def both_reps(value):
        other = lax.ppermute(value, "rep", [(0, 1), (1, 0)])
        return value.astype(wide) + other.astype(wide)

    blocks = jnp.concatenate(
        [
            ff_share[:, :, : 2 * units],
            first_share[:, :, :in_width],
            first_share[:, :, in_width + channels :],
        ],
        2,
    )
    blocks = lax.all_to_all(
        jnp.concatenate([blocks, blocks]),
        ("rep", "fsdp"),
        0,
        0,
        tiled=True,
        axis_index_groups=BOTH_TEAMS,
    )
    owned = jnp.concatenate([ff_share[:, :, 2 * units :], first_share[:, :, in_width:]], 2)
    owned, blocks = lax.optimization_barrier((owned, blocks))
    owned = both_reps(owned)
    down_total, out_total = owned[:, :, : model_width + SPARE], owned[:, :, model_width + SPARE :]
    down_rest = down_total[:, :, model_width:].reshape(block // rest, rest, -1)
    down_rest = down_rest.transpose(1, 0, 2).reshape(rest, model_width)
    down_total = jnp.concatenate(
        [down_total[:, :, :model_width].reshape(block, model_width), down_rest], 0
    )
    conv_total = out_total[0, :, channels + 2 : channels + 5]
    out_total = out_total[:, :, :channels].transpose(1, 0, 2).reshape(rows, model_width)
    in_total, gain_total = run(
        in_total_kernel,
        (1,),
        [whole(*blocks.shape)],
        [whole(rows, w_in.shape[1]), whole(rows, SPARE)],
        [array((rows, w_in.shape[1]), wide), array((rows, SPARE), wide)],
        [],
        16,
        2,
        [blocks],
    )
    ff_total = blocks[:, :, : 2 * units].astype(wide)
    ff_total = ff_total[:4] + ff_total[4:]

    return (
        result,
        grad_inputs,
        gain_total[:, 0],
        in_total,
        conv_total,
        out_total,
        gain_total[:, 1],
        from_members(ff_total[:, :, :units], 1),
        from_members(ff_total[:, :, units:], 1),
        down_total,
    )


def solution(mesh):
    return jax.shard_map(
        body,
        mesh=mesh,
        in_specs=(
            P(("rep", "fsdp"), None),
            P("fsdp"),
            P("fsdp", None),
            P("fsdp", None),
            P("fsdp", None),
            P("fsdp"),
            P("fsdp", None),
            P("fsdp", None),
            P("fsdp", None),
            P(("rep", "fsdp"), None),
        ),
        out_specs=(
            P(("rep", "fsdp"), None),
            P(("rep", "fsdp"), None),
            P("fsdp"),
            P("fsdp", None),
            P("fsdp", None),
            P("fsdp", None),
            P("fsdp"),
            P("fsdp", None),
            P("fsdp", None),
            P("fsdp", None),
        ),
        check_vma=False,
    )
```

```python
import jax
import jax.numpy as jnp
from jax import lax
from jax.experimental import pallas as pl
from jax.experimental.pallas import tpu as pltpu
from jax.sharding import PartitionSpec as P

epsilon = 1e-05

SIDE = 4
PLANE = SIDE * SIDE
HALF = PLANE * 2
SPARE = 128
EDGE = 16
CHUNK = 256
MIB = 1024 * 1024


def place(z, plane, core):
    return (z * PLANE + plane) * 2 + core


def moves(target):
    return [
        (place(z, plane, core), place(*target(z, plane, core)))
        for z in range(2)
        for plane in range(PLANE)
        for core in range(2)
    ]


TO_CORE = moves(lambda z, plane, core: (z, plane, 1 - core))
TO_Z = moves(lambda z, plane, core: (1 - z, plane, core))
TO_FOLLOWING = [(index, index + 1) for index in range(2 * HALF - 1)]
TO_PREVIOUS = moves(lambda z, plane, core: (z, (plane - 1) % PLANE, core))
TEAMS = [
    [place(z, plane, core) for z in range(2) for core in range(2)] for plane in range(PLANE)
]
PLANES = [
    [place(z, plane, core) for plane in range(PLANE)] for z in range(2) for core in range(2)
]
BOTH_TEAMS = [[rep * 2 * HALF + member for rep in range(2) for member in team] for team in TEAMS]


def to_core(value):
    return lax.ppermute(value, "fsdp", TO_CORE)


def to_z(value):
    return lax.ppermute(value, "fsdp", TO_Z)


def norm_scale(values):
    return lax.rsqrt(jnp.mean(values * values, axis=-1, keepdims=True) + epsilon)


def norm_back(grad_normed, values, scale):
    inner = jnp.mean(grad_normed * values, axis=-1, keepdims=True)
    return scale * (grad_normed - values * scale * scale * inner)


def contract_rows(left, right):
    return lax.dot_general(
        left, right, (((0,), (0,)), ((), ())), preferred_element_type=jnp.float32
    )


def contract_cols(left, right):
    return lax.dot_general(
        left, right, (((1,), (1,)), ((), ())), preferred_element_type=jnp.float32
    )


def by_member(shard, parts):
    rows, columns = shard.shape
    split = shard.reshape(rows, parts, 2, PLANE, 2, -1)
    return split.transpose(2, 4, 0, 1, 3, 5).reshape(4, rows, columns // 4)


def from_members(blocks, parts):
    members, rows, columns = blocks.shape
    split = blocks.reshape(2, 2, rows, parts, PLANE, -1)
    return split.transpose(2, 3, 0, 4, 1, 5).reshape(rows, 4 * columns)


def team_swap(blocks):
    return lax.all_to_all(blocks, "fsdp", 0, 0, tiled=True, axis_index_groups=TEAMS)


def plane_swap(blocks):
    return lax.all_to_all(blocks, "fsdp", 0, 0, tiled=True, axis_index_groups=PLANES)


def gather_rows(blocks):
    members, rows, columns = blocks.shape
    return lax.all_gather(
        blocks.reshape(2, 2 * rows, columns),
        "fsdp",
        axis=1,
        tiled=True,
        axis_index_groups=PLANES,
    ).reshape(-1, columns)


def scatter_rows(value):
    total, columns = value.shape
    return lax.psum_scatter(
        value.reshape(2, total // 2, columns),
        "fsdp",
        scatter_dimension=1,
        tiled=True,
        axis_index_groups=PLANES,
    ).reshape(4, -1, columns)


def core_sum(keep, sent):
    return keep + to_core(sent).astype(jnp.float32)


def own_sum(keep, sent):
    pair = core_sum(keep, sent)
    return pair[0] + to_z(pair[1].astype(jnp.bfloat16)).astype(jnp.float32)


def whole(*shape):
    return pl.BlockSpec(shape, lambda *_: (0,) * len(shape))


def per_slot(length, width, column=0):
    return pl.BlockSpec((1, length, width), lambda slot: (slot, 0, column))


def per_pair(length, width):
    return pl.BlockSpec((1, length, width), lambda slot: (slot // 2, 0, 0))


def run(kernel, grid, in_specs, out_specs, out_shape, scratch, room, busy, values):
    return pl.pallas_call(
        kernel,
        grid=grid,
        in_specs=in_specs,
        out_specs=out_specs,
        out_shape=out_shape,
        scratch_shapes=scratch,
        compiler_params=pltpu.CompilerParams(vmem_limit_bytes=room * MIB),
        cost_estimate=pl.CostEstimate(
            flops=int(busy * 1.15e9), bytes_accessed=0, transcendentals=0
        ),
    )(*values)


def array(shape, kind):
    return jax.ShapeDtypeStruct(shape, kind)


def pick(slot, even, odd):
    return jnp.where(slot % 2 == 0, even, odd)


def shifted_in(values, rows_before, steps):
    moved = pltpu.roll(values, steps, 0)
    row = lax.broadcasted_iota(jnp.int32, values.shape, 0)
    for index in range(steps):
        at = EDGE - steps + index
        moved = jnp.where(row == index, rows_before[at : at + 1], moved)
    return moved


def shifted_out(values, next_rows, steps):
    length = values.shape[0]
    moved = pltpu.roll(values, length - steps, 0)
    row = lax.broadcasted_iota(jnp.int32, values.shape, 0)
    for index in range(steps):
        moved = jnp.where(row == length - steps + index, next_rows[index : index + 1], moved)
    return moved


def store_pair(slot, value, keep_ref, sent_ref):
    @pl.when(slot % 2 == 0)
    def _():
        keep_ref[0] = value

    @pl.when(slot % 2 == 1)
    def _():
        sent_ref[0] = value.astype(sent_ref.dtype)


def project_kernel(
    pair_ref, other_ref, pair_edge_ref, other_edge_ref, first_ref,
    normed_ref, proj_ref, mixed_ref, earlier_ref, in_ref, out_ref, gains_ref, taps_ref,
    column, taps_column,
):
    slot = pl.program_id(0)
    width = in_ref.shape[1]
    channels = width // 3
    rows = channels // PLANE

    @pl.when(slot == 0)
    def _():
        for plane in range(PLANE):
            for z in range(2):
                at = pl.ds((z * PLANE + plane) * 2 * rows, 2 * rows)
                source = pl.ds(z * 2 * rows, 2 * rows)
                in_ref[at, :] = first_ref[plane, source, :width]
                column[at, :] = first_ref[plane, source, width + channels :].astype(jnp.float32)
            at = pl.ds(plane * rows, rows)
            for part in range(4):
                out_ref[at, part * channels : (part + 1) * channels] = first_ref[
                    plane, pl.ds(part * rows, rows), width : width + channels
                ]
            taps_column[at, :] = first_ref[plane, :rows, width + channels :].astype(jnp.float32)
        gains_ref[...] = column[...].T[:8]
        taps_ref[...] = taps_column[...].T[:8]

    def project(values):
        values = values.astype(jnp.float32)
        normed = (values * norm_scale(values) * gains_ref[0:1]).astype(jnp.bfloat16)
        projected = jnp.dot(normed, in_ref[...], preferred_element_type=jnp.float32)
        mixed = (projected[:, :channels] * projected[:, 2 * channels :]).astype(jnp.bfloat16)
        return normed, projected, mixed

    normed_ref[0], proj_ref[0], mixed_ref[0] = project(pick(slot, pair_ref[0], other_ref[0]))
    edge = project(pick(slot, pair_edge_ref[0], other_edge_ref[0]))[2]
    earlier_ref[0] = edge.astype(jnp.float32)


def branch_kernel(
    mixed_ref, earlier_ref, out_gate_ref, taps_ref, out_ref,
    convolved_ref, gated_ref, keep_ref, sent_ref,
):
    slot = pl.program_id(0)
    mixed = mixed_ref[0].astype(jnp.float32)
    earlier = earlier_ref[0]
    convolved = (
        taps_ref[2:3] * mixed
        + taps_ref[3:4] * shifted_in(mixed, earlier, 1)
        + taps_ref[4:5] * shifted_in(mixed, earlier, 2)
    )
    convolved_ref[0] = convolved
    gated = (out_gate_ref[0] * convolved).astype(jnp.bfloat16)
    gated_ref[0] = gated
    branch = jnp.dot(gated, out_ref[...], preferred_element_type=jnp.float32)
    store_pair(slot, branch, keep_ref, sent_ref)


def middle_kernel(inputs_ref, branch_ref, crossed_ref, gains_ref, middle_ref, normed_ref):
    middle = inputs_ref[0].astype(jnp.float32) + branch_ref[0]
    middle += crossed_ref[0].astype(jnp.float32)
    middle_ref[0] = middle
    normed_ref[0] = (middle * norm_scale(middle) * gains_ref[1:2]).astype(jnp.bfloat16)


def grad_middle_kernel(
    grad_ref, crossed_ref, middle_ref, outer_ref, gains_ref,
    grad_middle_ref, branch_ref, gain_ref,
):
    grad_normed = grad_ref[0] + crossed_ref[0].astype(jnp.float32)
    middle = middle_ref[0]
    scale = norm_scale(middle)

    @pl.when(pl.program_id(0) == 0)
    def _():
        gain_ref[...] = jnp.sum(grad_normed * middle * scale, axis=0, keepdims=True)

    grad_middle = norm_back(grad_normed * gains_ref[1:2], middle, scale)
    grad_middle += outer_ref[0].astype(jnp.float32)
    grad_middle_ref[0] = grad_middle
    branch_ref[0] = grad_middle.astype(jnp.bfloat16)


def ff_kernel(
    own_ref, swap_ref, pair_ref, other_ref, weights_ref, down_ref,
    hidden_ref, grad_gate_ref, grad_up_ref, keep_ref, sent_ref,
):
    slot = pl.program_id(0)
    units = down_ref.shape[0]
    normed = pick(slot, own_ref[0], swap_ref[0])
    outer = pick(slot, pair_ref[0], other_ref[0])
    for start in range(0, units, CHUNK):
        lanes = slice(start, min(start + CHUNK, units))
        up_lanes = slice(units + lanes.start, units + lanes.stop)
        gate = jnp.dot(normed, weights_ref[:, lanes], preferred_element_type=jnp.float32)
        up = jnp.dot(normed, weights_ref[:, up_lanes], preferred_element_type=jnp.float32)
        grad = contract_cols(outer, down_ref[lanes, :])
        sigmoid = jax.nn.sigmoid(gate)
        silu = gate * sigmoid
        hidden_ref[0, :, lanes] = (silu * up).astype(jnp.bfloat16)
        grad_gate = grad * up * sigmoid * (1.0 + gate * (1.0 - sigmoid))
        grad_gate_ref[0, :, lanes] = grad_gate.astype(jnp.bfloat16)
        grad_up_ref[0, :, lanes] = (grad * silu).astype(jnp.bfloat16)
    term = contract_cols(grad_gate_ref[0], weights_ref[:, :units])
    term += contract_cols(grad_up_ref[0], weights_ref[:, units : 2 * units])
    store_pair(slot, term, keep_ref, sent_ref)


def ff_grads_kernel(
    own_ref, swap_ref, pair_ref, other_ref, hidden_ref, grad_gate_ref, grad_up_ref,
    pack_ref,
    gate_total, up_total, down_total,
):
    slot = pl.program_id(0)
    width, units = gate_total.shape
    each = units // PLANE
    block = width // PLANE
    rest = each - block
    normed = pick(slot, own_ref[0], swap_ref[0])
    outer = pick(slot, pair_ref[0], other_ref[0])

    @pl.when(slot == 0)
    def _():
        gate_total[...] = jnp.zeros_like(gate_total)
        up_total[...] = jnp.zeros_like(up_total)
        down_total[...] = jnp.zeros_like(down_total)

    gate_total[...] += contract_rows(normed, grad_gate_ref[0])
    up_total[...] += contract_rows(normed, grad_up_ref[0])
    down_total[...] += contract_rows(hidden_ref[0], outer)

    @pl.when(slot == 3)
    def _():
        pack_ref[:, :units] = gate_total[...].astype(jnp.bfloat16)
        pack_ref[:, units : 2 * units] = up_total[...].astype(jnp.bfloat16)
        for plane in range(PLANE):
            start = plane * each
            for half in range(2):
                to = half * width // 2 + plane * block // 2
                pack_ref[to : to + block // 2, 2 * units : 2 * units + width] = down_total[
                    start + half * block // 2 : start + (half + 1) * block // 2
                ].astype(jnp.bfloat16)
                parts = block // rest // 2
                lanes = width * rest // block
                last = down_total[start + block : start + each]
                pieces = [
                    last[:, (half * parts + part) * lanes : (half * parts + part + 1) * lanes]
                    for part in range(parts)
                ]
                pack_ref[to : to + block // 2, 2 * units + width :] = jnp.concatenate(
                    pieces, 0
                ).astype(jnp.bfloat16)


def gated_back_kernel(
    own_ref, swap_ref, out_ref, convolved_ref, out_gate_ref, grad_out_ref, grad_conv_ref
):
    slot = pl.program_id(0)
    grad_gated = contract_cols(pick(slot, own_ref[0], swap_ref[0]), out_ref[...])
    grad_out_ref[0] = (grad_gated * convolved_ref[0]).astype(jnp.bfloat16)
    grad_conv_ref[0] = grad_gated * out_gate_ref[0]


def out_grads_kernel(
    own_ref, swap_ref, gated_ref, grad_conv_ref, mixed_ref, earlier_ref, gain_ref,
    part_ref, spare_ref,
    total, taps_rows, gain_rows,
):
    slot = pl.program_id(0)
    rows = spare_ref.shape[1] // 4
    channels = gated_ref.shape[2]

    @pl.when(slot == 0)
    def _():
        total[...] = jnp.zeros_like(total)
        taps_rows[...] = jnp.zeros_like(taps_rows)
        gain_rows[...] = jnp.zeros_like(gain_rows)
        gain_rows[1:2] = gain_ref[...]

    total[...] += contract_rows(gated_ref[0], pick(slot, own_ref[0], swap_ref[0]))
    grad_conv = grad_conv_ref[0]
    mixed = mixed_ref[0].astype(jnp.float32)
    earlier = earlier_ref[0]
    lagged = (mixed, shifted_in(mixed, earlier, 1), shifted_in(mixed, earlier, 2))
    for lag, value in enumerate(lagged):
        taps_rows[2 + lag : 3 + lag] += jnp.sum(grad_conv * value, axis=0, keepdims=True)

    @pl.when(slot == 3)
    def _():
        gain_column = gain_rows[...].T
        taps_column = taps_rows[...].T
        for plane in range(PLANE):
            at = slice(plane * rows, (plane + 1) * rows)
            for part in range(4):
                part_ref[plane, part * rows : (part + 1) * rows, :] = total[
                    at, part * channels : (part + 1) * channels
                ].astype(jnp.bfloat16)
            for z in range(2):
                start = (z * PLANE + plane) * 2 * rows
                spare_ref[plane, z * 2 * rows : (z + 1) * 2 * rows, :] = gain_column[
                    start : start + 2 * rows
                ]
            spare_ref[plane, :rows, :] += taps_column[at]


def project_back_kernel(
    grad_conv_ref, later_ref, proj_ref, grad_out_ref, normed_ref, in_ref, taps_ref,
    pair_ref, other_ref, part_ref, spare_ref,
    pack_ref, keep_ref, sent_ref,
    total, gain_rows,
):
    slot = pl.program_id(0)
    width = in_ref.shape[1]
    channels = width // 3
    rows = channels // PLANE

    @pl.when(slot == 0)
    def _():
        total[...] = jnp.zeros_like(total)
        gain_rows[...] = jnp.zeros_like(gain_rows)

    grad_conv, later = grad_conv_ref[0], later_ref[0]
    grad_mixed = (
        taps_ref[2:3] * grad_conv
        + taps_ref[3:4] * shifted_out(grad_conv, later, 1)
        + taps_ref[4:5] * shifted_out(grad_conv, later, 2)
    )
    grad_projected = jnp.concatenate(
        [
            (grad_mixed * proj_ref[0, :, 2 * channels :]).astype(jnp.bfloat16),
            grad_out_ref[0],
            (grad_mixed * proj_ref[0, :, :channels]).astype(jnp.bfloat16),
        ],
        1,
    )
    total[...] += contract_rows(normed_ref[0], grad_projected)
    grad_normed = contract_cols(grad_projected, in_ref[...])
    store_pair(slot, grad_normed, keep_ref, sent_ref)
    values = pick(slot, pair_ref[0], other_ref[0]).astype(jnp.float32)
    gain_rows[0:1] += jnp.sum(grad_normed * values * norm_scale(values), axis=0, keepdims=True)

    @pl.when(slot == 3)
    def _():
        gain_column = gain_rows[...].T
        for plane in range(PLANE):
            for z in range(2):
                start = (z * PLANE + plane) * 2 * rows
                to = slice(z * 2 * rows, (z + 1) * 2 * rows)
                pack_ref[plane, to, :width] = total[start : start + 2 * rows].astype(jnp.bfloat16)
                pack_ref[plane, to, width + channels :] = (
                    spare_ref[plane, to] + gain_column[start : start + 2 * rows]
                ).astype(jnp.bfloat16)
            pack_ref[plane, :, width : width + channels] = part_ref[plane]


def in_total_kernel(blocks_ref, total_ref, spare_ref):
    members, rows, width = blocks_ref.shape
    channels = total_ref.shape[1] // 12
    first = width - SPARE - 3 * channels
    unit = channels // PLANE
    source = lax.broadcasted_iota(jnp.int32, (channels, 2 * channels), 0)
    target = lax.broadcasted_iota(jnp.int32, (channels, 2 * channels), 1)
    for z in range(2):
        for part in range(3):
            total = jnp.zeros((rows, 2 * channels), jnp.float32)
            for core in range(2):
                placed = source // unit * (2 * unit) + core * unit + source % unit == target
                placed = placed.astype(jnp.float32).astype(jnp.bfloat16)
                for rep in range(2):
                    block = blocks_ref[rep * 4 + z * 2 + core]
                    total += jnp.dot(
                        block[:, first + part * channels : first + (part + 1) * channels],
                        placed,
                        preferred_element_type=jnp.float32,
                    )
            start = (part * 2 + z) * 2 * channels
            total_ref[:, start : start + 2 * channels] = total
    spare = jnp.zeros((rows, SPARE), jnp.float32)
    for member in range(members):
        spare += blocks_ref[member, :, width - SPARE :].astype(jnp.float32)
    spare_ref[...] = spare


def body(
    tokens, gain_first, w_in, conv_weight, w_out, gain_second, w_gate, w_up, w_down, cotangent
):
    low, wide = jnp.bfloat16, jnp.float32
    length, model_width = tokens.shape
    position = lax.axis_index("fsdp")
    core, plane, z = position % 2, position // 2 % PLANE, position // HALF
    rows = w_in.shape[0]
    channels = model_width // 4

    before = lax.ppermute(tokens[length - EDGE :], "fsdp", TO_FOLLOWING)
    extended = jnp.concatenate([tokens, before], 0)
    extended_z = to_z(extended)

    block = 4 * rows
    rest = w_down.shape[0] - block
    units = w_down.shape[0] * PLANE
    gains = jnp.pad(jnp.stack([gain_first, gain_second], 1), ((0, 0), (0, SPARE - 2)))
    gains = jnp.broadcast_to(gains, (4, rows, SPARE))
    swapped = team_swap(
        jnp.concatenate(
            [by_member(w_gate, 1), by_member(w_up, 1), by_member(w_in, 3), gains], 2
        )
    )
    down_main = w_down[:block].reshape(4, rows, model_width)
    down_rest = w_down[block:].reshape(rest, block // rest, -1).transpose(1, 0, 2)
    ff_all = gather_rows(
        jnp.concatenate(
            [swapped[:, :, : 2 * units], down_main, down_rest.reshape(4, rows, -1)], 2
        )
    )

    in_width = 3 * channels
    conv_lanes = jnp.pad(conv_weight, ((0, 0), (2, SPARE - 5)))
    first_pack = jnp.concatenate(
        [
            swapped[:, :, 2 * units : 2 * units + in_width],
            w_out.reshape(rows, 4, channels).transpose(1, 0, 2),
            swapped[:, :, 2 * units + in_width :] + conv_lanes,
        ],
        2,
    )
    first_pack, extended_z = lax.optimization_barrier((first_pack, extended_z))
    pair = jnp.stack([extended, extended_z])
    other = to_core(pair)
    first_all = plane_swap(jnp.broadcast_to(first_pack, (PLANE,) + first_pack.shape))
    first_all, outer = lax.optimization_barrier((first_all, cotangent))
    first_all = first_all.reshape(PLANE, 4 * rows, -1)
    outer_z = to_z(outer)

    main_rows = ff_all[:, 2 * units : 2 * units + model_width].reshape(2, PLANE, 2 * rows, -1)
    main_rows = main_rows.transpose(1, 0, 2, 3).reshape(PLANE, block, model_width)
    rest_rows = ff_all[:, 2 * units + model_width :].reshape(2, PLANE, 2 * rows, -1)
    rest_rows = rest_rows.transpose(1, 0, 2, 3).reshape(PLANE, block // rest, rest, -1)
    rest_rows = rest_rows.transpose(0, 2, 1, 3).reshape(PLANE, rest, model_width)
    down_full = jnp.concatenate([main_rows, rest_rows], 1).reshape(units, model_width)

    team_pairs = [per_pair(length, model_width)] * 2
    slot_wide, slot_narrow = (4, length, model_width), (4, length, channels)
    pair_wide = (2, length, model_width)
    pairs = [per_pair(length, model_width)] * 2
    narrow = per_slot(length, channels)
    out_gate = per_slot(length, channels, 1)
    edge, edge_after = per_slot(EDGE, channels), per_slot(8, channels)
    team_edges = [
        pl.BlockSpec((1, EDGE, model_width), lambda slot: (slot // 2, length // EDGE, 0))
    ] * 2
    out_matrix, in_matrix = whole(channels, model_width), whole(model_width, in_width)
    taps = whole(8, channels)

    normed, projected, mixed, earlier, in_full, out_full, gains, kernel = run(
        project_kernel,
        (4,),
        team_pairs + team_edges + [whole(*first_all.shape)],
        [
            per_slot(length, model_width),
            per_slot(length, in_width),
            narrow,
            edge,
            in_matrix,
            out_matrix,
            whole(8, model_width),
            taps,
        ],
        [
            array(slot_wide, low),
            array((4, length, in_width), wide),
            array(slot_narrow, low),
            array((4, EDGE, channels), wide),
            array((model_width, in_width), low),
            array((channels, model_width), low),
            array((8, model_width), wide),
            array((8, channels), wide),
        ],
        [pltpu.VMEM((model_width, SPARE), wide), pltpu.VMEM((channels, SPARE), wide)],
        24,
        0.2,
        [pair, other, pair, other, first_all],
    )

    def by_core(first, second):
        return jnp.where(core == 0, first, second)

    convolved, gated, branch_keep, branch_sent = run(
        branch_kernel,
        (4,),
        [narrow, edge, out_gate, taps, out_matrix],
        [narrow, narrow] + pairs,
        [
            array(slot_narrow, wide),
            array(slot_narrow, low),
            array(pair_wide, wide),
            array(pair_wide, low),
        ],
        [],
        16,
        0.2,
        [mixed, earlier, projected, kernel, out_full],
    )
    branch_pair = core_sum(branch_keep, branch_sent)
    branch_sent, outer_z = lax.optimization_barrier((branch_pair.astype(low), outer_z))
    outer_pair = jnp.stack([outer, outer_z])
    outer_other = to_core(outer_pair)
    branch_other = to_z(branch_sent)
    branch_other, down_full, outer_other = lax.optimization_barrier(
        (branch_other, down_full, outer_other)
    )
    one = pl.BlockSpec((1, length, model_width), lambda index: (index, 0, 0))
    crossed = pl.BlockSpec((1, length, model_width), lambda index: (1 - index, 0, 0))
    gain_rows = whole(8, model_width)
    middle, normed_two = run(
        middle_kernel,
        (2,),
        [one, one, crossed, gain_rows],
        [one, one],
        [array(pair_wide, wide), array(pair_wide, low)],
        [],
        20,
        3,
        [pair, branch_pair, branch_other, gains],
    )
    normed_swap = to_core(normed_two)

    unit_slot = per_slot(length, units)
    unit_shape = array((4, length, units), low)
    hidden, grad_gate, grad_upper, grad_keep, grad_sent = run(
        ff_kernel,
        (4,),
        pairs
        + pairs
        + [whole(*ff_all.shape), whole(units, model_width)],
        [unit_slot] * 3 + pairs,
        [unit_shape] * 3 + [array(pair_wide, wide), array(pair_wide, low)],
        [],
        40,
        21,
        [normed_two, normed_swap, outer_pair, outer_other, ff_all, down_full],
    )
    grad_pair = core_sum(grad_keep, grad_sent)
    grad_sent = grad_pair.astype(low)
    grad_other = to_z(grad_sent)

    (ff_grads,) = run(
        ff_grads_kernel,
        (4,),
        pairs + pairs + [unit_slot] * 3,
        [whole(*ff_all.shape)],
        [array(ff_all.shape, low)],
        [
            pltpu.VMEM((model_width, units), wide),
            pltpu.VMEM((model_width, units), wide),
            pltpu.VMEM((units, model_width), wide),
        ],
        44,
        16,
        [normed_two, normed_swap, outer_pair, outer_other, hidden, grad_gate, grad_upper],
    )
    ff_share = scatter_rows(ff_grads)
    down_term = jnp.dot(
        hidden.reshape(4 * length, units), down_full, preferred_element_type=wide
    ).reshape(4, length, model_width)
    grad_other, ff_grads, down_term = lax.optimization_barrier((grad_other, ff_grads, down_term))
    grad_middle, grad_branch, grad_gain_two = run(
        grad_middle_kernel,
        (2,),
        [one, crossed, one, one, gain_rows],
        [one, one, whole(1, model_width)],
        [array(pair_wide, wide), array(pair_wide, low), array((1, model_width), wide)],
        [],
        24,
        4,
        [grad_pair, grad_other, middle, outer_pair, gains],
    )
    grad_swap = to_core(grad_branch)

    grad_out, grad_conv = run(
        gated_back_kernel,
        (4,),
        pairs + [out_matrix, narrow, out_gate],
        [narrow, narrow],
        [array(slot_narrow, low), array(slot_narrow, wide)],
        [],
        16,
        2,
        [grad_branch, grad_swap, out_full, convolved, projected],
    )
    heads = grad_conv[:, :2]
    sent = by_core(heads[0::2], heads[1::2])
    received = lax.ppermute(sent, "fsdp", TO_PREVIOUS)
    nothing = jnp.zeros_like(received[0])
    shifted = jnp.where(
        z == 0, jnp.stack([received[1], nothing]), jnp.stack([nothing, received[0]])
    )
    after = jnp.where(plane == PLANE - 1, shifted, received)
    own_after = by_core(heads[1::2], after)
    other_after = by_core(after, heads[0::2])
    later = jnp.stack([own_after[0], other_after[0], own_after[1], other_after[1]])
    later = jnp.pad(later, ((0, 0), (0, 6), (0, 0)))
    part_shape, spare_shape = (PLANE, 4 * rows, channels), (PLANE, 4 * rows, SPARE)
    out_part, spare_part = run(
        out_grads_kernel,
        (4,),
        pairs + [narrow, narrow, narrow, edge, whole(1, model_width)],
        [whole(*part_shape), whole(*spare_shape)],
        [array(part_shape, low), array(spare_shape, wide)],
        [
            pltpu.VMEM((channels, model_width), wide),
            pltpu.VMEM((SPARE, channels), wide),
            pltpu.VMEM((SPARE, model_width), wide),
        ],
        20,
        2.5,
        [grad_branch, grad_swap, gated, grad_conv, mixed, earlier, grad_gain_two],
    )
    first_grads, normed_keep, normed_sent = run(
        project_back_kernel,
        (4,),
        [
            narrow,
            edge_after,
            per_slot(length, in_width),
            narrow,
            per_slot(length, model_width),
            in_matrix,
            taps,
        ]
        + team_pairs
        + [whole(*part_shape), whole(*spare_shape)],
        [whole(*first_all.shape)] + pairs,
        [array(first_all.shape, low), array(pair_wide, wide), array(pair_wide, low)],
        [pltpu.VMEM((model_width, in_width), wide), pltpu.VMEM((SPARE, model_width), wide)],
        32,
        8,
        [
            grad_conv,
            later,
            projected,
            grad_out,
            normed,
            in_full,
            kernel,
            pair,
            other,
            out_part,
            spare_part,
        ],
    )
    first_grads = first_grads.reshape(PLANE, 4, rows, -1)
    first_arrived = plane_swap(first_grads)

    down_term, normed_sent = lax.optimization_barrier((down_term, normed_sent))
    result = middle[0] + own_sum(down_term[0::2], down_term[1::2].astype(low))
    grad_normed_own = own_sum(normed_keep, normed_sent)
    inputs = tokens.astype(wide)
    grad_inputs = grad_middle[0] + norm_back(
        grad_normed_own * gains[0], inputs, norm_scale(inputs)
    )
    result, grad_inputs, first_arrived = lax.optimization_barrier(
        (result.astype(low), grad_inputs, first_arrived)
    )
    first_share = jnp.sum(first_arrived.astype(wide), axis=0).astype(low)

    def both_reps(value):
        other = lax.ppermute(value, "rep", [(0, 1), (1, 0)])
        return value.astype(wide) + other.astype(wide)

    blocks = jnp.concatenate(
        [
            ff_share[:, :, : 2 * units],
            first_share[:, :, :in_width],
            first_share[:, :, in_width + channels :],
        ],
        2,
    )
    blocks = lax.all_to_all(
        jnp.concatenate([blocks, blocks]),
        ("rep", "fsdp"),
        0,
        0,
        tiled=True,
        axis_index_groups=BOTH_TEAMS,
    )
    owned = jnp.concatenate([ff_share[:, :, 2 * units :], first_share[:, :, in_width:]], 2)
    owned, blocks = lax.optimization_barrier((owned, blocks))
    owned = both_reps(owned)
    down_total, out_total = owned[:, :, : model_width + SPARE], owned[:, :, model_width + SPARE :]
    down_rest = down_total[:, :, model_width:].reshape(block // rest, rest, -1)
    down_rest = down_rest.transpose(1, 0, 2).reshape(rest, model_width)
    down_total = jnp.concatenate(
        [down_total[:, :, :model_width].reshape(block, model_width), down_rest], 0
    )
    conv_total = out_total[0, :, channels + 2 : channels + 5]
    out_total = out_total[:, :, :channels].transpose(1, 0, 2).reshape(rows, model_width)
    in_total, gain_total = run(
        in_total_kernel,
        (1,),
        [whole(*blocks.shape)],
        [whole(rows, w_in.shape[1]), whole(rows, SPARE)],
        [array((rows, w_in.shape[1]), wide), array((rows, SPARE), wide)],
        [],
        16,
        2,
        [blocks],
    )
    ff_total = blocks[:, :, : 2 * units].astype(wide)
    ff_total = ff_total[:4] + ff_total[4:]

    return (
        result,
        grad_inputs,
        gain_total[:, 0],
        in_total,
        conv_total,
        out_total,
        gain_total[:, 1],
        from_members(ff_total[:, :, :units], 1),
        from_members(ff_total[:, :, units:], 1),
        down_total,
    )


def solution(mesh):
    return jax.shard_map(
        body,
        mesh=mesh,
        in_specs=(
            P(("rep", "fsdp"), None),
            P("fsdp"),
            P("fsdp", None),
            P("fsdp", None),
            P("fsdp", None),
            P("fsdp"),
            P("fsdp", None),
            P("fsdp", None),
            P("fsdp", None),
            P(("rep", "fsdp"), None),
        ),
        out_specs=(
            P(("rep", "fsdp"), None),
            P(("rep", "fsdp"), None),
            P("fsdp"),
            P("fsdp", None),
            P("fsdp", None),
            P("fsdp", None),
            P("fsdp"),
            P("fsdp", None),
            P("fsdp", None),
            P("fsdp", None),
        ),
        check_vma=False,
    )
```

```python
import jax
import jax.numpy as jnp
from jax import lax
from jax.experimental import pallas as pl
from jax.experimental.pallas import tpu as pltpu
from jax.sharding import PartitionSpec as P

epsilon = 1e-05

SIDE = 4
PLANE = SIDE * SIDE
HALF = PLANE * 2
SPARE = 128
EDGE = 8
CHUNK = 256
MIB = 1024 * 1024


def place(z, plane, core):
    return (z * PLANE + plane) * 2 + core


def moves(target):
    return [
        (place(z, plane, core), place(*target(z, plane, core)))
        for z in range(2)
        for plane in range(PLANE)
        for core in range(2)
    ]


TO_CORE = moves(lambda z, plane, core: (z, plane, 1 - core))
TO_Z = moves(lambda z, plane, core: (1 - z, plane, core))
TO_NEXT = moves(lambda z, plane, core: (z, (plane + 1) % PLANE, core))
TO_PREVIOUS = moves(lambda z, plane, core: (z, (plane - 1) % PLANE, core))
TEAMS = [
    [place(z, plane, core) for z in range(2) for core in range(2)] for plane in range(PLANE)
]
PLANES = [
    [place(z, plane, core) for plane in range(PLANE)] for z in range(2) for core in range(2)
]
BOTH_TEAMS = [[rep * 2 * HALF + member for rep in range(2) for member in team] for team in TEAMS]


def to_core(value):
    return lax.ppermute(value, "fsdp", TO_CORE)


def to_z(value):
    return lax.ppermute(value, "fsdp", TO_Z)


def norm_scale(values):
    return lax.rsqrt(jnp.mean(values * values, axis=-1, keepdims=True) + epsilon)


def norm_back(grad_normed, values, scale):
    inner = jnp.mean(grad_normed * values, axis=-1, keepdims=True)
    return scale * (grad_normed - values * scale * scale * inner)


def contract_rows(left, right):
    return lax.dot_general(
        left, right, (((0,), (0,)), ((), ())), preferred_element_type=jnp.float32
    )


def contract_cols(left, right):
    return lax.dot_general(
        left, right, (((1,), (1,)), ((), ())), preferred_element_type=jnp.float32
    )


def by_member(shard, parts):
    rows, columns = shard.shape
    split = shard.reshape(rows, parts, 2, PLANE, 2, -1)
    return split.transpose(2, 4, 0, 1, 3, 5).reshape(4, rows, columns // 4)


def from_members(blocks, parts):
    members, rows, columns = blocks.shape
    split = blocks.reshape(2, 2, rows, parts, PLANE, -1)
    return split.transpose(2, 3, 0, 4, 1, 5).reshape(rows, 4 * columns)


def team_swap(blocks):
    return lax.all_to_all(blocks, "fsdp", 0, 0, tiled=True, axis_index_groups=TEAMS)


def plane_swap(blocks):
    return lax.all_to_all(blocks, "fsdp", 0, 0, tiled=True, axis_index_groups=PLANES)


def gather_rows(blocks):
    members, rows, columns = blocks.shape
    return lax.all_gather(
        blocks.reshape(2, 2 * rows, columns),
        "fsdp",
        axis=1,
        tiled=True,
        axis_index_groups=PLANES,
    ).reshape(-1, columns)


def scatter_rows(value):
    total, columns = value.shape
    return lax.psum_scatter(
        value.reshape(2, total // 2, columns),
        "fsdp",
        scatter_dimension=1,
        tiled=True,
        axis_index_groups=PLANES,
    ).reshape(4, -1, columns)


def core_sum(keep, sent):
    return keep + to_core(sent).astype(jnp.float32)


def own_sum(keep, sent):
    pair = core_sum(keep, sent)
    return pair[0] + to_z(pair[1].astype(jnp.bfloat16)).astype(jnp.float32)


def whole(*shape):
    return pl.BlockSpec(shape, lambda *_: (0,) * len(shape))


def per_slot(length, width, column=0):
    return pl.BlockSpec((1, length, width), lambda slot: (slot, 0, column))


def per_pair(length, width):
    return pl.BlockSpec((1, length, width), lambda slot: (slot // 2, 0, 0))


def pair_of_values(length, width, which):
    return pl.BlockSpec((1, 1, length, width), lambda slot: (slot // 2, which, 0, 0))


def run(kernel, grid, in_specs, out_specs, out_shape, scratch, room, busy, values):
    return pl.pallas_call(
        kernel,
        grid=grid,
        in_specs=in_specs,
        out_specs=out_specs,
        out_shape=out_shape,
        scratch_shapes=scratch,
        compiler_params=pltpu.CompilerParams(vmem_limit_bytes=room * MIB),
        cost_estimate=pl.CostEstimate(
            flops=int(busy * 1.15e9), bytes_accessed=0, transcendentals=0
        ),
    )(*values)


def array(shape, kind):
    return jax.ShapeDtypeStruct(shape, kind)


def pick(slot, even, odd):
    return jnp.where(slot % 2 == 0, even, odd)


def shifted_in(values, rows_before, steps):
    moved = pltpu.roll(values, steps, 0)
    row = lax.broadcasted_iota(jnp.int32, values.shape, 0)
    for index in range(steps):
        at = EDGE - steps + index
        moved = jnp.where(row == index, rows_before[at : at + 1], moved)
    return moved


def shifted_out(values, next_rows, steps):
    length = values.shape[0]
    moved = pltpu.roll(values, length - steps, 0)
    row = lax.broadcasted_iota(jnp.int32, values.shape, 0)
    for index in range(steps):
        moved = jnp.where(row == length - steps + index, next_rows[index : index + 1], moved)
    return moved


def store_pair(slot, value, keep_ref, sent_ref):
    @pl.when(slot % 2 == 0)
    def _():
        keep_ref[0] = value

    @pl.when(slot % 2 == 1)
    def _():
        sent_ref[0] = value.astype(sent_ref.dtype)


def project_kernel(
    pair_ref, other_ref, first_ref,
    normed_ref, proj_ref, mixed_ref, in_ref, out_ref, gains_ref, taps_ref,
    column, taps_column,
):
    slot = pl.program_id(0)
    width = in_ref.shape[1]
    channels = width // 3
    rows = channels // PLANE

    @pl.when(slot == 0)
    def _():
        for plane in range(PLANE):
            for z in range(2):
                at = pl.ds((z * PLANE + plane) * 2 * rows, 2 * rows)
                source = pl.ds(z * 2 * rows, 2 * rows)
                in_ref[at, :] = first_ref[plane, source, :width]
                column[at, :] = first_ref[plane, source, width + channels :].astype(jnp.float32)
            at = pl.ds(plane * rows, rows)
            for part in range(4):
                out_ref[at, part * channels : (part + 1) * channels] = first_ref[
                    plane, pl.ds(part * rows, rows), width : width + channels
                ]
            taps_column[at, :] = first_ref[plane, :rows, width + channels :].astype(jnp.float32)
        gains_ref[...] = column[...].T[:8]
        taps_ref[...] = taps_column[...].T[:8]

    values = pick(slot, pair_ref[0, 0], other_ref[0, 0]).astype(jnp.float32)
    normed = (values * norm_scale(values) * gains_ref[0:1]).astype(jnp.bfloat16)
    normed_ref[0] = normed
    projected = jnp.dot(normed, in_ref[...], preferred_element_type=jnp.float32)
    proj_ref[0] = projected
    mixed = projected[:, :channels] * projected[:, 2 * channels :]
    mixed_ref[0] = mixed.astype(jnp.bfloat16)


def branch_kernel(
    mixed_ref, earlier_ref, out_gate_ref, taps_ref, out_ref,
    convolved_ref, gated_ref, keep_ref, sent_ref,
):
    slot = pl.program_id(0)
    mixed = mixed_ref[0].astype(jnp.float32)
    earlier = earlier_ref[0]
    convolved = (
        taps_ref[2:3] * mixed
        + taps_ref[3:4] * shifted_in(mixed, earlier, 1)
        + taps_ref[4:5] * shifted_in(mixed, earlier, 2)
    )
    convolved_ref[0] = convolved
    gated = (out_gate_ref[0] * convolved).astype(jnp.bfloat16)
    gated_ref[0] = gated
    branch = jnp.dot(gated, out_ref[...], preferred_element_type=jnp.float32)
    store_pair(slot, branch, keep_ref, sent_ref)


def middle_kernel(inputs_ref, branch_ref, crossed_ref, gains_ref, middle_ref, normed_ref):
    middle = inputs_ref[0, 0].astype(jnp.float32) + branch_ref[0]
    middle += crossed_ref[0].astype(jnp.float32)
    middle_ref[0] = middle
    normed_ref[0] = (middle * norm_scale(middle) * gains_ref[1:2]).astype(jnp.bfloat16)


def grad_middle_kernel(
    grad_ref, crossed_ref, middle_ref, outer_ref, gains_ref,
    grad_middle_ref, branch_ref, gain_ref,
):
    grad_normed = grad_ref[0] + crossed_ref[0].astype(jnp.float32)
    middle = middle_ref[0]
    scale = norm_scale(middle)

    @pl.when(pl.program_id(0) == 0)
    def _():
        gain_ref[...] = jnp.sum(grad_normed * middle * scale, axis=0, keepdims=True)

    grad_middle = norm_back(grad_normed * gains_ref[1:2], middle, scale)
    grad_middle += outer_ref[0, 0].astype(jnp.float32)
    grad_middle_ref[0] = grad_middle
    branch_ref[0] = grad_middle.astype(jnp.bfloat16)


def ff_kernel(
    own_ref, swap_ref, pair_ref, other_ref, weights_ref, down_ref,
    hidden_ref, grad_gate_ref, grad_up_ref, keep_ref, sent_ref,
):
    slot = pl.program_id(0)
    units = down_ref.shape[0]
    normed = pick(slot, own_ref[0], swap_ref[0])
    outer = pick(slot, pair_ref[0, 0], other_ref[0, 0])
    for start in range(0, units, CHUNK):
        lanes = slice(start, min(start + CHUNK, units))
        up_lanes = slice(units + lanes.start, units + lanes.stop)
        gate = jnp.dot(normed, weights_ref[:, lanes], preferred_element_type=jnp.float32)
        up = jnp.dot(normed, weights_ref[:, up_lanes], preferred_element_type=jnp.float32)
        grad = contract_cols(outer, down_ref[lanes, :])
        sigmoid = jax.nn.sigmoid(gate)
        silu = gate * sigmoid
        hidden_ref[0, :, lanes] = (silu * up).astype(jnp.bfloat16)
        grad_gate = grad * up * sigmoid * (1.0 + gate * (1.0 - sigmoid))
        grad_gate_ref[0, :, lanes] = grad_gate.astype(jnp.bfloat16)
        grad_up_ref[0, :, lanes] = (grad * silu).astype(jnp.bfloat16)
    term = contract_cols(grad_gate_ref[0], weights_ref[:, :units])
    term += contract_cols(grad_up_ref[0], weights_ref[:, units : 2 * units])
    store_pair(slot, term, keep_ref, sent_ref)


def ff_grads_kernel(
    own_ref, swap_ref, pair_ref, other_ref, hidden_ref, grad_gate_ref, grad_up_ref,
    pack_ref,
    gate_total, up_total, down_total,
):
    slot = pl.program_id(0)
    width, units = gate_total.shape
    each = units // PLANE
    block = width // PLANE
    rest = each - block
    normed = pick(slot, own_ref[0], swap_ref[0])
    outer = pick(slot, pair_ref[0, 0], other_ref[0, 0])

    @pl.when(slot == 0)
    def _():
        gate_total[...] = jnp.zeros_like(gate_total)
        up_total[...] = jnp.zeros_like(up_total)
        down_total[...] = jnp.zeros_like(down_total)

    gate_total[...] += contract_rows(normed, grad_gate_ref[0])
    up_total[...] += contract_rows(normed, grad_up_ref[0])
    down_total[...] += contract_rows(hidden_ref[0], outer)

    @pl.when(slot == 3)
    def _():
        pack_ref[:, :units] = gate_total[...].astype(jnp.bfloat16)
        pack_ref[:, units : 2 * units] = up_total[...].astype(jnp.bfloat16)
        for plane in range(PLANE):
            start = plane * each
            for half in range(2):
                to = half * width // 2 + plane * block // 2
                pack_ref[to : to + block // 2, 2 * units : 2 * units + width] = down_total[
                    start + half * block // 2 : start + (half + 1) * block // 2
                ].astype(jnp.bfloat16)
                parts = block // rest // 2
                lanes = width * rest // block
                last = down_total[start + block : start + each]
                pieces = [
                    last[:, (half * parts + part) * lanes : (half * parts + part + 1) * lanes]
                    for part in range(parts)
                ]
                pack_ref[to : to + block // 2, 2 * units + width :] = jnp.concatenate(
                    pieces, 0
                ).astype(jnp.bfloat16)


def gated_back_kernel(
    own_ref, swap_ref, out_ref, convolved_ref, out_gate_ref, grad_out_ref, grad_conv_ref
):
    slot = pl.program_id(0)
    grad_gated = contract_cols(pick(slot, own_ref[0], swap_ref[0]), out_ref[...])
    grad_out_ref[0] = (grad_gated * convolved_ref[0]).astype(jnp.bfloat16)
    grad_conv_ref[0] = grad_gated * out_gate_ref[0]


def out_grads_kernel(
    own_ref, swap_ref, gated_ref, grad_conv_ref, mixed_ref, earlier_ref, gain_ref,
    part_ref, spare_ref,
    total, taps_rows, gain_rows,
):
    slot = pl.program_id(0)
    rows = spare_ref.shape[1] // 4
    channels = gated_ref.shape[2]

    @pl.when(slot == 0)
    def _():
        total[...] = jnp.zeros_like(total)
        taps_rows[...] = jnp.zeros_like(taps_rows)
        gain_rows[...] = jnp.zeros_like(gain_rows)
        gain_rows[1:2] = gain_ref[...]

    total[...] += contract_rows(gated_ref[0], pick(slot, own_ref[0], swap_ref[0]))
    grad_conv = grad_conv_ref[0]
    mixed = mixed_ref[0].astype(jnp.float32)
    earlier = earlier_ref[0]
    lagged = (mixed, shifted_in(mixed, earlier, 1), shifted_in(mixed, earlier, 2))
    for lag, value in enumerate(lagged):
        taps_rows[2 + lag : 3 + lag] += jnp.sum(grad_conv * value, axis=0, keepdims=True)

    @pl.when(slot == 3)
    def _():
        gain_column = gain_rows[...].T
        taps_column = taps_rows[...].T
        for plane in range(PLANE):
            at = slice(plane * rows, (plane + 1) * rows)
            for part in range(4):
                part_ref[plane, part * rows : (part + 1) * rows, :] = total[
                    at, part * channels : (part + 1) * channels
                ].astype(jnp.bfloat16)
            for z in range(2):
                start = (z * PLANE + plane) * 2 * rows
                spare_ref[plane, z * 2 * rows : (z + 1) * 2 * rows, :] = gain_column[
                    start : start + 2 * rows
                ]
            spare_ref[plane, :rows, :] += taps_column[at]


def project_back_kernel(
    grad_conv_ref, later_ref, proj_ref, grad_out_ref, normed_ref, in_ref, taps_ref,
    pair_ref, other_ref, part_ref, spare_ref,
    pack_ref, keep_ref, sent_ref,
    total, gain_rows,
):
    slot = pl.program_id(0)
    width = in_ref.shape[1]
    channels = width // 3
    rows = channels // PLANE

    @pl.when(slot == 0)
    def _():
        total[...] = jnp.zeros_like(total)
        gain_rows[...] = jnp.zeros_like(gain_rows)

    grad_conv, later = grad_conv_ref[0], later_ref[0]
    grad_mixed = (
        taps_ref[2:3] * grad_conv
        + taps_ref[3:4] * shifted_out(grad_conv, later, 1)
        + taps_ref[4:5] * shifted_out(grad_conv, later, 2)
    )
    grad_projected = jnp.concatenate(
        [
            (grad_mixed * proj_ref[0, :, 2 * channels :]).astype(jnp.bfloat16),
            grad_out_ref[0],
            (grad_mixed * proj_ref[0, :, :channels]).astype(jnp.bfloat16),
        ],
        1,
    )
    total[...] += contract_rows(normed_ref[0], grad_projected)
    grad_normed = contract_cols(grad_projected, in_ref[...])
    store_pair(slot, grad_normed, keep_ref, sent_ref)
    values = pick(slot, pair_ref[0, 0], other_ref[0, 0]).astype(jnp.float32)
    gain_rows[0:1] += jnp.sum(grad_normed * values * norm_scale(values), axis=0, keepdims=True)

    @pl.when(slot == 3)
    def _():
        gain_column = gain_rows[...].T
        for plane in range(PLANE):
            for z in range(2):
                start = (z * PLANE + plane) * 2 * rows
                to = slice(z * 2 * rows, (z + 1) * 2 * rows)
                pack_ref[plane, to, :width] = total[start : start + 2 * rows].astype(jnp.bfloat16)
                pack_ref[plane, to, width + channels :] = (
                    spare_ref[plane, to] + gain_column[start : start + 2 * rows]
                ).astype(jnp.bfloat16)
            pack_ref[plane, :, width : width + channels] = part_ref[plane]


def in_total_kernel(blocks_ref, total_ref, spare_ref):
    members, rows, width = blocks_ref.shape
    channels = total_ref.shape[1] // 12
    first = width - SPARE - 3 * channels
    unit = channels // PLANE
    source = lax.broadcasted_iota(jnp.int32, (channels, 2 * channels), 0)
    target = lax.broadcasted_iota(jnp.int32, (channels, 2 * channels), 1)
    for z in range(2):
        for part in range(3):
            total = jnp.zeros((rows, 2 * channels), jnp.float32)
            for core in range(2):
                placed = source // unit * (2 * unit) + core * unit + source % unit == target
                placed = placed.astype(jnp.float32).astype(jnp.bfloat16)
                for rep in range(2):
                    block = blocks_ref[rep * 4 + z * 2 + core]
                    total += jnp.dot(
                        block[:, first + part * channels : first + (part + 1) * channels],
                        placed,
                        preferred_element_type=jnp.float32,
                    )
            start = (part * 2 + z) * 2 * channels
            total_ref[:, start : start + 2 * channels] = total
    spare = jnp.zeros((rows, SPARE), jnp.float32)
    for member in range(members):
        spare += blocks_ref[member, :, width - SPARE :].astype(jnp.float32)
    spare_ref[...] = spare


def body(
    tokens, gain_first, w_in, conv_weight, w_out, gain_second, w_gate, w_up, w_down, cotangent
):
    low, wide = jnp.bfloat16, jnp.float32
    length, model_width = tokens.shape
    position = lax.axis_index("fsdp")
    core, plane, z = position % 2, position // 2 % PLANE, position // HALF
    rows = w_in.shape[0]
    channels = model_width // 4

    block = 4 * rows
    rest = w_down.shape[0] - block
    units = w_down.shape[0] * PLANE
    gains = jnp.pad(jnp.stack([gain_first, gain_second], 1), ((0, 0), (0, SPARE - 2)))
    gains = jnp.broadcast_to(gains, (4, rows, SPARE))
    swapped = team_swap(
        jnp.concatenate(
            [by_member(w_gate, 1), by_member(w_up, 1), by_member(w_in, 3), gains], 2
        )
    )
    down_main = w_down[:block].reshape(4, rows, model_width)
    down_rest = w_down[block:].reshape(rest, block // rest, -1).transpose(1, 0, 2)
    ff_all = gather_rows(
        jnp.concatenate(
            [swapped[:, :, : 2 * units], down_main, down_rest.reshape(4, rows, -1)], 2
        )
    )

    in_width = 3 * channels
    conv_lanes = jnp.pad(conv_weight, ((0, 0), (2, SPARE - 5)))
    first_pack = jnp.concatenate(
        [
            swapped[:, :, 2 * units : 2 * units + in_width],
            w_out.reshape(rows, 4, channels).transpose(1, 0, 2),
            swapped[:, :, 2 * units + in_width :] + conv_lanes,
        ],
        2,
    )
    first_all = plane_swap(jnp.broadcast_to(first_pack, (PLANE,) + first_pack.shape))
    first_all = first_all.reshape(PLANE, 4 * rows, -1)

    main_rows = ff_all[:, 2 * units : 2 * units + model_width].reshape(2, PLANE, 2 * rows, -1)
    main_rows = main_rows.transpose(1, 0, 2, 3).reshape(PLANE, block, model_width)
    rest_rows = ff_all[:, 2 * units + model_width :].reshape(2, PLANE, 2 * rows, -1)
    rest_rows = rest_rows.transpose(1, 0, 2, 3).reshape(PLANE, block // rest, rest, -1)
    rest_rows = rest_rows.transpose(0, 2, 1, 3).reshape(PLANE, rest, model_width)
    down_full = jnp.concatenate([main_rows, rest_rows], 1).reshape(units, model_width)

    pair = jnp.stack([tokens, cotangent])
    pair = jnp.stack([pair, to_z(pair)])
    other = to_core(pair)
    team_pairs = [pair_of_values(length, model_width, 0)] * 2
    outer_pairs = [pair_of_values(length, model_width, 1)] * 2
    slot_wide, slot_narrow = (4, length, model_width), (4, length, channels)
    pair_wide = (2, length, model_width)
    pairs = [per_pair(length, model_width)] * 2
    narrow = per_slot(length, channels)
    out_gate = per_slot(length, channels, 1)
    edge, edge_after = per_slot(EDGE, channels), per_slot(8, channels)
    out_matrix, in_matrix = whole(channels, model_width), whole(model_width, in_width)
    taps = whole(8, channels)

    normed, projected, mixed, in_full, out_full, gains, kernel = run(
        project_kernel,
        (4,),
        team_pairs + [whole(*first_all.shape)],
        [
            per_slot(length, model_width),
            per_slot(length, in_width),
            narrow,
            in_matrix,
            out_matrix,
            whole(8, model_width),
            taps,
        ],
        [
            array(slot_wide, low),
            array((4, length, in_width), wide),
            array(slot_narrow, low),
            array((model_width, in_width), low),
            array((channels, model_width), low),
            array((8, model_width), wide),
            array((8, channels), wide),
        ],
        [pltpu.VMEM((model_width, SPARE), wide), pltpu.VMEM((channels, SPARE), wide)],
        24,
        4,
        [pair, other, first_all],
    )

    def by_core(first, second):
        return jnp.where(core == 0, first, second)

    tails = mixed[:, length - 2 :]
    sent = by_core(tails[1::2], tails[0::2])
    received = lax.ppermute(sent, "fsdp", TO_NEXT)
    nothing = jnp.zeros_like(received[0])
    shifted = jnp.where(
        z == 0, jnp.stack([nothing, received[0]]), jnp.stack([received[1], nothing])
    )
    before = jnp.where(plane == 0, shifted, received)
    own_before = by_core(before, tails[1::2])
    other_before = by_core(tails[0::2], before)
    earlier = jnp.stack([own_before[0], other_before[0], own_before[1], other_before[1]])
    earlier = jnp.pad(earlier.astype(wide), ((0, 0), (EDGE - 2, 0), (0, 0)))
    convolved, gated, branch_keep, branch_sent = run(
        branch_kernel,
        (4,),
        [narrow, edge, out_gate, taps, out_matrix],
        [narrow, narrow] + pairs,
        [
            array(slot_narrow, wide),
            array(slot_narrow, low),
            array(pair_wide, wide),
            array(pair_wide, low),
        ],
        [],
        16,
        2,
        [mixed, earlier, projected, kernel, out_full],
    )
    branch_pair = core_sum(branch_keep, branch_sent)
    branch_other = to_z(branch_pair.astype(low))
    branch_other, down_full = lax.optimization_barrier((branch_other, down_full))
    one = pl.BlockSpec((1, length, model_width), lambda index: (index, 0, 0))
    crossed = pl.BlockSpec((1, length, model_width), lambda index: (1 - index, 0, 0))
    tokens_one, outer_one = (
        pl.BlockSpec((1, 1, length, model_width), lambda index, which=which: (index, which, 0, 0))
        for which in range(2)
    )
    gain_rows = whole(8, model_width)
    middle, normed_two = run(
        middle_kernel,
        (2,),
        [tokens_one, one, crossed, gain_rows],
        [one, one],
        [array(pair_wide, wide), array(pair_wide, low)],
        [],
        20,
        3,
        [pair, branch_pair, branch_other, gains],
    )
    normed_swap = to_core(normed_two)

    unit_slot = per_slot(length, units)
    unit_shape = array((4, length, units), low)
    hidden, grad_gate, grad_upper, grad_keep, grad_sent = run(
        ff_kernel,
        (4,),
        pairs
        + outer_pairs
        + [whole(*ff_all.shape), whole(units, model_width)],
        [unit_slot] * 3 + pairs,
        [unit_shape] * 3 + [array(pair_wide, wide), array(pair_wide, low)],
        [],
        40,
        21,
        [normed_two, normed_swap, pair, other, ff_all, down_full],
    )
    grad_pair = core_sum(grad_keep, grad_sent)
    grad_sent = grad_pair.astype(low)
    grad_other = to_z(grad_sent)

    (ff_grads,) = run(
        ff_grads_kernel,
        (4,),
        pairs + outer_pairs + [unit_slot] * 3,
        [whole(*ff_all.shape)],
        [array(ff_all.shape, low)],
        [
            pltpu.VMEM((model_width, units), wide),
            pltpu.VMEM((model_width, units), wide),
            pltpu.VMEM((units, model_width), wide),
        ],
        44,
        16,
        [normed_two, normed_swap, pair, other, hidden, grad_gate, grad_upper],
    )
    ff_share = scatter_rows(ff_grads)
    down_term = jnp.dot(
        hidden.reshape(4 * length, units), down_full, preferred_element_type=wide
    ).reshape(4, length, model_width)
    grad_other, ff_grads, down_term = lax.optimization_barrier((grad_other, ff_grads, down_term))
    grad_middle, grad_branch, grad_gain_two = run(
        grad_middle_kernel,
        (2,),
        [one, crossed, one, outer_one, gain_rows],
        [one, one, whole(1, model_width)],
        [array(pair_wide, wide), array(pair_wide, low), array((1, model_width), wide)],
        [],
        24,
        4,
        [grad_pair, grad_other, middle, pair, gains],
    )
    grad_swap = to_core(grad_branch)

    grad_out, grad_conv = run(
        gated_back_kernel,
        (4,),
        pairs + [out_matrix, narrow, out_gate],
        [narrow, narrow],
        [array(slot_narrow, low), array(slot_narrow, wide)],
        [],
        16,
        2,
        [grad_branch, grad_swap, out_full, convolved, projected],
    )
    heads = grad_conv[:, :2]
    sent = by_core(heads[0::2], heads[1::2])
    received = lax.ppermute(sent, "fsdp", TO_PREVIOUS)
    nothing = jnp.zeros_like(received[0])
    shifted = jnp.where(
        z == 0, jnp.stack([received[1], nothing]), jnp.stack([nothing, received[0]])
    )
    after = jnp.where(plane == PLANE - 1, shifted, received)
    own_after = by_core(heads[1::2], after)
    other_after = by_core(after, heads[0::2])
    later = jnp.stack([own_after[0], other_after[0], own_after[1], other_after[1]])
    later = jnp.pad(later, ((0, 0), (0, 6), (0, 0)))
    part_shape, spare_shape = (PLANE, 4 * rows, channels), (PLANE, 4 * rows, SPARE)
    out_part, spare_part = run(
        out_grads_kernel,
        (4,),
        pairs + [narrow, narrow, narrow, edge, whole(1, model_width)],
        [whole(*part_shape), whole(*spare_shape)],
        [array(part_shape, low), array(spare_shape, wide)],
        [
            pltpu.VMEM((channels, model_width), wide),
            pltpu.VMEM((SPARE, channels), wide),
            pltpu.VMEM((SPARE, model_width), wide),
        ],
        20,
        2.5,
        [grad_branch, grad_swap, gated, grad_conv, mixed, earlier, grad_gain_two],
    )
    first_grads, normed_keep, normed_sent = run(
        project_back_kernel,
        (4,),
        [
            narrow,
            edge_after,
            per_slot(length, in_width),
            narrow,
            per_slot(length, model_width),
            in_matrix,
            taps,
        ]
        + team_pairs
        + [whole(*part_shape), whole(*spare_shape)],
        [whole(*first_all.shape)] + pairs,
        [array(first_all.shape, low), array(pair_wide, wide), array(pair_wide, low)],
        [pltpu.VMEM((model_width, in_width), wide), pltpu.VMEM((SPARE, model_width), wide)],
        32,
        8,
        [
            grad_conv,
            later,
            projected,
            grad_out,
            normed,
            in_full,
            kernel,
            pair,
            other,
            out_part,
            spare_part,
        ],
    )
    first_grads = first_grads.reshape(PLANE, 4, rows, -1)
    first_arrived = plane_swap(first_grads)

    down_term, normed_sent = lax.optimization_barrier((down_term, normed_sent))
    result = middle[0] + own_sum(down_term[0::2], down_term[1::2].astype(low))
    grad_normed_own = own_sum(normed_keep, normed_sent)
    inputs = tokens.astype(wide)
    grad_inputs = grad_middle[0] + norm_back(
        grad_normed_own * gains[0], inputs, norm_scale(inputs)
    )
    result, grad_inputs, first_arrived = lax.optimization_barrier(
        (result.astype(low), grad_inputs, first_arrived)
    )
    first_share = jnp.sum(first_arrived.astype(wide), axis=0).astype(low)

    def both_reps(value):
        other = lax.ppermute(value, "rep", [(0, 1), (1, 0)])
        return value.astype(wide) + other.astype(wide)

    blocks = jnp.concatenate(
        [
            ff_share[:, :, : 2 * units],
            first_share[:, :, :in_width],
            first_share[:, :, in_width + channels :],
        ],
        2,
    )
    blocks = lax.all_to_all(
        jnp.concatenate([blocks, blocks]),
        ("rep", "fsdp"),
        0,
        0,
        tiled=True,
        axis_index_groups=BOTH_TEAMS,
    )
    owned = jnp.concatenate([ff_share[:, :, 2 * units :], first_share[:, :, in_width:]], 2)
    owned, blocks = lax.optimization_barrier((owned, blocks))
    owned = both_reps(owned)
    down_total, out_total = owned[:, :, : model_width + SPARE], owned[:, :, model_width + SPARE :]
    down_rest = down_total[:, :, model_width:].reshape(block // rest, rest, -1)
    down_rest = down_rest.transpose(1, 0, 2).reshape(rest, model_width)
    down_total = jnp.concatenate(
        [down_total[:, :, :model_width].reshape(block, model_width), down_rest], 0
    )
    conv_total = out_total[0, :, channels + 2 : channels + 5]
    out_total = out_total[:, :, :channels].transpose(1, 0, 2).reshape(rows, model_width)
    in_total, gain_total = run(
        in_total_kernel,
        (1,),
        [whole(*blocks.shape)],
        [whole(rows, w_in.shape[1]), whole(rows, SPARE)],
        [array((rows, w_in.shape[1]), wide), array((rows, SPARE), wide)],
        [],
        16,
        2,
        [blocks],
    )
    ff_total = blocks[:, :, : 2 * units].astype(wide)
    ff_total = ff_total[:4] + ff_total[4:]

    return (
        result,
        grad_inputs,
        gain_total[:, 0],
        in_total,
        conv_total,
        out_total,
        gain_total[:, 1],
        from_members(ff_total[:, :, :units], 1),
        from_members(ff_total[:, :, units:], 1),
        down_total,
    )


def solution(mesh):
    return jax.shard_map(
        body,
        mesh=mesh,
        in_specs=(
            P(("rep", "fsdp"), None),
            P("fsdp"),
            P("fsdp", None),
            P("fsdp", None),
            P("fsdp", None),
            P("fsdp"),
            P("fsdp", None),
            P("fsdp", None),
            P("fsdp", None),
            P(("rep", "fsdp"), None),
        ),
        out_specs=(
            P(("rep", "fsdp"), None),
            P(("rep", "fsdp"), None),
            P("fsdp"),
            P("fsdp", None),
            P("fsdp", None),
            P("fsdp", None),
            P("fsdp"),
            P("fsdp", None),
            P("fsdp", None),
            P("fsdp", None),
        ),
        check_vma=False,
    )
```

```python
import jax
import jax.numpy as jnp
from jax import lax
from jax.experimental import pallas as pl
from jax.experimental.pallas import tpu as pltpu
from jax.sharding import PartitionSpec as P

epsilon = 1e-05

SIDE = 4
PLANE = SIDE * SIDE
HALF = PLANE * 2
SPARE = 128
EDGE = 8
CHUNK = 256
MIB = 1024 * 1024


def place(z, plane, core):
    return (z * PLANE + plane) * 2 + core


def moves(target):
    return [
        (place(z, plane, core), place(*target(z, plane, core)))
        for z in range(2)
        for plane in range(PLANE)
        for core in range(2)
    ]


TO_CORE = moves(lambda z, plane, core: (z, plane, 1 - core))
TO_Z = moves(lambda z, plane, core: (1 - z, plane, core))
TO_NEXT = moves(lambda z, plane, core: (z, (plane + 1) % PLANE, core))
TO_PREVIOUS = moves(lambda z, plane, core: (z, (plane - 1) % PLANE, core))
TEAMS = [
    [place(z, plane, core) for z in range(2) for core in range(2)] for plane in range(PLANE)
]
PLANES = [
    [place(z, plane, core) for plane in range(PLANE)] for z in range(2) for core in range(2)
]
BOTH_TEAMS = [[rep * 2 * HALF + member for rep in range(2) for member in team] for team in TEAMS]


def to_core(value):
    return lax.ppermute(value, "fsdp", TO_CORE)


def to_z(value):
    return lax.ppermute(value, "fsdp", TO_Z)


def norm_scale(values):
    return lax.rsqrt(jnp.mean(values * values, axis=-1, keepdims=True) + epsilon)


def norm_back(grad_normed, values, scale):
    inner = jnp.mean(grad_normed * values, axis=-1, keepdims=True)
    return scale * (grad_normed - values * scale * scale * inner)


def contract_rows(left, right):
    return lax.dot_general(
        left, right, (((0,), (0,)), ((), ())), preferred_element_type=jnp.float32
    )


def contract_cols(left, right):
    return lax.dot_general(
        left, right, (((1,), (1,)), ((), ())), preferred_element_type=jnp.float32
    )


def by_member(shard, parts):
    rows, columns = shard.shape
    split = shard.reshape(rows, parts, 2, PLANE, 2, -1)
    return split.transpose(2, 4, 0, 1, 3, 5).reshape(4, rows, columns // 4)


def from_members(blocks, parts):
    members, rows, columns = blocks.shape
    split = blocks.reshape(2, 2, rows, parts, PLANE, -1)
    return split.transpose(2, 3, 0, 4, 1, 5).reshape(rows, 4 * columns)


def team_swap(blocks):
    return lax.all_to_all(blocks, "fsdp", 0, 0, tiled=True, axis_index_groups=TEAMS)


def plane_swap(blocks):
    return lax.all_to_all(blocks, "fsdp", 0, 0, tiled=True, axis_index_groups=PLANES)


def gather_rows(blocks):
    members, rows, columns = blocks.shape
    return lax.all_gather(
        blocks.reshape(2, 2 * rows, columns),
        "fsdp",
        axis=1,
        tiled=True,
        axis_index_groups=PLANES,
    ).reshape(-1, columns)


def scatter_rows(value):
    total, columns = value.shape
    return lax.psum_scatter(
        value.reshape(2, total // 2, columns),
        "fsdp",
        scatter_dimension=1,
        tiled=True,
        axis_index_groups=PLANES,
    ).reshape(4, -1, columns)


def core_sum(keep, sent):
    return keep + to_core(sent).astype(jnp.float32)


def own_sum(keep, sent):
    pair = core_sum(keep, sent)
    return pair[0] + to_z(pair[1].astype(jnp.bfloat16)).astype(jnp.float32)


def whole(*shape):
    return pl.BlockSpec(shape, lambda *_: (0,) * len(shape), pipeline_mode=pl.Buffered(1))


def per_slot(length, width, column=0):
    return pl.BlockSpec((1, length, width), lambda slot: (slot, 0, column))


def per_pair(length, width):
    return pl.BlockSpec((1, length, width), lambda slot: (slot // 2, 0, 0))


def pair_of_values(length, width, which):
    return pl.BlockSpec((1, 1, length, width), lambda slot: (slot // 2, which, 0, 0))


def run(kernel, grid, in_specs, out_specs, out_shape, scratch, room, busy, values):
    return pl.pallas_call(
        kernel,
        grid=grid,
        in_specs=in_specs,
        out_specs=out_specs,
        out_shape=out_shape,
        scratch_shapes=scratch,
        compiler_params=pltpu.CompilerParams(vmem_limit_bytes=room * MIB),
        cost_estimate=pl.CostEstimate(
            flops=int(busy * 1.15e9), bytes_accessed=0, transcendentals=0
        ),
    )(*values)


def array(shape, kind):
    return jax.ShapeDtypeStruct(shape, kind)


def pick(slot, even, odd):
    return jnp.where(slot % 2 == 0, even, odd)


def shifted_in(values, rows_before, steps):
    moved = pltpu.roll(values, steps, 0)
    row = lax.broadcasted_iota(jnp.int32, values.shape, 0)
    for index in range(steps):
        at = EDGE - steps + index
        moved = jnp.where(row == index, rows_before[at : at + 1], moved)
    return moved


def shifted_out(values, next_rows, steps):
    length = values.shape[0]
    moved = pltpu.roll(values, length - steps, 0)
    row = lax.broadcasted_iota(jnp.int32, values.shape, 0)
    for index in range(steps):
        moved = jnp.where(row == length - steps + index, next_rows[index : index + 1], moved)
    return moved


def store_pair(slot, value, keep_ref, sent_ref):
    @pl.when(slot % 2 == 0)
    def _():
        keep_ref[0] = value

    @pl.when(slot % 2 == 1)
    def _():
        sent_ref[0] = value.astype(sent_ref.dtype)


def project_kernel(
    pair_ref, other_ref, first_ref,
    normed_ref, proj_ref, mixed_ref, in_ref, out_ref, gains_ref, taps_ref,
    column, taps_column,
):
    slot = pl.program_id(0)
    width = in_ref.shape[1]
    channels = width // 3
    rows = channels // PLANE

    @pl.when(slot == 0)
    def _():
        for plane in range(PLANE):
            for z in range(2):
                at = pl.ds((z * PLANE + plane) * 2 * rows, 2 * rows)
                source = pl.ds(z * 2 * rows, 2 * rows)
                in_ref[at, :] = first_ref[plane, source, :width]
                column[at, :] = first_ref[plane, source, width + channels :].astype(jnp.float32)
            at = pl.ds(plane * rows, rows)
            for part in range(4):
                out_ref[at, part * channels : (part + 1) * channels] = first_ref[
                    plane, pl.ds(part * rows, rows), width : width + channels
                ]
            taps_column[at, :] = first_ref[plane, :rows, width + channels :].astype(jnp.float32)
        gains_ref[...] = column[...].T[:8]
        taps_ref[...] = taps_column[...].T[:8]

    values = pick(slot, pair_ref[0, 0], other_ref[0, 0]).astype(jnp.float32)
    normed = (values * norm_scale(values) * gains_ref[0:1]).astype(jnp.bfloat16)
    normed_ref[0] = normed
    projected = jnp.dot(normed, in_ref[...], preferred_element_type=jnp.float32)
    proj_ref[0] = projected
    mixed = projected[:, :channels] * projected[:, 2 * channels :]
    mixed_ref[0] = mixed.astype(jnp.bfloat16)


def branch_kernel(
    mixed_ref, earlier_ref, out_gate_ref, taps_ref, out_ref,
    convolved_ref, gated_ref, keep_ref, sent_ref,
):
    slot = pl.program_id(0)
    mixed = mixed_ref[0].astype(jnp.float32)
    earlier = earlier_ref[0]
    convolved = (
        taps_ref[2:3] * mixed
        + taps_ref[3:4] * shifted_in(mixed, earlier, 1)
        + taps_ref[4:5] * shifted_in(mixed, earlier, 2)
    )
    convolved_ref[0] = convolved
    gated = (out_gate_ref[0] * convolved).astype(jnp.bfloat16)
    gated_ref[0] = gated
    branch = jnp.dot(gated, out_ref[...], preferred_element_type=jnp.float32)
    store_pair(slot, branch, keep_ref, sent_ref)


def middle_kernel(inputs_ref, branch_ref, crossed_ref, gains_ref, middle_ref, normed_ref):
    middle = inputs_ref[0, 0].astype(jnp.float32) + branch_ref[0]
    middle += crossed_ref[0].astype(jnp.float32)
    middle_ref[0] = middle
    normed_ref[0] = (middle * norm_scale(middle) * gains_ref[1:2]).astype(jnp.bfloat16)


def grad_middle_kernel(
    grad_ref, crossed_ref, middle_ref, outer_ref, gains_ref,
    grad_middle_ref, branch_ref, gain_ref,
):
    grad_normed = grad_ref[0] + crossed_ref[0].astype(jnp.float32)
    middle = middle_ref[0]
    scale = norm_scale(middle)

    @pl.when(pl.program_id(0) == 0)
    def _():
        gain_ref[...] = jnp.sum(grad_normed * middle * scale, axis=0, keepdims=True)

    grad_middle = norm_back(grad_normed * gains_ref[1:2], middle, scale)
    grad_middle += outer_ref[0, 0].astype(jnp.float32)
    grad_middle_ref[0] = grad_middle
    branch_ref[0] = grad_middle.astype(jnp.bfloat16)


def ff_kernel(
    own_ref, swap_ref, pair_ref, other_ref, weights_ref, down_ref,
    hidden_ref, grad_gate_ref, grad_up_ref, keep_ref, sent_ref,
):
    units, width = down_ref.shape
    length = own_ref.shape[1]
    normed = jnp.concatenate([own_ref[0], swap_ref[0]], 0)
    outer = jnp.concatenate([pair_ref[0, 0], other_ref[0, 0]], 0)
    for start in range(0, units, CHUNK):
        lanes = slice(start, min(start + CHUNK, units))
        up_lanes = slice(units + lanes.start, units + lanes.stop)
        shape = (2, length, lanes.stop - lanes.start)
        gate = jnp.dot(normed, weights_ref[:, lanes], preferred_element_type=jnp.float32)
        up = jnp.dot(normed, weights_ref[:, up_lanes], preferred_element_type=jnp.float32)
        grad = contract_cols(outer, down_ref[lanes, :])
        sigmoid = jax.nn.sigmoid(gate)
        silu = gate * sigmoid
        hidden_ref[:, :, lanes] = (silu * up).astype(jnp.bfloat16).reshape(shape)
        grad_gate = grad * up * sigmoid * (1.0 + gate * (1.0 - sigmoid))
        grad_gate_ref[:, :, lanes] = grad_gate.astype(jnp.bfloat16).reshape(shape)
        grad_up_ref[:, :, lanes] = (grad * silu).astype(jnp.bfloat16).reshape(shape)
    grad_gate = grad_gate_ref[...].reshape(2 * length, units)
    grad_up = grad_up_ref[...].reshape(2 * length, units)
    term = contract_cols(grad_gate, weights_ref[:, :units])
    term += contract_cols(grad_up, weights_ref[:, units : 2 * units])
    keep_ref[0] = term[:length]
    sent_ref[0] = term[length:].astype(jnp.bfloat16)


def ff_grads_kernel(
    own_ref, swap_ref, pair_ref, other_ref, hidden_ref, grad_gate_ref, grad_up_ref,
    pack_ref,
    gate_total, up_total, down_total,
):
    step = pl.program_id(0)
    width, units = gate_total.shape
    each = units // PLANE
    block = width // PLANE
    rest = each - block
    tokens = 2 * own_ref.shape[1]
    normed = jnp.concatenate([own_ref[0], swap_ref[0]], 0)
    outer = jnp.concatenate([pair_ref[0, 0], other_ref[0, 0]], 0)

    def gate_term():
        return contract_rows(normed, grad_gate_ref[...].reshape(tokens, units))

    def up_term():
        return contract_rows(normed, grad_up_ref[...].reshape(tokens, units))

    def down_term():
        return contract_rows(hidden_ref[...].reshape(tokens, units), outer)

    @pl.when(step == 0)
    def _():
        gate_total[...] = gate_term()
        up_total[...] = up_term()
        down_total[...] = down_term()

    @pl.when(step == 1)
    def _():
        pack_ref[:, :units] = (gate_total[...] + gate_term()).astype(jnp.bfloat16)
        pack_ref[:, units : 2 * units] = (up_total[...] + up_term()).astype(jnp.bfloat16)
        down_total[...] += down_term()
        for plane in range(PLANE):
            start = plane * each
            for half in range(2):
                to = half * width // 2 + plane * block // 2
                pack_ref[to : to + block // 2, 2 * units : 2 * units + width] = down_total[
                    start + half * block // 2 : start + (half + 1) * block // 2
                ].astype(jnp.bfloat16)
                parts = block // rest // 2
                lanes = width * rest // block
                last = down_total[start + block : start + each]
                pieces = [
                    last[:, (half * parts + part) * lanes : (half * parts + part + 1) * lanes]
                    for part in range(parts)
                ]
                pack_ref[to : to + block // 2, 2 * units + width :] = jnp.concatenate(
                    pieces, 0
                ).astype(jnp.bfloat16)


def gated_back_kernel(
    own_ref, swap_ref, out_ref, convolved_ref, out_gate_ref, grad_out_ref, grad_conv_ref
):
    slot = pl.program_id(0)
    grad_gated = contract_cols(pick(slot, own_ref[0], swap_ref[0]), out_ref[...])
    grad_out_ref[0] = (grad_gated * convolved_ref[0]).astype(jnp.bfloat16)
    grad_conv_ref[0] = grad_gated * out_gate_ref[0]


def out_grads_kernel(
    own_ref, swap_ref, gated_ref, grad_conv_ref, mixed_ref, earlier_ref, gain_ref,
    part_ref, spare_ref,
    total, taps_rows, gain_rows,
):
    slot = pl.program_id(0)
    rows = spare_ref.shape[1] // 4
    channels = gated_ref.shape[2]

    @pl.when(slot == 0)
    def _():
        total[...] = jnp.zeros_like(total)
        taps_rows[...] = jnp.zeros_like(taps_rows)
        gain_rows[...] = jnp.zeros_like(gain_rows)
        gain_rows[1:2] = gain_ref[...]

    total[...] += contract_rows(gated_ref[0], pick(slot, own_ref[0], swap_ref[0]))
    grad_conv = grad_conv_ref[0]
    mixed = mixed_ref[0].astype(jnp.float32)
    earlier = earlier_ref[0]
    lagged = (mixed, shifted_in(mixed, earlier, 1), shifted_in(mixed, earlier, 2))
    for lag, value in enumerate(lagged):
        taps_rows[2 + lag : 3 + lag] += jnp.sum(grad_conv * value, axis=0, keepdims=True)

    @pl.when(slot == 3)
    def _():
        gain_column = gain_rows[...].T
        taps_column = taps_rows[...].T
        for plane in range(PLANE):
            at = slice(plane * rows, (plane + 1) * rows)
            for part in range(4):
                part_ref[plane, part * rows : (part + 1) * rows, :] = total[
                    at, part * channels : (part + 1) * channels
                ].astype(jnp.bfloat16)
            for z in range(2):
                start = (z * PLANE + plane) * 2 * rows
                spare_ref[plane, z * 2 * rows : (z + 1) * 2 * rows, :] = gain_column[
                    start : start + 2 * rows
                ]
            spare_ref[plane, :rows, :] += taps_column[at]


def project_back_kernel(
    grad_conv_ref, later_ref, proj_ref, grad_out_ref, normed_ref, in_ref, taps_ref,
    pair_ref, other_ref, part_ref, spare_ref,
    pack_ref, keep_ref, sent_ref,
    total, gain_rows,
):
    slot = pl.program_id(0)
    width = in_ref.shape[1]
    channels = width // 3
    rows = channels // PLANE

    @pl.when(slot == 0)
    def _():
        total[...] = jnp.zeros_like(total)
        gain_rows[...] = jnp.zeros_like(gain_rows)

    grad_conv, later = grad_conv_ref[0], later_ref[0]
    grad_mixed = (
        taps_ref[2:3] * grad_conv
        + taps_ref[3:4] * shifted_out(grad_conv, later, 1)
        + taps_ref[4:5] * shifted_out(grad_conv, later, 2)
    )
    grad_projected = jnp.concatenate(
        [
            (grad_mixed * proj_ref[0, :, 2 * channels :]).astype(jnp.bfloat16),
            grad_out_ref[0],
            (grad_mixed * proj_ref[0, :, :channels]).astype(jnp.bfloat16),
        ],
        1,
    )
    total[...] += contract_rows(normed_ref[0], grad_projected)
    grad_normed = contract_cols(grad_projected, in_ref[...])
    store_pair(slot, grad_normed, keep_ref, sent_ref)
    values = pick(slot, pair_ref[0, 0], other_ref[0, 0]).astype(jnp.float32)
    gain_rows[0:1] += jnp.sum(grad_normed * values * norm_scale(values), axis=0, keepdims=True)

    @pl.when(slot == 3)
    def _():
        gain_column = gain_rows[...].T
        for plane in range(PLANE):
            for z in range(2):
                start = (z * PLANE + plane) * 2 * rows
                to = slice(z * 2 * rows, (z + 1) * 2 * rows)
                pack_ref[plane, to, :width] = total[start : start + 2 * rows].astype(jnp.bfloat16)
                pack_ref[plane, to, width + channels :] = (
                    spare_ref[plane, to] + gain_column[start : start + 2 * rows]
                ).astype(jnp.bfloat16)
            pack_ref[plane, :, width : width + channels] = part_ref[plane]


def in_total_kernel(blocks_ref, total_ref, spare_ref):
    members, rows, width = blocks_ref.shape
    channels = total_ref.shape[1] // 12
    first = width - SPARE - 3 * channels
    unit = channels // PLANE
    source = lax.broadcasted_iota(jnp.int32, (channels, 2 * channels), 0)
    target = lax.broadcasted_iota(jnp.int32, (channels, 2 * channels), 1)
    for z in range(2):
        for part in range(3):
            total = jnp.zeros((rows, 2 * channels), jnp.float32)
            for core in range(2):
                placed = source // unit * (2 * unit) + core * unit + source % unit == target
                placed = placed.astype(jnp.float32).astype(jnp.bfloat16)
                for rep in range(2):
                    block = blocks_ref[rep * 4 + z * 2 + core]
                    total += jnp.dot(
                        block[:, first + part * channels : first + (part + 1) * channels],
                        placed,
                        preferred_element_type=jnp.float32,
                    )
            start = (part * 2 + z) * 2 * channels
            total_ref[:, start : start + 2 * channels] = total
    spare = jnp.zeros((rows, SPARE), jnp.float32)
    for member in range(members):
        spare += blocks_ref[member, :, width - SPARE :].astype(jnp.float32)
    spare_ref[...] = spare


def body(
    tokens, gain_first, w_in, conv_weight, w_out, gain_second, w_gate, w_up, w_down, cotangent
):
    low, wide = jnp.bfloat16, jnp.float32
    length, model_width = tokens.shape
    position = lax.axis_index("fsdp")
    core, plane, z = position % 2, position // 2 % PLANE, position // HALF
    rows = w_in.shape[0]
    channels = model_width // 4

    block = 4 * rows
    rest = w_down.shape[0] - block
    units = w_down.shape[0] * PLANE
    gains = jnp.pad(jnp.stack([gain_first, gain_second], 1), ((0, 0), (0, SPARE - 2)))
    gains = jnp.broadcast_to(gains, (4, rows, SPARE))
    swapped = team_swap(
        jnp.concatenate(
            [by_member(w_gate, 1), by_member(w_up, 1), by_member(w_in, 3), gains], 2
        )
    )
    down_main = w_down[:block].reshape(4, rows, model_width)
    down_rest = w_down[block:].reshape(rest, block // rest, -1).transpose(1, 0, 2)
    ff_all = gather_rows(
        jnp.concatenate(
            [swapped[:, :, : 2 * units], down_main, down_rest.reshape(4, rows, -1)], 2
        )
    )

    in_width = 3 * channels
    conv_lanes = jnp.pad(conv_weight, ((0, 0), (2, SPARE - 5)))
    first_pack = jnp.concatenate(
        [
            swapped[:, :, 2 * units : 2 * units + in_width],
            w_out.reshape(rows, 4, channels).transpose(1, 0, 2),
            swapped[:, :, 2 * units + in_width :] + conv_lanes,
        ],
        2,
    )
    first_all = plane_swap(jnp.broadcast_to(first_pack, (PLANE,) + first_pack.shape))
    first_all = first_all.reshape(PLANE, 4 * rows, -1)

    main_rows = ff_all[:, 2 * units : 2 * units + model_width].reshape(2, PLANE, 2 * rows, -1)
    main_rows = main_rows.transpose(1, 0, 2, 3).reshape(PLANE, block, model_width)
    rest_rows = ff_all[:, 2 * units + model_width :].reshape(2, PLANE, 2 * rows, -1)
    rest_rows = rest_rows.transpose(1, 0, 2, 3).reshape(PLANE, block // rest, rest, -1)
    rest_rows = rest_rows.transpose(0, 2, 1, 3).reshape(PLANE, rest, model_width)
    down_full = jnp.concatenate([main_rows, rest_rows], 1).reshape(units, model_width)

    pair = jnp.stack([tokens, cotangent])
    pair = jnp.stack([pair, to_z(pair)])
    other = to_core(pair)
    team_pairs = [pair_of_values(length, model_width, 0)] * 2
    slot_wide, slot_narrow = (4, length, model_width), (4, length, channels)
    pair_wide = (2, length, model_width)
    pairs = [per_pair(length, model_width)] * 2
    narrow = per_slot(length, channels)
    out_gate = per_slot(length, channels, 1)
    edge, edge_after = per_slot(EDGE, channels), per_slot(8, channels)
    out_matrix, in_matrix = whole(channels, model_width), whole(model_width, in_width)
    taps = whole(8, channels)

    normed, projected, mixed, in_full, out_full, gains, kernel = run(
        project_kernel,
        (4,),
        team_pairs + [whole(*first_all.shape)],
        [
            per_slot(length, model_width),
            per_slot(length, in_width),
            narrow,
            in_matrix,
            out_matrix,
            whole(8, model_width),
            taps,
        ],
        [
            array(slot_wide, low),
            array((4, length, in_width), wide),
            array(slot_narrow, low),
            array((model_width, in_width), low),
            array((channels, model_width), low),
            array((8, model_width), wide),
            array((8, channels), wide),
        ],
        [pltpu.VMEM((model_width, SPARE), wide), pltpu.VMEM((channels, SPARE), wide)],
        24,
        4,
        [pair, other, first_all],
    )

    def by_core(first, second):
        return jnp.where(core == 0, first, second)

    tails = mixed[:, length - 2 :]
    sent = by_core(tails[1::2], tails[0::2])
    received = lax.ppermute(sent, "fsdp", TO_NEXT)
    nothing = jnp.zeros_like(received[0])
    shifted = jnp.where(
        z == 0, jnp.stack([nothing, received[0]]), jnp.stack([received[1], nothing])
    )
    before = jnp.where(plane == 0, shifted, received)
    own_before = by_core(before, tails[1::2])
    other_before = by_core(tails[0::2], before)
    earlier = jnp.stack([own_before[0], other_before[0], own_before[1], other_before[1]])
    earlier = jnp.pad(earlier.astype(wide), ((0, 0), (EDGE - 2, 0), (0, 0)))
    convolved, gated, branch_keep, branch_sent = run(
        branch_kernel,
        (4,),
        [narrow, edge, out_gate, taps, out_matrix],
        [narrow, narrow] + pairs,
        [
            array(slot_narrow, wide),
            array(slot_narrow, low),
            array(pair_wide, wide),
            array(pair_wide, low),
        ],
        [],
        16,
        2,
        [mixed, earlier, projected, kernel, out_full],
    )
    branch_pair = core_sum(branch_keep, branch_sent)
    branch_other = to_z(branch_pair.astype(low))
    branch_other, down_full = lax.optimization_barrier((branch_other, down_full))
    one = pl.BlockSpec((1, length, model_width), lambda index: (index, 0, 0))
    crossed = pl.BlockSpec((1, length, model_width), lambda index: (1 - index, 0, 0))
    tokens_one, outer_one = (
        pl.BlockSpec((1, 1, length, model_width), lambda index, which=which: (index, which, 0, 0))
        for which in range(2)
    )
    gain_rows = whole(8, model_width)
    middle, normed_two = run(
        middle_kernel,
        (2,),
        [tokens_one, one, crossed, gain_rows],
        [one, one],
        [array(pair_wide, wide), array(pair_wide, low)],
        [],
        20,
        3,
        [pair, branch_pair, branch_other, gains],
    )
    normed_swap = to_core(normed_two)

    step_pairs = [pl.BlockSpec((1, length, model_width), lambda step: (step, 0, 0))] * 2
    step_outer = [pl.BlockSpec((1, 1, length, model_width), lambda step: (step, 1, 0, 0))] * 2
    unit_slot = pl.BlockSpec((2, length, units), lambda step: (step, 0, 0))
    unit_shape = array((4, length, units), low)
    hidden, grad_gate, grad_upper, grad_keep, grad_sent = run(
        ff_kernel,
        (2,),
        step_pairs + step_outer + [whole(model_width, 2 * units), whole(units, model_width)],
        [unit_slot] * 3 + step_pairs,
        [unit_shape] * 3 + [array(pair_wide, wide), array(pair_wide, low)],
        [],
        44,
        17,
        [normed_two, normed_swap, pair, other, ff_all, down_full],
    )
    grad_pair = core_sum(grad_keep, grad_sent)
    grad_sent = grad_pair.astype(low)
    grad_other = to_z(grad_sent)

    (ff_grads,) = run(
        ff_grads_kernel,
        (2,),
        step_pairs + step_outer + [unit_slot] * 3,
        [whole(*ff_all.shape)],
        [array(ff_all.shape, low)],
        [
            pltpu.VMEM((model_width, units), wide),
            pltpu.VMEM((model_width, units), wide),
            pltpu.VMEM((units, model_width), wide),
        ],
        54,
        12,
        [normed_two, normed_swap, pair, other, hidden, grad_gate, grad_upper],
    )
    ff_share = scatter_rows(ff_grads)
    down_term = jnp.dot(
        hidden.reshape(4 * length, units), down_full, preferred_element_type=wide
    ).reshape(4, length, model_width)
    grad_other, ff_grads, down_term = lax.optimization_barrier((grad_other, ff_grads, down_term))
    grad_middle, grad_branch, grad_gain_two = run(
        grad_middle_kernel,
        (2,),
        [one, crossed, one, outer_one, gain_rows],
        [one, one, whole(1, model_width)],
        [array(pair_wide, wide), array(pair_wide, low), array((1, model_width), wide)],
        [],
        24,
        4,
        [grad_pair, grad_other, middle, pair, gains],
    )
    grad_swap = to_core(grad_branch)

    grad_out, grad_conv = run(
        gated_back_kernel,
        (4,),
        pairs + [out_matrix, narrow, out_gate],
        [narrow, narrow],
        [array(slot_narrow, low), array(slot_narrow, wide)],
        [],
        16,
        2,
        [grad_branch, grad_swap, out_full, convolved, projected],
    )
    heads = grad_conv[:, :2]
    sent = by_core(heads[0::2], heads[1::2])
    received = lax.ppermute(sent, "fsdp", TO_PREVIOUS)
    nothing = jnp.zeros_like(received[0])
    shifted = jnp.where(
        z == 0, jnp.stack([received[1], nothing]), jnp.stack([nothing, received[0]])
    )
    after = jnp.where(plane == PLANE - 1, shifted, received)
    own_after = by_core(heads[1::2], after)
    other_after = by_core(after, heads[0::2])
    later = jnp.stack([own_after[0], other_after[0], own_after[1], other_after[1]])
    later = jnp.pad(later, ((0, 0), (0, 6), (0, 0)))
    part_shape, spare_shape = (PLANE, 4 * rows, channels), (PLANE, 4 * rows, SPARE)
    out_part, spare_part = run(
        out_grads_kernel,
        (4,),
        pairs + [narrow, narrow, narrow, edge, whole(1, model_width)],
        [whole(*part_shape), whole(*spare_shape)],
        [array(part_shape, low), array(spare_shape, wide)],
        [
            pltpu.VMEM((channels, model_width), wide),
            pltpu.VMEM((SPARE, channels), wide),
            pltpu.VMEM((SPARE, model_width), wide),
        ],
        20,
        2.5,
        [grad_branch, grad_swap, gated, grad_conv, mixed, earlier, grad_gain_two],
    )
    first_grads, normed_keep, normed_sent = run(
        project_back_kernel,
        (4,),
        [
            narrow,
            edge_after,
            per_slot(length, in_width),
            narrow,
            per_slot(length, model_width),
            in_matrix,
            taps,
        ]
        + team_pairs
        + [whole(*part_shape), whole(*spare_shape)],
        [whole(*first_all.shape)] + pairs,
        [array(first_all.shape, low), array(pair_wide, wide), array(pair_wide, low)],
        [pltpu.VMEM((model_width, in_width), wide), pltpu.VMEM((SPARE, model_width), wide)],
        32,
        8,
        [
            grad_conv,
            later,
            projected,
            grad_out,
            normed,
            in_full,
            kernel,
            pair,
            other,
            out_part,
            spare_part,
        ],
    )
    first_grads = first_grads.reshape(PLANE, 4, rows, -1)
    first_arrived = plane_swap(first_grads)

    down_term, normed_sent = lax.optimization_barrier((down_term, normed_sent))
    result = middle[0] + own_sum(down_term[0::2], down_term[1::2].astype(low))
    grad_normed_own = own_sum(normed_keep, normed_sent)
    inputs = tokens.astype(wide)
    grad_inputs = grad_middle[0] + norm_back(
        grad_normed_own * gains[0], inputs, norm_scale(inputs)
    )
    result, grad_inputs, first_arrived = lax.optimization_barrier(
        (result.astype(low), grad_inputs, first_arrived)
    )
    first_share = jnp.sum(first_arrived.astype(wide), axis=0).astype(low)

    def both_reps(value):
        other = lax.ppermute(value, "rep", [(0, 1), (1, 0)])
        return value.astype(wide) + other.astype(wide)

    blocks = jnp.concatenate(
        [
            ff_share[:, :, : 2 * units],
            first_share[:, :, :in_width],
            first_share[:, :, in_width + channels :],
        ],
        2,
    )
    blocks = lax.all_to_all(
        jnp.concatenate([blocks, blocks]),
        ("rep", "fsdp"),
        0,
        0,
        tiled=True,
        axis_index_groups=BOTH_TEAMS,
    )
    owned = jnp.concatenate([ff_share[:, :, 2 * units :], first_share[:, :, in_width:]], 2)
    owned, blocks = lax.optimization_barrier((owned, blocks))
    owned = both_reps(owned)
    down_total, out_total = owned[:, :, : model_width + SPARE], owned[:, :, model_width + SPARE :]
    down_rest = down_total[:, :, model_width:].reshape(block // rest, rest, -1)
    down_rest = down_rest.transpose(1, 0, 2).reshape(rest, model_width)
    down_total = jnp.concatenate(
        [down_total[:, :, :model_width].reshape(block, model_width), down_rest], 0
    )
    conv_total = out_total[0, :, channels + 2 : channels + 5]
    out_total = out_total[:, :, :channels].transpose(1, 0, 2).reshape(rows, model_width)
    in_total, gain_total = run(
        in_total_kernel,
        (1,),
        [whole(*blocks.shape)],
        [whole(rows, w_in.shape[1]), whole(rows, SPARE)],
        [array((rows, w_in.shape[1]), wide), array((rows, SPARE), wide)],
        [],
        16,
        2,
        [blocks],
    )
    ff_total = blocks[:, :, : 2 * units].astype(wide)
    ff_total = ff_total[:4] + ff_total[4:]

    return (
        result,
        grad_inputs,
        gain_total[:, 0],
        in_total,
        conv_total,
        out_total,
        gain_total[:, 1],
        from_members(ff_total[:, :, :units], 1),
        from_members(ff_total[:, :, units:], 1),
        down_total,
    )


def solution(mesh):
    return jax.shard_map(
        body,
        mesh=mesh,
        in_specs=(
            P(("rep", "fsdp"), None),
            P("fsdp"),
            P("fsdp", None),
            P("fsdp", None),
            P("fsdp", None),
            P("fsdp"),
            P("fsdp", None),
            P("fsdp", None),
            P("fsdp", None),
            P(("rep", "fsdp"), None),
        ),
        out_specs=(
            P(("rep", "fsdp"), None),
            P(("rep", "fsdp"), None),
            P("fsdp"),
            P("fsdp", None),
            P("fsdp", None),
            P("fsdp", None),
            P("fsdp"),
            P("fsdp", None),
            P("fsdp", None),
            P("fsdp", None),
        ),
        check_vma=False,
    )
```

```python
import jax
import jax.numpy as jnp
from jax import lax
from jax.experimental import pallas as pl
from jax.experimental.pallas import tpu as pltpu
from jax.sharding import PartitionSpec as P

epsilon = 1e-05

SIDE = 4
PLANE = SIDE * SIDE
HALF = PLANE * 2
SPARE = 128
EDGE = 8
CHUNK = 256
MIB = 1024 * 1024


def place(z, plane, core):
    return (z * PLANE + plane) * 2 + core


def moves(target):
    return [
        (place(z, plane, core), place(*target(z, plane, core)))
        for z in range(2)
        for plane in range(PLANE)
        for core in range(2)
    ]


TO_CORE = moves(lambda z, plane, core: (z, plane, 1 - core))
TO_Z = moves(lambda z, plane, core: (1 - z, plane, core))
TO_NEXT = moves(lambda z, plane, core: (z, (plane + 1) % PLANE, core))
TO_PREVIOUS = moves(lambda z, plane, core: (z, (plane - 1) % PLANE, core))
TEAMS = [
    [place(z, plane, core) for z in range(2) for core in range(2)] for plane in range(PLANE)
]
PLANES = [
    [place(z, plane, core) for plane in range(PLANE)] for z in range(2) for core in range(2)
]
BOTH_TEAMS = [[rep * 2 * HALF + member for rep in range(2) for member in team] for team in TEAMS]


def to_core(value):
    return lax.ppermute(value, "fsdp", TO_CORE)


def to_z(value):
    return lax.ppermute(value, "fsdp", TO_Z)


def norm_scale(values):
    return lax.rsqrt(jnp.mean(values * values, axis=-1, keepdims=True) + epsilon)


def norm_back(grad_normed, values, scale):
    inner = jnp.mean(grad_normed * values, axis=-1, keepdims=True)
    return scale * (grad_normed - values * scale * scale * inner)


def contract_rows(left, right):
    return lax.dot_general(
        left, right, (((0,), (0,)), ((), ())), preferred_element_type=jnp.float32
    )


def contract_cols(left, right):
    return lax.dot_general(
        left, right, (((1,), (1,)), ((), ())), preferred_element_type=jnp.float32
    )


def by_member(shard, parts):
    rows, columns = shard.shape
    split = shard.reshape(rows, parts, 2, PLANE, 2, -1)
    return split.transpose(2, 4, 0, 1, 3, 5).reshape(4, rows, columns // 4)


def from_members(blocks, parts):
    members, rows, columns = blocks.shape
    split = blocks.reshape(2, 2, rows, parts, PLANE, -1)
    return split.transpose(2, 3, 0, 4, 1, 5).reshape(rows, 4 * columns)


def team_swap(blocks):
    return lax.all_to_all(blocks, "fsdp", 0, 0, tiled=True, axis_index_groups=TEAMS)


def plane_swap(blocks):
    return lax.all_to_all(blocks, "fsdp", 0, 0, tiled=True, axis_index_groups=PLANES)


def gather_rows(blocks):
    members, rows, columns = blocks.shape
    return lax.all_gather(
        blocks.reshape(2, 2 * rows, columns),
        "fsdp",
        axis=1,
        tiled=True,
        axis_index_groups=PLANES,
    ).reshape(-1, columns)


def scatter_rows(value):
    total, columns = value.shape
    return lax.psum_scatter(
        value.reshape(2, total // 2, columns),
        "fsdp",
        scatter_dimension=1,
        tiled=True,
        axis_index_groups=PLANES,
    ).reshape(4, -1, columns)


def core_sum(keep, sent):
    return keep + to_core(sent).astype(jnp.float32)


def own_sum(keep, sent):
    pair = core_sum(keep, sent)
    return pair[0] + to_z(pair[1].astype(jnp.bfloat16)).astype(jnp.float32)


def whole(*shape):
    return pl.BlockSpec(shape, lambda *_: (0,) * len(shape), pipeline_mode=pl.Buffered(1))


def per_slot(length, width, column=0):
    return pl.BlockSpec((1, length, width), lambda slot: (slot, 0, column))


def per_pair(length, width):
    return pl.BlockSpec((1, length, width), lambda slot: (slot // 2, 0, 0))


def pair_of_values(length, width, which):
    return pl.BlockSpec((1, 1, length, width), lambda slot: (slot // 2, which, 0, 0))


def run(kernel, grid, in_specs, out_specs, out_shape, scratch, room, busy, values):
    return pl.pallas_call(
        kernel,
        grid=grid,
        in_specs=in_specs,
        out_specs=out_specs,
        out_shape=out_shape,
        scratch_shapes=scratch,
        compiler_params=pltpu.CompilerParams(vmem_limit_bytes=room * MIB),
        cost_estimate=pl.CostEstimate(
            flops=int(busy * 1.15e9), bytes_accessed=0, transcendentals=0
        ),
    )(*values)


def array(shape, kind):
    return jax.ShapeDtypeStruct(shape, kind)


def pick(slot, even, odd):
    return jnp.where(slot % 2 == 0, even, odd)


def shifted_in(values, rows_before, steps):
    moved = pltpu.roll(values, steps, 0)
    row = lax.broadcasted_iota(jnp.int32, values.shape, 0)
    for index in range(steps):
        at = EDGE - steps + index
        moved = jnp.where(row == index, rows_before[at : at + 1], moved)
    return moved


def shifted_out(values, next_rows, steps):
    length = values.shape[0]
    moved = pltpu.roll(values, length - steps, 0)
    row = lax.broadcasted_iota(jnp.int32, values.shape, 0)
    for index in range(steps):
        moved = jnp.where(row == length - steps + index, next_rows[index : index + 1], moved)
    return moved


def store_pair(slot, value, keep_ref, sent_ref):
    @pl.when(slot % 2 == 0)
    def _():
        keep_ref[0] = value

    @pl.when(slot % 2 == 1)
    def _():
        sent_ref[0] = value.astype(sent_ref.dtype)


def project_kernel(
    pair_ref, other_ref, first_ref,
    normed_ref, proj_ref, mixed_ref, in_ref, out_ref, gains_ref, taps_ref,
    column, taps_column,
):
    slot = pl.program_id(0)
    width = in_ref.shape[1]
    channels = width // 3
    rows = channels // PLANE

    @pl.when(slot == 0)
    def _():
        for plane in range(PLANE):
            for z in range(2):
                at = pl.ds((z * PLANE + plane) * 2 * rows, 2 * rows)
                source = pl.ds(z * 2 * rows, 2 * rows)
                in_ref[at, :] = first_ref[plane, source, :width]
                column[at, :] = first_ref[plane, source, width + channels :].astype(jnp.float32)
            at = pl.ds(plane * rows, rows)
            for part in range(4):
                out_ref[at, part * channels : (part + 1) * channels] = first_ref[
                    plane, pl.ds(part * rows, rows), width : width + channels
                ]
            taps_column[at, :] = first_ref[plane, :rows, width + channels :].astype(jnp.float32)
        gains_ref[...] = column[...].T[:8]
        taps_ref[...] = taps_column[...].T[:8]

    values = pick(slot, pair_ref[0, 0], other_ref[0, 0]).astype(jnp.float32)
    normed = (values * norm_scale(values) * gains_ref[0:1]).astype(jnp.bfloat16)
    normed_ref[0] = normed
    projected = jnp.dot(normed, in_ref[...], preferred_element_type=jnp.float32)
    proj_ref[0] = projected
    mixed = projected[:, :channels] * projected[:, 2 * channels :]
    mixed_ref[0] = mixed.astype(jnp.bfloat16)


def branch_kernel(
    mixed_ref, earlier_ref, out_gate_ref, taps_ref, out_ref,
    convolved_ref, gated_ref, keep_ref, sent_ref,
):
    slot = pl.program_id(0)
    mixed = mixed_ref[0].astype(jnp.float32)
    earlier = earlier_ref[0]
    convolved = (
        taps_ref[2:3] * mixed
        + taps_ref[3:4] * shifted_in(mixed, earlier, 1)
        + taps_ref[4:5] * shifted_in(mixed, earlier, 2)
    )
    convolved_ref[0] = convolved
    gated = (out_gate_ref[0] * convolved).astype(jnp.bfloat16)
    gated_ref[0] = gated
    branch = jnp.dot(gated, out_ref[...], preferred_element_type=jnp.float32)
    store_pair(slot, branch, keep_ref, sent_ref)


def middle_kernel(inputs_ref, branch_ref, crossed_ref, gains_ref, middle_ref, normed_ref):
    middle = inputs_ref[0, 0].astype(jnp.float32) + branch_ref[0]
    middle += crossed_ref[0].astype(jnp.float32)
    middle_ref[0] = middle
    normed_ref[0] = (middle * norm_scale(middle) * gains_ref[1:2]).astype(jnp.bfloat16)


def grad_middle_kernel(
    grad_ref, crossed_ref, middle_ref, outer_ref, gains_ref,
    grad_middle_ref, branch_ref, gain_ref,
):
    grad_normed = grad_ref[0] + crossed_ref[0].astype(jnp.float32)
    middle = middle_ref[0]
    scale = norm_scale(middle)

    @pl.when(pl.program_id(0) == 0)
    def _():
        gain_ref[...] = jnp.sum(grad_normed * middle * scale, axis=0, keepdims=True)

    grad_middle = norm_back(grad_normed * gains_ref[1:2], middle, scale)
    grad_middle += outer_ref[0, 0].astype(jnp.float32)
    grad_middle_ref[0] = grad_middle
    branch_ref[0] = grad_middle.astype(jnp.bfloat16)


def ff_kernel(
    own_ref, swap_ref, pair_ref, other_ref, weights_ref, down_ref,
    hidden_ref, grad_gate_ref, grad_up_ref, keep_ref, sent_ref,
):
    units, width = down_ref.shape
    length = own_ref.shape[1]
    normed = jnp.concatenate([own_ref[0], swap_ref[0]], 0)
    outer = jnp.concatenate([pair_ref[0, 0], other_ref[0, 0]], 0)
    for start in range(0, units, CHUNK):
        lanes = slice(start, min(start + CHUNK, units))
        up_lanes = slice(units + lanes.start, units + lanes.stop)
        shape = (2, length, lanes.stop - lanes.start)
        gate = jnp.dot(normed, weights_ref[:, lanes], preferred_element_type=jnp.float32)
        up = jnp.dot(normed, weights_ref[:, up_lanes], preferred_element_type=jnp.float32)
        grad = contract_cols(outer, down_ref[lanes, :])
        sigmoid = jax.nn.sigmoid(gate)
        silu = gate * sigmoid
        hidden_ref[:, :, lanes] = (silu * up).astype(jnp.bfloat16).reshape(shape)
        grad_gate = grad * up * sigmoid * (1.0 + gate * (1.0 - sigmoid))
        grad_gate_ref[:, :, lanes] = grad_gate.astype(jnp.bfloat16).reshape(shape)
        grad_up_ref[:, :, lanes] = (grad * silu).astype(jnp.bfloat16).reshape(shape)
    grad_gate = grad_gate_ref[...].reshape(2 * length, units)
    grad_up = grad_up_ref[...].reshape(2 * length, units)
    term = contract_cols(grad_gate, weights_ref[:, :units])
    term += contract_cols(grad_up, weights_ref[:, units : 2 * units])
    keep_ref[0] = term[:length]
    sent_ref[0] = term[length:].astype(jnp.bfloat16)


def ff_grads_kernel(
    own_ref, swap_ref, pair_ref, other_ref, hidden_ref, grad_gate_ref, grad_up_ref,
    pack_ref,
    gate_total, up_total, down_total,
):
    step = pl.program_id(0)
    width, units = gate_total.shape
    each = units // PLANE
    block = width // PLANE
    rest = each - block
    tokens = 2 * own_ref.shape[1]
    normed = jnp.concatenate([own_ref[0], swap_ref[0]], 0)
    outer = jnp.concatenate([pair_ref[0, 0], other_ref[0, 0]], 0)

    def gate_term():
        return contract_rows(normed, grad_gate_ref[...].reshape(tokens, units))

    def up_term():
        return contract_rows(normed, grad_up_ref[...].reshape(tokens, units))

    def down_term():
        return contract_rows(hidden_ref[...].reshape(tokens, units), outer)

    @pl.when(step == 0)
    def _():
        gate_total[...] = gate_term()
        up_total[...] = up_term()
        down_total[...] = down_term()

    @pl.when(step == 1)
    def _():
        pack_ref[:, :units] = (gate_total[...] + gate_term()).astype(jnp.bfloat16)
        pack_ref[:, units : 2 * units] = (up_total[...] + up_term()).astype(jnp.bfloat16)
        down_total[...] += down_term()
        for plane in range(PLANE):
            start = plane * each
            for half in range(2):
                to = half * width // 2 + plane * block // 2
                pack_ref[to : to + block // 2, 2 * units : 2 * units + width] = down_total[
                    start + half * block // 2 : start + (half + 1) * block // 2
                ].astype(jnp.bfloat16)
                parts = block // rest // 2
                lanes = width * rest // block
                last = down_total[start + block : start + each]
                pieces = [
                    last[:, (half * parts + part) * lanes : (half * parts + part + 1) * lanes]
                    for part in range(parts)
                ]
                pack_ref[to : to + block // 2, 2 * units + width :] = jnp.concatenate(
                    pieces, 0
                ).astype(jnp.bfloat16)


def gated_back_kernel(
    own_ref, swap_ref, out_ref, convolved_ref, out_gate_ref, grad_out_ref, grad_conv_ref
):
    slot = pl.program_id(0)
    grad_gated = contract_cols(pick(slot, own_ref[0], swap_ref[0]), out_ref[...])
    grad_out_ref[0] = (grad_gated * convolved_ref[0]).astype(jnp.bfloat16)
    grad_conv_ref[0] = grad_gated * out_gate_ref[0]


def out_grads_kernel(
    own_ref, swap_ref, gated_ref, grad_conv_ref, mixed_ref, earlier_ref, gain_ref,
    part_ref, spare_ref,
    total, taps_rows, gain_rows,
):
    slot = pl.program_id(0)
    rows = spare_ref.shape[1] // 4
    channels = gated_ref.shape[2]

    @pl.when(slot == 0)
    def _():
        total[...] = jnp.zeros_like(total)
        taps_rows[...] = jnp.zeros_like(taps_rows)
        gain_rows[...] = jnp.zeros_like(gain_rows)
        gain_rows[1:2] = gain_ref[...]

    total[...] += contract_rows(gated_ref[0], pick(slot, own_ref[0], swap_ref[0]))
    grad_conv = grad_conv_ref[0]
    mixed = mixed_ref[0].astype(jnp.float32)
    earlier = earlier_ref[0]
    lagged = (mixed, shifted_in(mixed, earlier, 1), shifted_in(mixed, earlier, 2))
    for lag, value in enumerate(lagged):
        taps_rows[2 + lag : 3 + lag] += jnp.sum(grad_conv * value, axis=0, keepdims=True)

    @pl.when(slot == 3)
    def _():
        gain_column = gain_rows[...].T
        taps_column = taps_rows[...].T
        for plane in range(PLANE):
            at = slice(plane * rows, (plane + 1) * rows)
            for part in range(4):
                part_ref[plane, part * rows : (part + 1) * rows, :] = total[
                    at, part * channels : (part + 1) * channels
                ].astype(jnp.bfloat16)
            for z in range(2):
                start = (z * PLANE + plane) * 2 * rows
                spare_ref[plane, z * 2 * rows : (z + 1) * 2 * rows, :] = gain_column[
                    start : start + 2 * rows
                ]
            spare_ref[plane, :rows, :] += taps_column[at]


def project_back_kernel(
    grad_conv_ref, later_ref, proj_ref, grad_out_ref, normed_ref, in_ref, taps_ref,
    pair_ref, other_ref, part_ref, spare_ref,
    pack_ref, keep_ref, sent_ref,
    total, gain_rows,
):
    slot = pl.program_id(0)
    width = in_ref.shape[1]
    channels = width // 3
    rows = channels // PLANE

    @pl.when(slot == 0)
    def _():
        total[...] = jnp.zeros_like(total)
        gain_rows[...] = jnp.zeros_like(gain_rows)

    grad_conv, later = grad_conv_ref[0], later_ref[0]
    grad_mixed = (
        taps_ref[2:3] * grad_conv
        + taps_ref[3:4] * shifted_out(grad_conv, later, 1)
        + taps_ref[4:5] * shifted_out(grad_conv, later, 2)
    )
    grad_projected = jnp.concatenate(
        [
            (grad_mixed * proj_ref[0, :, 2 * channels :]).astype(jnp.bfloat16),
            grad_out_ref[0],
            (grad_mixed * proj_ref[0, :, :channels]).astype(jnp.bfloat16),
        ],
        1,
    )
    total[...] += contract_rows(normed_ref[0], grad_projected)
    grad_normed = contract_cols(grad_projected, in_ref[...])
    store_pair(slot, grad_normed, keep_ref, sent_ref)
    values = pick(slot, pair_ref[0, 0], other_ref[0, 0]).astype(jnp.float32)
    gain_rows[0:1] += jnp.sum(grad_normed * values * norm_scale(values), axis=0, keepdims=True)

    @pl.when(slot == 3)
    def _():
        gain_column = gain_rows[...].T
        for plane in range(PLANE):
            for z in range(2):
                start = (z * PLANE + plane) * 2 * rows
                to = slice(z * 2 * rows, (z + 1) * 2 * rows)
                pack_ref[plane, to, :width] = total[start : start + 2 * rows].astype(jnp.bfloat16)
                pack_ref[plane, to, width + channels :] = (
                    spare_ref[plane, to] + gain_column[start : start + 2 * rows]
                ).astype(jnp.bfloat16)
            pack_ref[plane, :, width : width + channels] = part_ref[plane]


def in_total_kernel(blocks_ref, total_ref, spare_ref):
    members, rows, width = blocks_ref.shape
    channels = total_ref.shape[1] // 12
    first = width - SPARE - 3 * channels
    unit = channels // PLANE
    source = lax.broadcasted_iota(jnp.int32, (channels, 2 * channels), 0)
    target = lax.broadcasted_iota(jnp.int32, (channels, 2 * channels), 1)
    for z in range(2):
        for part in range(3):
            total = jnp.zeros((rows, 2 * channels), jnp.float32)
            for core in range(2):
                placed = source // unit * (2 * unit) + core * unit + source % unit == target
                placed = placed.astype(jnp.float32).astype(jnp.bfloat16)
                for rep in range(2):
                    block = blocks_ref[rep * 4 + z * 2 + core]
                    total += jnp.dot(
                        block[:, first + part * channels : first + (part + 1) * channels],
                        placed,
                        preferred_element_type=jnp.float32,
                    )
            start = (part * 2 + z) * 2 * channels
            total_ref[:, start : start + 2 * channels] = total
    spare = jnp.zeros((rows, SPARE), jnp.float32)
    for member in range(members):
        spare += blocks_ref[member, :, width - SPARE :].astype(jnp.float32)
    spare_ref[...] = spare


def body(
    tokens, gain_first, w_in, conv_weight, w_out, gain_second, w_gate, w_up, w_down, cotangent
):
    low, wide = jnp.bfloat16, jnp.float32
    length, model_width = tokens.shape
    position = lax.axis_index("fsdp")
    core, plane, z = position % 2, position // 2 % PLANE, position // HALF
    rows = w_in.shape[0]
    channels = model_width // 4

    block = 4 * rows
    rest = w_down.shape[0] - block
    units = w_down.shape[0] * PLANE
    gains = jnp.pad(jnp.stack([gain_first, gain_second], 1), ((0, 0), (0, SPARE - 2)))
    gains = jnp.broadcast_to(gains, (4, rows, SPARE))
    swapped = team_swap(
        jnp.concatenate(
            [by_member(w_gate, 1), by_member(w_up, 1), by_member(w_in, 3), gains], 2
        )
    )
    down_main = w_down[:block].reshape(4, rows, model_width)
    down_rest = w_down[block:].reshape(rest, block // rest, -1).transpose(1, 0, 2)
    ff_all = gather_rows(
        jnp.concatenate(
            [swapped[:, :, : 2 * units], down_main, down_rest.reshape(4, rows, -1)], 2
        )
    )

    in_width = 3 * channels
    conv_lanes = jnp.pad(conv_weight, ((0, 0), (2, SPARE - 5)))
    first_pack = jnp.concatenate(
        [
            swapped[:, :, 2 * units : 2 * units + in_width],
            w_out.reshape(rows, 4, channels).transpose(1, 0, 2),
            swapped[:, :, 2 * units + in_width :] + conv_lanes,
        ],
        2,
    )
    first_all = plane_swap(jnp.broadcast_to(first_pack, (PLANE,) + first_pack.shape))
    first_all = first_all.reshape(PLANE, 4 * rows, -1)

    main_rows = ff_all[:, 2 * units : 2 * units + model_width].reshape(2, PLANE, 2 * rows, -1)
    main_rows = main_rows.transpose(1, 0, 2, 3).reshape(PLANE, block, model_width)
    rest_rows = ff_all[:, 2 * units + model_width :].reshape(2, PLANE, 2 * rows, -1)
    rest_rows = rest_rows.transpose(1, 0, 2, 3).reshape(PLANE, block // rest, rest, -1)
    rest_rows = rest_rows.transpose(0, 2, 1, 3).reshape(PLANE, rest, model_width)
    down_full = jnp.concatenate([main_rows, rest_rows], 1).reshape(units, model_width)

    pair = jnp.stack([tokens, cotangent])
    pair = jnp.stack([pair, to_z(pair)])
    other = to_core(pair)
    team_pairs = [pair_of_values(length, model_width, 0)] * 2
    slot_wide, slot_narrow = (4, length, model_width), (4, length, channels)
    pair_wide = (2, length, model_width)
    pairs = [per_pair(length, model_width)] * 2
    narrow = per_slot(length, channels)
    out_gate = per_slot(length, channels, 1)
    edge, edge_after = per_slot(EDGE, channels), per_slot(8, channels)
    out_matrix, in_matrix = whole(channels, model_width), whole(model_width, in_width)
    taps = whole(8, channels)

    normed, projected, mixed, in_full, out_full, gains, kernel = run(
        project_kernel,
        (4,),
        team_pairs + [whole(*first_all.shape)],
        [
            per_slot(length, model_width),
            per_slot(length, in_width),
            narrow,
            in_matrix,
            out_matrix,
            whole(8, model_width),
            taps,
        ],
        [
            array(slot_wide, low),
            array((4, length, in_width), wide),
            array(slot_narrow, low),
            array((model_width, in_width), low),
            array((channels, model_width), low),
            array((8, model_width), wide),
            array((8, channels), wide),
        ],
        [pltpu.VMEM((model_width, SPARE), wide), pltpu.VMEM((channels, SPARE), wide)],
        20,
        4,
        [pair, other, first_all],
    )

    def by_core(first, second):
        return jnp.where(core == 0, first, second)

    tails = mixed[:, length - 2 :]
    sent = by_core(tails[1::2], tails[0::2])
    received = lax.ppermute(sent, "fsdp", TO_NEXT)
    nothing = jnp.zeros_like(received[0])
    shifted = jnp.where(
        z == 0, jnp.stack([nothing, received[0]]), jnp.stack([received[1], nothing])
    )
    before = jnp.where(plane == 0, shifted, received)
    own_before = by_core(before, tails[1::2])
    other_before = by_core(tails[0::2], before)
    earlier = jnp.stack([own_before[0], other_before[0], own_before[1], other_before[1]])
    earlier = jnp.pad(earlier.astype(wide), ((0, 0), (EDGE - 2, 0), (0, 0)))
    convolved, gated, branch_keep, branch_sent = run(
        branch_kernel,
        (4,),
        [narrow, edge, out_gate, taps, out_matrix],
        [narrow, narrow] + pairs,
        [
            array(slot_narrow, wide),
            array(slot_narrow, low),
            array(pair_wide, wide),
            array(pair_wide, low),
        ],
        [],
        12,
        2,
        [mixed, earlier, projected, kernel, out_full],
    )
    branch_pair = core_sum(branch_keep, branch_sent)
    branch_other = to_z(branch_pair.astype(low))
    branch_other, down_full = lax.optimization_barrier((branch_other, down_full))
    one = pl.BlockSpec((1, length, model_width), lambda index: (index, 0, 0))
    crossed = pl.BlockSpec((1, length, model_width), lambda index: (1 - index, 0, 0))
    tokens_one, outer_one = (
        pl.BlockSpec((1, 1, length, model_width), lambda index, which=which: (index, which, 0, 0))
        for which in range(2)
    )
    gain_rows = whole(8, model_width)
    middle, normed_two = run(
        middle_kernel,
        (2,),
        [tokens_one, one, crossed, gain_rows],
        [one, one],
        [array(pair_wide, wide), array(pair_wide, low)],
        [],
        16,
        3,
        [pair, branch_pair, branch_other, gains],
    )
    normed_swap = to_core(normed_two)

    step_pairs = [pl.BlockSpec((1, length, model_width), lambda step: (step, 0, 0))] * 2
    step_outer = [pl.BlockSpec((1, 1, length, model_width), lambda step: (step, 1, 0, 0))] * 2
    unit_slot = pl.BlockSpec((2, length, units), lambda step: (step, 0, 0))
    unit_shape = array((4, length, units), low)
    hidden, grad_gate, grad_upper, grad_keep, grad_sent = run(
        ff_kernel,
        (2,),
        step_pairs + step_outer + [whole(model_width, 2 * units), whole(units, model_width)],
        [unit_slot] * 3 + step_pairs,
        [unit_shape] * 3 + [array(pair_wide, wide), array(pair_wide, low)],
        [],
        36,
        17,
        [normed_two, normed_swap, pair, other, ff_all, down_full],
    )
    grad_pair = core_sum(grad_keep, grad_sent)
    grad_sent = grad_pair.astype(low)
    grad_other = to_z(grad_sent)

    (ff_grads,) = run(
        ff_grads_kernel,
        (2,),
        step_pairs + step_outer + [unit_slot] * 3,
        [whole(*ff_all.shape)],
        [array(ff_all.shape, low)],
        [
            pltpu.VMEM((model_width, units), wide),
            pltpu.VMEM((model_width, units), wide),
            pltpu.VMEM((units, model_width), wide),
        ],
        48,
        12,
        [normed_two, normed_swap, pair, other, hidden, grad_gate, grad_upper],
    )
    ff_share = scatter_rows(ff_grads)
    down_term = jnp.dot(
        hidden.reshape(4 * length, units), down_full, preferred_element_type=wide
    ).reshape(4, length, model_width)
    grad_other, ff_grads, down_term = lax.optimization_barrier((grad_other, ff_grads, down_term))
    grad_middle, grad_branch, grad_gain_two = run(
        grad_middle_kernel,
        (2,),
        [one, crossed, one, outer_one, gain_rows],
        [one, one, whole(1, model_width)],
        [array(pair_wide, wide), array(pair_wide, low), array((1, model_width), wide)],
        [],
        18,
        4,
        [grad_pair, grad_other, middle, pair, gains],
    )
    grad_swap = to_core(grad_branch)

    grad_out, grad_conv = run(
        gated_back_kernel,
        (4,),
        pairs + [out_matrix, narrow, out_gate],
        [narrow, narrow],
        [array(slot_narrow, low), array(slot_narrow, wide)],
        [],
        12,
        2,
        [grad_branch, grad_swap, out_full, convolved, projected],
    )
    heads = grad_conv[:, :2]
    sent = by_core(heads[0::2], heads[1::2])
    received = lax.ppermute(sent, "fsdp", TO_PREVIOUS)
    nothing = jnp.zeros_like(received[0])
    shifted = jnp.where(
        z == 0, jnp.stack([received[1], nothing]), jnp.stack([nothing, received[0]])
    )
    after = jnp.where(plane == PLANE - 1, shifted, received)
    own_after = by_core(heads[1::2], after)
    other_after = by_core(after, heads[0::2])
    later = jnp.stack([own_after[0], other_after[0], own_after[1], other_after[1]])
    later = jnp.pad(later, ((0, 0), (0, 6), (0, 0)))
    part_shape, spare_shape = (PLANE, 4 * rows, channels), (PLANE, 4 * rows, SPARE)
    out_part, spare_part = run(
        out_grads_kernel,
        (4,),
        pairs + [narrow, narrow, narrow, edge, whole(1, model_width)],
        [whole(*part_shape), whole(*spare_shape)],
        [array(part_shape, low), array(spare_shape, wide)],
        [
            pltpu.VMEM((channels, model_width), wide),
            pltpu.VMEM((SPARE, channels), wide),
            pltpu.VMEM((SPARE, model_width), wide),
        ],
        14,
        2.5,
        [grad_branch, grad_swap, gated, grad_conv, mixed, earlier, grad_gain_two],
    )
    first_grads, normed_keep, normed_sent = run(
        project_back_kernel,
        (4,),
        [
            narrow,
            edge_after,
            per_slot(length, in_width),
            narrow,
            per_slot(length, model_width),
            in_matrix,
            taps,
        ]
        + team_pairs
        + [whole(*part_shape), whole(*spare_shape)],
        [whole(*first_all.shape)] + pairs,
        [array(first_all.shape, low), array(pair_wide, wide), array(pair_wide, low)],
        [pltpu.VMEM((model_width, in_width), wide), pltpu.VMEM((SPARE, model_width), wide)],
        26,
        8,
        [
            grad_conv,
            later,
            projected,
            grad_out,
            normed,
            in_full,
            kernel,
            pair,
            other,
            out_part,
            spare_part,
        ],
    )
    first_grads = first_grads.reshape(PLANE, 4, rows, -1)
    first_arrived = plane_swap(first_grads)

    down_term, normed_sent = lax.optimization_barrier((down_term, normed_sent))
    result = middle[0] + own_sum(down_term[0::2], down_term[1::2].astype(low))
    grad_normed_own = own_sum(normed_keep, normed_sent)
    inputs = tokens.astype(wide)
    grad_inputs = grad_middle[0] + norm_back(
        grad_normed_own * gains[0], inputs, norm_scale(inputs)
    )
    result, grad_inputs, first_arrived = lax.optimization_barrier(
        (result.astype(low), grad_inputs, first_arrived)
    )
    first_share = jnp.sum(first_arrived.astype(wide), axis=0).astype(low)

    def both_reps(value):
        other = lax.ppermute(value, "rep", [(0, 1), (1, 0)])
        return value.astype(wide) + other.astype(wide)

    blocks = jnp.concatenate(
        [
            ff_share[:, :, : 2 * units],
            first_share[:, :, :in_width],
            first_share[:, :, in_width + channels :],
        ],
        2,
    )
    blocks = lax.all_to_all(
        jnp.concatenate([blocks, blocks]),
        ("rep", "fsdp"),
        0,
        0,
        tiled=True,
        axis_index_groups=BOTH_TEAMS,
    )
    owned = jnp.concatenate([ff_share[:, :, 2 * units :], first_share[:, :, in_width:]], 2)
    owned, blocks = lax.optimization_barrier((owned, blocks))
    owned = both_reps(owned)
    down_total, out_total = owned[:, :, : model_width + SPARE], owned[:, :, model_width + SPARE :]
    down_rest = down_total[:, :, model_width:].reshape(block // rest, rest, -1)
    down_rest = down_rest.transpose(1, 0, 2).reshape(rest, model_width)
    down_total = jnp.concatenate(
        [down_total[:, :, :model_width].reshape(block, model_width), down_rest], 0
    )
    conv_total = out_total[0, :, channels + 2 : channels + 5]
    out_total = out_total[:, :, :channels].transpose(1, 0, 2).reshape(rows, model_width)
    in_total, gain_total = run(
        in_total_kernel,
        (1,),
        [whole(*blocks.shape)],
        [whole(rows, w_in.shape[1]), whole(rows, SPARE)],
        [array((rows, w_in.shape[1]), wide), array((rows, SPARE), wide)],
        [],
        16,
        2,
        [blocks],
    )
    ff_total = blocks[:, :, : 2 * units].astype(wide)
    ff_total = ff_total[:4] + ff_total[4:]

    return (
        result,
        grad_inputs,
        gain_total[:, 0],
        in_total,
        conv_total,
        out_total,
        gain_total[:, 1],
        from_members(ff_total[:, :, :units], 1),
        from_members(ff_total[:, :, units:], 1),
        down_total,
    )


def solution(mesh):
    return jax.shard_map(
        body,
        mesh=mesh,
        in_specs=(
            P(("rep", "fsdp"), None),
            P("fsdp"),
            P("fsdp", None),
            P("fsdp", None),
            P("fsdp", None),
            P("fsdp"),
            P("fsdp", None),
            P("fsdp", None),
            P("fsdp", None),
            P(("rep", "fsdp"), None),
        ),
        out_specs=(
            P(("rep", "fsdp"), None),
            P(("rep", "fsdp"), None),
            P("fsdp"),
            P("fsdp", None),
            P("fsdp", None),
            P("fsdp", None),
            P("fsdp"),
            P("fsdp", None),
            P("fsdp", None),
            P("fsdp", None),
        ),
        check_vma=False,
    )
```
